32 devices in a mesh: chan: 2 (over x), tm: 16 (over z, y, core).
Axes of the slice: x: 2, y: 2, z: 4, core: 2. Of those that a mesh axis runs over, the one named last changes fastest.
Arguments:
- frames_in: bfloat16 [65536, 128], P(('tm', 'chan')), may hold values from -6 to 6
- item_lengths: int32 [16], replicated, may hold values from 1 to 8192, 65536 in all
- out_cotangent: bfloat16 [65536, 128], P(('tm', 'chan')), may hold values from -6 to 6
- skip_cotangent: bfloat16 [65536, 128], P(('tm', 'chan')), may hold values from -6 to 6
- expand: float32 [128, 512], P(None, 'chan'), may hold values from -0.5 to 0.5
- expand_moment: float32 [128, 512], P(None, 'chan'), may hold values from -0.0078125 to 0.0078125
- expand_square: float32 [128, 512], P(None, 'chan'), may hold values from 6.2042744e-08 to 9.926839e-07
- depthwise: float32 [3, 512], P(None, 'chan'), may hold values from -3.5 to 3.5
- depth_moment: float32 [3, 512], P(None, 'chan'), may hold values from -0.0078125 to 0.0078125
- depth_square: float32 [3, 512], P(None, 'chan'), may hold values from 6.2042744e-08 to 9.926839e-07
- project: float32 [2, 512, 128], P(None, 'chan'), may hold values from -0.17872982 to 0.17872982
- project_moment: float32 [2, 512, 128], P(None, 'chan'), may hold values from -0.0078125 to 0.0078125
- project_square: float32 [2, 512, 128], P(None, 'chan'), may hold values from 6.2042744e-08 to 9.926839e-07
- channel_vectors: float32 [6, 512], P(None, 'chan'), may hold values from 0.5 to 1.5
- vector_moment: float32 [6, 512], P(None, 'chan'), may hold values from -0.0078125 to 0.0078125
- vector_square: float32 [6, 512], P(None, 'chan'), may hold values from 6.2042744e-08 to 9.926839e-07
- output_biases: float32 [2, 128], replicated, may hold values from -3 to 3
- bias_moment: float32 [2, 128], replicated, may hold values from -0.0078125 to 0.0078125
- bias_square: float32 [2, 128], replicated, may hold values from 6.2042744e-08 to 9.926839e-07
- prelu_slopes: float32 [2], replicated, may hold values from 0.1 to 0.4
- slope_moment: float32 [2], replicated, may hold values from -0.15625 to 0.15625
- slope_square: float32 [2], replicated, may hold values from 2.4817098e-05 to 0.00039707357
Outputs:
- block_out: bfloat16 [65536, 128], P(('tm', 'chan'))
- skip_out: bfloat16 [65536, 128], P(('tm', 'chan'))
- input_grad: float32 [65536, 128], P(('tm', 'chan'))
- grad_norm: float32 [], replicated
- expand_new: float32 [128, 512], P(None, 'chan')
- expand_moment_new: float32 [128, 512], P(None, 'chan')
- expand_square_new: float32 [128, 512], P(None, 'chan')
- depthwise_new: float32 [3, 512], P(None, 'chan')
- depth_moment_new: float32 [3, 512], P(None, 'chan')
- depth_square_new: float32 [3, 512], P(None, 'chan')
- project_new: float32 [2, 512, 128], P(None, 'chan')
- project_moment_new: float32 [2, 512, 128], P(None, 'chan')
- project_square_new: float32 [2, 512, 128], P(None, 'chan')
- vectors_new: float32 [6, 512], P(None, 'chan')
- vector_moment_new: float32 [6, 512], P(None, 'chan')
- vector_square_new: float32 [6, 512], P(None, 'chan')
- biases_new: float32 [2, 128], replicated
- bias_moment_new: float32 [2, 128], replicated
- bias_square_new: float32 [2, 128], replicated
- slopes_new: float32 [2], replicated
- slope_moment_new: float32 [2], replicated
- slope_square_new: float32 [2], replicated
The draws below stay inside these ranges and needn't reach their ends.
Inputs may be any that keep to these rules, and one draw needn't show every extreme that they name: `item_lengths`: frame counts of the 16 items laid end to end; they sum to 65536, and the largest is exactly 8192.
All inputs are finite; a program needn't handle non-finite values.
Results may differ from the reference program's by a relative error of at most 0.005.
The reference program's roundings to bfloat16 on the way count: a program that leaves them out, or rounds other values in their place, can miss the bound.
Values may be sent and summed in bfloat16 or wider, within the bound.
A program may use at most 64 MiB of HBM per device.

```python
import math
import jax
import jax.numpy as jnp
import numpy as np
from jax import lax

N = 128
H = 512
DILATION_STEP = 16
FR_DEV = 4096
FRAMES = 65536
AVG_LEN = 4096
ITEMS = 16


def block_positions():
    block_span = max(FR_DEV // 2, 1)
    return (jnp.arange(FRAMES, dtype=jnp.int32) // block_span, FRAMES // block_span + 1)


def signed_sizes(key, count, lowest, highest):
    pieces = jax.random.split(key, 2)
    signs = jnp.where(jax.random.bernoulli(pieces[0], 0.5, (count,)), 1.0, -1.0).astype(jnp.float32)
    sizes = jax.random.uniform(pieces[1], (count,), jnp.float32, lowest, highest)
    return signs * sizes


def channel_pattern(key):
    return jnp.where(jax.random.bernoulli(jax.random.fold_in(key, 500), 0.5, (N,)), 1.0, -1.0).astype(jnp.float32)


def cotangent_offsets(key, lowest, highest):
    positions, count = block_positions()
    amplitudes = signed_sizes(jax.random.fold_in(key, 501), count, lowest, highest)
    return amplitudes[positions][:, None] * channel_pattern(key)[None, :]


def draw_out_cotangent(key, part):
    offsets = cotangent_offsets(key, 0.0, 2.5)
    key = jax.random.fold_in(key, 11)
    noise = jnp.clip(jax.random.normal(key, (FRAMES, N), jnp.float32), -3.5, 3.5)
    return (noise + offsets).astype(jnp.bfloat16)


def draw_skip_cotangent(key, part):
    offsets = cotangent_offsets(key, 0.0, 2.5)
    key = jax.random.fold_in(key, 12)
    noise = jnp.clip(jax.random.normal(key, (FRAMES, N), jnp.float32), -3.5, 3.5)
    return (noise + offsets).astype(jnp.bfloat16)


def draw_project(key, part):
    common_part = 0.25 / N * channel_pattern(key)
    key = jax.random.fold_in(key, 14)
    noise = jnp.clip(jax.random.normal(key, (2, H, N), jnp.float32), -4.0, 4.0)
    return (noise * H ** (-0.5) + common_part[None, None, :]).astype(jnp.float32)


def draw_frames_in(key, part):
    key = jax.random.fold_in(key, 13)
    positions, count = block_positions()
    pattern_key, size_key, noise_key = jax.random.split(key, 3)
    pattern = jnp.where(jax.random.bernoulli(pattern_key, 0.5, (N,)), 1.0, -1.0).astype(jnp.float32)
    amplitudes = signed_sizes(size_key, count, 0.0, 2.5)
    noise = jnp.clip(jax.random.normal(noise_key, (FRAMES, N), jnp.float32), -3.5, 3.5)
    return (noise + amplitudes[positions][:, None] * pattern[None, :]).astype(jnp.bfloat16)


def block_levels(rng, shape, cuts, smallest, largest):
    def one(position, parts):
        draws = jax.random.uniform(jax.random.fold_in(jax.random.fold_in(rng, 6), position), (parts,), jnp.float32, smallest / len(cuts), largest / len(cuts))
        return jnp.repeat(jnp.exp(draws), shape[position] // parts).reshape((-1,) + (1,) * (len(shape) - position - 1))

    factor_of = one(*cuts[0])
    for cut in cuts[1:]:
        factor_of = factor_of * one(*cut)
    return factor_of


def length_profile(number_of, total, most, skew):
    weights = [(1 << 20) // math.isqrt(standing ** skew) + 1 for standing in range(2, number_of + 1)]
    spare, counts = total - most - (number_of - 1), [1] * (number_of - 1)
    while spare > 0:
        movable = [i for i in range(number_of - 1) if counts[i] < most]
        whole, remaining = sum([weights[i] for i in movable]), spare
        for i in movable:
            more = min(most - counts[i], max(1, remaining * weights[i] // whole), spare)
            counts[i] = counts[i] + more
            spare = spare - more
    return np.array([most] + counts)


def ragged_sizes(key, count, total, reach, skew):
    if count == 2:
        one = jax.random.randint(key, (), max(1, total - reach), min(reach, total - 1) + 1)
        return jnp.stack([one, total - one])
    lengths = jnp.asarray(length_profile(count, total, reach, skew), jnp.int32)
    pairs = (count - 1) // 2
    donor, taker = lengths[1:1 + 2 * pairs:2], lengths[2:2 + 2 * pairs:2]
    room = jnp.minimum(donor - 1, reach - taker)
    shifted = jax.random.randint(jax.random.fold_in(key, 1), (pairs,), 0, 1 << 20) % (room + 1)
    lengths = lengths.at[1:1 + 2 * pairs:2].set(donor - shifted).at[2:2 + 2 * pairs:2].set(taker + shifted)
    return lengths[jax.random.permutation(jax.random.fold_in(key, 2), count)]


def normal_values(key, shape, width, most, cuts=(), kind=jnp.bfloat16):
    array = width * jax.random.normal(key, shape, jnp.float32)
    if cuts:
        array = array * block_levels(key, shape, cuts, -0.22, 0.18)
    return jnp.clip(array, -most, most).astype(kind)


def setup_inputs(seed: int = 0) -> dict:
    splits = jax.random.split(jax.random.key(seed), 23)
    return {
        "frames_in": draw_frames_in(jax.random.fold_in(splits[22], 71), 0),
        "item_lengths": ragged_sizes(splits[1], ITEMS, FRAMES, 2 * AVG_LEN, 2).astype(jnp.int32),
        "out_cotangent": draw_out_cotangent(jax.random.fold_in(splits[22], 71), 0),
        "skip_cotangent": draw_skip_cotangent(jax.random.fold_in(splits[22], 71), 0),
        "expand": normal_values(splits[4], (N, H), N ** -0.5, 0.5, ((1, 2),), jnp.float32),
        "expand_moment": normal_values(splits[5], (N, H), (0.555 / (3 * N * H + 9 * H + 2 * N + 2) ** 0.5), 0.0078125, ((1, 2),), jnp.float32),
        "expand_square": jnp.clip(jnp.exp(math.log(9.926839084073436e-07) - 2.7725887 * jax.random.uniform(splits[6], (N, H), jnp.float32) ** block_levels(splits[6], (N, H), ((1, 2),), -0.2, 0.2)), 6.204274427545897e-08, 9.926839084073436e-07),
        "depthwise": normal_values(splits[7], (3, H), 3 ** -0.5, 3.5, ((1, 2),), jnp.float32),
        "depth_moment": normal_values(splits[8], (3, H), (0.555 / (3 * N * H + 9 * H + 2 * N + 2) ** 0.5), 0.0078125, ((1, 2),), jnp.float32),
        "depth_square": jnp.clip(jnp.exp(math.log(9.926839084073436e-07) - 2.7725887 * jax.random.uniform(splits[9], (3, H), jnp.float32) ** block_levels(splits[9], (3, H), ((1, 2),), -0.2, 0.2)), 6.204274427545897e-08, 9.926839084073436e-07),
        "project": draw_project(jax.random.fold_in(splits[22], 71), 0),
        "project_moment": normal_values(splits[11], (2, H, N), (0.555 / (3 * N * H + 9 * H + 2 * N + 2) ** 0.5), 0.0078125, ((1, 2),), jnp.float32),
        "project_square": jnp.clip(jnp.exp(math.log(9.926839084073436e-07) - 2.7725887 * jax.random.uniform(splits[12], (2, H, N), jnp.float32) ** block_levels(splits[12], (2, H, N), ((1, 2),), -0.2, 0.2)), 6.204274427545897e-08, 9.926839084073436e-07),
        "channel_vectors": jnp.clip(0.5 + 1.0 * jax.random.uniform(splits[13], (6, H), jnp.float32) ** block_levels(splits[13], (6, H), ((1, 2),), -0.2, 0.2), 0.5, 1.5),
        "vector_moment": normal_values(splits[14], (6, H), (0.555 / (3 * N * H + 9 * H + 2 * N + 2) ** 0.5), 0.0078125, ((1, 2),), jnp.float32),
        "vector_square": jnp.clip(jnp.exp(math.log(9.926839084073436e-07) - 2.7725887 * jax.random.uniform(splits[15], (6, H), jnp.float32) ** block_levels(splits[15], (6, H), ((1, 2),), -0.2, 0.2)), 6.204274427545897e-08, 9.926839084073436e-07),
        "output_biases": normal_values(splits[16], (2, N), 0.5, 3.0, (), jnp.float32),
        "bias_moment": normal_values(splits[17], (2, N), (0.555 / (3 * N * H + 9 * H + 2 * N + 2) ** 0.5), 0.0078125, (), jnp.float32),
        "bias_square": jnp.clip(jnp.exp(jax.random.uniform(splits[18], (2, N), jnp.float32, math.log(6.204274427545897e-08), math.log(9.926839084073436e-07))), 6.204274427545897e-08, 9.926839084073436e-07),
        "prelu_slopes": jnp.clip(jax.random.uniform(splits[19], (2,), jnp.float32, 0.1, 0.4), 0.1, 0.4),
        "slope_moment": normal_values(splits[20], (2,), (11.1 / (3 * N * H + 9 * H + 2 * N + 2) ** 0.5), 0.15625, (), jnp.float32),
        "slope_square": jnp.clip(jnp.exp(jax.random.uniform(splits[21], (2,), jnp.float32, math.log(2.481709816493094e-05), math.log(0.00039707357))), 2.481709816493094e-05, 0.00039707357),
    }


norm_eps = 1e-06
clip_level = 5.0
rate = 0.05
small_rate = 0.5
beta_first = 0.9
beta_second = 0.999
adam_eps = 1e-08
decay = 0.01
step_count = 10.0

@jax.custom_vjp
def low(v):
    return lax.optimization_barrier(v.astype(jnp.bfloat16)).astype(jnp.float32)

@jax.custom_vjp
def low_back(v):
    return v

def low_keep(v):
    return (low(v), None)

def low_pass(kept, grad):
    return (grad,)

def back_keep(v):
    return (v, None)

def back_low(kept, grad):
    return (low(grad),)
low.defvjp(low_keep, low_pass)
low_back.defvjp(back_keep, back_low)

def prelu(value_entries, slope_value):
    return jnp.where(value_entries > 0, value_entries, slope_value * value_entries)

def group_norm(active, gain_vector_row, shift_vector_row, item_ids, element_count):
    groups = element_count.shape[0]
    item_mean = jax.ops.segment_sum(lax.optimization_barrier(jnp.sum(active, axis=1)), item_ids, num_segments=groups) / element_count
    mean_removed = active - item_mean[item_ids][:, None]
    item_spread = jax.ops.segment_sum(lax.optimization_barrier(jnp.sum(mean_removed * mean_removed, axis=1)), item_ids, num_segments=groups) / element_count
    return gain_vector_row * (mean_removed * lax.rsqrt(item_spread + norm_eps)[item_ids][:, None]) + shift_vector_row

def dilated(value_entries, taps, item_ids, whole_frames):
    frame_positions = jnp.arange(whole_frames, dtype=jnp.int32)
    result = jnp.zeros(value_entries.shape, jnp.float32)
    for tap_position_index in range(3):
        source_frames = (frame_positions + (tap_position_index - 1) * DILATION_STEP).astype(jnp.int32)
        inside_window = (source_frames >= 0) & (source_frames < whole_frames)
        clipped = jnp.clip(source_frames, 0, whole_frames - 1).astype(jnp.int32)
        usable = inside_window & (item_ids[clipped] == item_ids)
        result = result + taps[tap_position_index] * jnp.where(usable[:, None], value_entries[clipped], 0.0)
    return result

def adam(weight, moment, square, incoming_gradient, clip_scale, step_rate):
    clipped = incoming_gradient * clip_scale
    moment_next = beta_first * moment + (1.0 - beta_first) * clipped
    square_next = beta_second * square + (1.0 - beta_second) * clipped * clipped
    update = moment_next / (1.0 - beta_first ** step_count) / (jnp.sqrt(square_next / (1.0 - beta_second ** step_count)) + adam_eps)
    return (weight - step_rate * (update + decay * weight), moment_next, square_next)

def reference(frames_in, item_lengths, out_cotangent, skip_cotangent, expand, expand_moment, expand_square, depthwise, depth_moment, depth_square, project, project_moment, project_square, channel_vectors, vector_moment, vector_square, output_biases, bias_moment, bias_square, prelu_slopes, slope_moment, slope_square):
    whole_frames = frames_in.shape[0]
    starts = jnp.cumsum(item_lengths) - item_lengths
    frame_positions = jnp.arange(whole_frames, dtype=jnp.int32)
    item_ids = (lax.optimization_barrier(jnp.sum((frame_positions[:, None] >= starts[None, :]).astype(jnp.int32), axis=1)) - 1).astype(jnp.int32)
    element_count = item_lengths.astype(jnp.float32) * H
    highest = lax.Precision.HIGHEST

    def forward(inputs, w_expand, w_depth, w_project, parameter_vectors, biases, slopes):
        hidden_state = low_back(jnp.dot(low(inputs), low(w_expand), precision=highest) + parameter_vectors[0])
        normalized_values = low(group_norm(prelu(hidden_state, slopes[0]), parameter_vectors[1], parameter_vectors[2], item_ids, element_count))
        depthwise_output = low_back(dilated(normalized_values, w_depth, item_ids, whole_frames) + parameter_vectors[3])
        mixed = low(group_norm(prelu(depthwise_output, slopes[1]), parameter_vectors[4], parameter_vectors[5], item_ids, element_count))
        residual = jnp.dot(mixed, low(w_project[0]), precision=highest) + biases[0]
        skipped = jnp.dot(mixed, low(w_project[1]), precision=highest) + biases[1]
        return (inputs + residual, skipped)
    outputs, pull = jax.vjp(forward, frames_in.astype(jnp.float32), expand, depthwise, project, channel_vectors, output_biases, prelu_slopes)
    grads = pull((out_cotangent.astype(jnp.float32), skip_cotangent.astype(jnp.float32)))
    total_squares = jnp.float32(0.0)
    for piece in grads[1:]:
        total_squares = total_squares + jnp.sum(piece * piece)
    grad_norm = jnp.sqrt(total_squares)
    clip_scale = jnp.minimum(1.0, clip_level / grad_norm)
    expand_set = adam(expand, expand_moment, expand_square, grads[1], clip_scale, rate)
    depth_set = adam(depthwise, depth_moment, depth_square, grads[2], clip_scale, small_rate)
    project_set = adam(project, project_moment, project_square, grads[3], clip_scale, rate)
    vector_set = adam(channel_vectors, vector_moment, vector_square, grads[4], clip_scale, small_rate)
    bias_set = adam(output_biases, bias_moment, bias_square, grads[5], clip_scale, small_rate)
    slope_set = adam(prelu_slopes, slope_moment, slope_square, grads[6], clip_scale, small_rate)
    return (outputs[0].astype(jnp.bfloat16), outputs[1].astype(jnp.bfloat16), grads[0], grad_norm, expand_set[0], expand_set[1], expand_set[2], depth_set[0], depth_set[1], depth_set[2], project_set[0], project_set[1], project_set[2], vector_set[0], vector_set[1], vector_set[2], bias_set[0], bias_set[1], bias_set[2], slope_set[0], slope_set[1], slope_set[2])
```

```python
import functools

import jax
import jax.numpy as jnp
from jax import lax
from jax.experimental import pallas as pl
from jax.experimental.pallas import tpu as pltpu
from jax.sharding import PartitionSpec as P

F32 = jnp.float32
BF16 = jnp.bfloat16
MESH = pl.DeviceIdType.MESH

DILATION = 16
HALO = 2 * DILATION
LONGEST_ITEM = 8192
LANES = 128
ROWS = 64
BLOCK = 512
PIECES = 16

norm_eps = 1e-06
clip_level = 5.0
rate = 0.05
small_rate = 0.5
beta_first = 0.9
beta_second = 0.999
adam_eps = 1e-08
decay = 0.01
step_count = 10.0

TAP_ROW = 6
BIAS_ROW = 9
SLOPE_TWO_ROW = 10
SLOPE_ONE_ROW = 11
SQUARES_ROW = 12

(GAIN_TWO, SHIFT_TWO, TAP_A, TAP_B, TAP_C, DEPTH_BIAS, GAIN_ONE, SHIFT_ONE, SLOPE_TWO, SLOPE_ONE, COLUMN_SUMS) = range(11)


def dot(a, b):
    return lax.dot_general(a, b, (((1,), (0,)), ((), ())), preferred_element_type=F32)


def dot_rows(a, b):
    return lax.dot_general(a, b, (((1,), (1,)), ((), ())), preferred_element_type=F32)


def dot_frames(a, b):
    return lax.dot_general(a, b, (((0,), (0,)), ((), ())), preferred_element_type=F32)


def rounded(v):
    return v.astype(BF16).astype(F32)


def spread_lanes(v):
    return jnp.broadcast_to(jnp.sum(v, axis=1, keepdims=True), (v.shape[0], LANES))


def fold_rows(v):
    return jnp.sum(v.reshape(v.shape[0] // 8, 8, v.shape[1]), axis=0)


def block_kernel(
    tm_size,
    item_count,
    item_pad,
    len_ref,
    slope_ref,
    frames_ref,
    out_cot_ref,
    skip_cot_ref,
    expand_ref,
    project_ref,
    taps_ref,
    vectors_ref,
    biases_ref,
    block_ref,
    skip_ref,
    input_grad_ref,
    expand_grad_ref,
    project_grad_ref,
    small_grad_ref,
    x,
    cots,
    w_expand,
    w_project,
    params,
    item_rows,
    item_cols,
    mask_low,
    mask_high,
    table,
    counts,
    act_one,
    xhat_one,
    normed,
    mixed_grad,
    act_two,
    mixed,
    hidden_grad,
    seg,
    column,
    block_out,
    skip_out,
    input_out,
    tile_one,
    tile_two,
    tile_three,
    stats_one,
    stats_two,
    stats_three,
    project_part,
    expand_part,
    project_in,
    expand_in,
    small_part,
    small_in,
    late_part,
    late_in,
    project_sum,
    expand_sum,
    small_sum,
    late_sum,
    square_part,
    square_in,
    local_sem,
    out_sem,
    send_sem,
    recv_sem,
):
    frames = block_out.shape[0]
    wide = x.shape[0]
    half = expand_ref.shape[1]
    hidden = 2 * half
    blocks = hidden // LANES
    devices = 2 * tm_size
    stride = tm_size // PIECES
    spans = -(-LONGEST_ITEM // frames)
    chan = lax.axis_index("chan")
    tm = lax.axis_index("tm")
    me = tm * 2 + chan
    other = 1 - chan

    def device(index):
        return {"chan": lax.rem(index, 2), "tm": lax.div(index, 2)}

    def remote(src, dst, phase, target):
        return pltpu.make_async_remote_copy(
            src_ref=src,
            dst_ref=dst,
            send_sem=send_sem.at[phase],
            recv_sem=recv_sem.at[phase],
            device_id=target,
            device_id_type=MESH,
        )

    def wait_bytes(ref, sem):
        pltpu.make_async_copy(ref, ref, sem).wait()

    own = pl.ds(HALO, frames)
    loads = [
        pltpu.make_async_copy(frames_ref, x.at[own, :], local_sem.at[0]),
        pltpu.make_async_copy(out_cot_ref, cots.at[own, pl.ds(0, LANES)], local_sem.at[1]),
        pltpu.make_async_copy(skip_cot_ref, cots.at[own, pl.ds(LANES, LANES)], local_sem.at[2]),
    ]
    for load in loads:
        load.start()

    barrier = pltpu.get_barrier_semaphore()

    def greet(k, carry):
        pl.semaphore_signal(
            barrier, inc=1, device_id=device(lax.rem(me + k, devices)), device_id_type=MESH
        )
        return carry

    lax.fori_loop(1, devices, greet, 0)

    my_half = pl.ds(pl.multiple_of(chan * half, half), half)
    w_expand[:, my_half] = expand_ref[...].astype(BF16)
    w_project[my_half, 0:LANES] = project_ref[0].astype(BF16)
    w_project[my_half, LANES : 2 * LANES] = project_ref[1].astype(BF16)
    params[0:6, my_half] = vectors_ref[...]
    params[6:9, my_half] = taps_ref[...]
    params[9:16, my_half] = jnp.zeros((7, half), F32)

    width = table.shape[0]
    lane = lax.broadcasted_iota(jnp.int32, (8, width), 1)
    lane_item = lax.rem(lane, item_pad)
    row_item = lax.broadcasted_iota(jnp.int32, (item_pad, LANES), 0)

    def bounds(j, carry):
        lane_start, lane_end, row_start, row_end = carry
        length = len_ref[j]
        return (
            lane_start + jnp.where(lane_item > j, length, 0),
            lane_end + jnp.where(lane_item >= j, length, 0),
            row_start + jnp.where(row_item > j, length, 0),
            row_end + jnp.where(row_item >= j, length, 0),
        )

    lane_zero, row_zero = jnp.zeros_like(lane), jnp.zeros_like(row_item)
    lane_start, lane_end, row_start, row_end = lax.fori_loop(
        0, item_count, bounds, (lane_zero, lane_zero, row_zero, row_zero)
    )
    lane_end = jnp.where(lane < 3 * item_pad, lane_end, lane_start)
    first = me * frames
    lane_start_row, lane_end_row = lane_start[0:1], lane_end[0:1]
    elements = jnp.maximum((row_end - row_start).astype(F32) * hidden, 1.0)

    def count_of(index):
        low = jnp.maximum(row_start, index * frames)
        high = jnp.minimum(row_end, (index + 1) * frames)
        return jnp.maximum(high - low, 0).astype(F32) * hidden

    my_count = count_of(me)
    my_safe = jnp.maximum(my_count, 1.0)
    offsets = [o for o in range(-spans, spans + 1) if o != 0]
    for slot, offset in enumerate(offsets):
        counts[slot] = count_of(lax.rem(me - offset + devices, devices))
    column[...] = jnp.zeros_like(column)

    def put_table(place, v):
        high = v.astype(BF16)
        rest = v - high.astype(F32)
        middle = rest.astype(BF16)
        low = (rest - middle.astype(F32)).astype(BF16)
        where = slice(place * LANES, (place + 1) * LANES)
        table[0:item_pad, where] = high
        table[item_pad : 2 * item_pad, where] = middle
        table[2 * item_pad : 3 * item_pad, where] = low

    def rows_of(r, n, count):
        return dot(item_rows[pl.ds(r, n), :], table[:, 0 : count * LANES])

    def part(values, k, n, b):
        return values[k : k + n, b * LANES : (b + 1) * LANES]

    def put_seg(r, n, place, v):
        high = v.astype(BF16)
        seg[pl.ds(r, n), pl.ds(2 * place * LANES, LANES)] = high
        seg[pl.ds(r, n), pl.ds((2 * place + 1) * LANES, LANES)] = (v - high.astype(F32)).astype(BF16)

    def item_sums(count):
        sums = dot(item_cols[...], seg[:, 0 : 2 * count * LANES])
        return [
            spread_lanes(
                sums[:, 2 * k * LANES : (2 * k + 1) * LANES]
                + sums[:, (2 * k + 1) * LANES : (2 * k + 2) * LANES]
            )
            for k in range(count)
        ]

    def loop(start, size, count, body, rep=1):
        def step(i, carry):
            i = i if rep == 1 else lax.rem(i, count)
            body(pl.multiple_of(start + i * size, 16))
            return carry

        lax.fori_loop(0, count * rep, step, 0)

    def at(r, k, shift=0):
        return pl.multiple_of(r + (k - shift), 16)

    table[...] = jnp.zeros_like(table)
    put_table(0, row_start.astype(F32))
    put_table(1, row_end.astype(F32))

    wide_block = wide // 4
    wide_rows = wide_block // 11

    @functools.partial(loop, 0, wide_block, 4)
    def _(r):
        for k in range(0, wide_block, wide_rows):
            position = first - HALO + r + k + lax.broadcasted_iota(jnp.int32, (wide_rows, width), 0)
            inside = (position >= lane_start_row) & (position < lane_end_row)
            item_rows[pl.ds(at(r, k), wide_rows), :] = inside.astype(F32).astype(BF16)
        ends = rows_of(r, wide_block, 2)
        for k in range(0, wide_block, wide_rows):
            here = first - HALO + r + k + lax.broadcasted_iota(jnp.int32, (wide_rows, LANES), 0)
            here = here.astype(F32)
            after = here - part(ends, k, wide_rows, 0)
            before = part(ends, k, wide_rows, 1) - here
            mask_low[pl.ds(at(r, k), wide_rows), :] = (after >= DILATION).astype(F32)
            mask_high[pl.ds(at(r, k), wide_rows), :] = (before > DILATION).astype(F32)

    for i in range(frames // LANES):
        position = first + i * LANES + lax.broadcasted_iota(jnp.int32, (item_pad, LANES), 1)
        inside = (position >= row_start) & (position < row_end)
        item_cols[:, i * LANES : (i + 1) * LANES] = inside.astype(F32).astype(BF16)

    loads[0].wait()
    pl.semaphore_wait(barrier, devices - 1)

    partner = device(tm * 2 + other)
    left, right = device(lax.rem(me + devices - 1, devices)), device(lax.rem(me + 1, devices))
    sends = [
        remote(w_expand.at[:, my_half], w_expand.at[:, my_half], 0, partner),
        remote(params.at[:, my_half], params.at[:, my_half], 1, partner),
        remote(x.at[pl.ds(HALO, HALO), :], x.at[pl.ds(HALO + frames, HALO), :], 2, left),
        remote(x.at[pl.ds(frames, HALO), :], x.at[pl.ds(0, HALO), :], 3, right),
        remote(w_project.at[my_half, :], w_project.at[my_half, :], 4, partner),
    ]
    for send in sends:
        send.start()
    loads[1].wait()
    loads[2].wait()
    edges = [
        remote(
            cots.at[pl.ds(HALO, DILATION), :], cots.at[pl.ds(HALO + frames, DILATION), :], 5, left
        ),
        remote(
            cots.at[pl.ds(HALO + frames - DILATION, DILATION), :],
            cots.at[pl.ds(HALO - DILATION, DILATION), :],
            6,
            right,
        ),
    ]
    for send in edges:
        send.start()

    slope_one, slope_two = slope_ref[0], slope_ref[1]

    def lanes_of(which, b):
        return pl.ds(pl.multiple_of(which * half + b * LANES, LANES), LANES)

    def half_of(which):
        return pl.ds(pl.multiple_of(which * half, half), half)

    def activate(product, k, n, which, b):
        v = part(product, k, n, b) + params[0:1, lanes_of(which, b)]
        return jnp.maximum(v, slope_one * v)

    own_loop = functools.partial(functools.partial, loop, HALO, BLOCK, frames // BLOCK)

    @own_loop()
    def _(r):
        product = dot(x[pl.ds(r, BLOCK), :], w_expand[:, half_of(chan)])
        for k in range(0, BLOCK, ROWS):
            total = jnp.zeros((ROWS, LANES), F32)
            for b in range(blocks // 2):
                a = activate(product, k, ROWS, chan, b)
                act_one[pl.ds(at(r, k), ROWS), lanes_of(chan, b)] = a
                total = total + a
            put_seg(at(r, k, HALO), ROWS, 0, total)

    (total,) = item_sums(1)
    shift = total / jnp.maximum(my_count * 0.5, 1.0)
    put_table(0, shift)
    for k in range(4):
        sends[k].wait_recv()

    @own_loop()
    def _(r):
        centres = rows_of(r, BLOCK, 1)
        product = dot(x[pl.ds(r, BLOCK), :], w_expand[:, half_of(other)])
        for k in range(0, BLOCK, ROWS):
            rows = pl.ds(at(r, k), ROWS)
            centre = part(centres, k, ROWS, 0)
            total = jnp.zeros((ROWS, LANES), F32)
            squares = jnp.zeros((ROWS, LANES), F32)
            for b in range(blocks // 2):
                d = act_one[rows, lanes_of(chan, b)] - centre
                total = total + d
                squares = squares + d * d
                a = activate(product, k, ROWS, other, b)
                act_one[rows, lanes_of(other, b)] = a
                d = a - centre
                total = total + d
                squares = squares + d * d
            put_seg(at(r, k, HALO), ROWS, 0, total)
            put_seg(at(r, k, HALO), ROWS, 1, squares)

    tile_lane = lax.broadcasted_iota(jnp.int32, (item_pad, LANES), 1)

    def pack_tile(values):
        tile = jnp.zeros((item_pad, LANES), F32)
        for k, v in enumerate(values):
            tile = jnp.where(tile_lane == k, v, tile)
        return tile

    def lane_of(tile, k):
        return spread_lanes(jnp.where(tile_lane == k, tile, 0.0))

    def local_moments(shift, total, squares):
        mean = shift + total / my_safe
        spread = jnp.maximum(squares - total * total / my_safe, 0.0)
        return mean, spread

    def exchange(tile, stats, phase):
        for slot, offset in enumerate(offsets):
            target = device(lax.rem(me + offset + devices, devices))
            remote(tile, stats.at[slot], phase, target).start()

    def arrived(stats, phase):
        wait_bytes(stats, recv_sem.at[phase])

    def combined(tile, stats):
        tiles = [tile[...]] + [stats[slot] for slot in range(len(offsets))]
        sizes = [my_count] + [counts[slot] for slot in range(len(offsets))]
        plain = tiles[0]
        for t in tiles[1:]:
            plain = plain + t
        mean = lane_of(plain, 0) / elements
        between = jnp.zeros((item_pad, LANES), F32)
        for t, size in zip(tiles, sizes):
            gap = t - mean
            between = between + size * gap * gap
        spread = (lane_of(plain, 1) + lane_of(between, 2)) / elements
        return tiles, plain, mean, lax.rsqrt(spread + norm_eps)

    total, squares = item_sums(2)
    mean, spread = local_moments(shift, total, squares)
    tile_one[...] = pack_tile([mean * my_count, spread, mean])
    exchange(tile_one, stats_one, 7)

    for r in (0, HALO + frames):
        for which in (chan, other):
            product = dot(x[pl.ds(r, HALO), :], w_expand[:, half_of(which)])
            for b in range(blocks // 2):
                act_one[pl.ds(r, HALO), lanes_of(which, b)] = activate(product, 0, HALO, which, b)

    sends[4].wait_recv()
    for send in edges:
        send.wait_recv()

    def lanes(b):
        return pl.ds(b * LANES, LANES)

    def mixed_rows(r, n, size, add):
        product = dot_rows(cots[pl.ds(r, n), :], w_project[...])
        for k in range(0, n, size):
            total = jnp.zeros((size, LANES), F32)
            for b in range(blocks):
                y = part(product, k, size, b)
                mixed_grad[pl.ds(at(r, k), size), lanes(b)] = y
                if add:
                    total = total + params[4:5, lanes(b)] * y
                    column[SHIFT_TWO, :, lanes(b)] += fold_rows(y)
            if add:
                put_seg(at(r, k, HALO), size, 2, total)

    @own_loop()
    def _(r):
        mixed_rows(r, BLOCK, ROWS, True)

    for r in (HALO - DILATION, HALO + frames):
        mixed_rows(r, DILATION, DILATION, False)
    bias_sum = dot(jnp.ones((16, frames), BF16), cots[own, :])[0:1]

    arrived(stats_one, 7)
    _, _, mean_one, scale_one = combined(tile_one, stats_one)
    put_table(0, mean_one)
    put_table(1, scale_one)

    @functools.partial(loop, 0, wide_block, 4)
    def _(r):
        values = rows_of(r, wide_block, 2)
        for k in range(0, wide_block, wide_rows):
            rows = pl.ds(at(r, k), wide_rows)
            mean, scale = part(values, k, wide_rows, 0), part(values, k, wide_rows, 1)
            for b in range(blocks):
                xhat = (act_one[rows, lanes(b)] - mean) * scale
                xhat_one[rows, lanes(b)] = xhat
                normed[rows, lanes(b)] = rounded(
                    params[1:2, lanes(b)] * xhat + params[2:3, lanes(b)]
                )

    def depth_rows(r, n, b):
        low, high = mask_low[pl.ds(r, n), :], mask_high[pl.ds(r, n), :]
        v = (
            params[3:4, lanes(b)]
            + params[6:7, lanes(b)] * (low * normed[pl.ds(r - DILATION, n), lanes(b)])
            + params[7:8, lanes(b)] * normed[pl.ds(r, n), lanes(b)]
            + params[8:9, lanes(b)] * (high * normed[pl.ds(r + DILATION, n), lanes(b)])
        )
        return jnp.maximum(v, slope_two * v)

    @own_loop()
    def _(r):
        for k in range(0, BLOCK, ROWS):
            a = depth_rows(at(r, k), ROWS, 0)
            act_two[pl.ds(at(r, k), ROWS), lanes(0)] = a
            put_seg(at(r, k, HALO), ROWS, 0, a)

    (total,) = item_sums(1)
    shift = total / jnp.maximum(my_count * (1.0 / blocks), 1.0)
    put_table(0, shift)

    @own_loop()
    def _(r):
        centres = rows_of(r, BLOCK, 1)
        for k in range(0, BLOCK, ROWS):
            rows = pl.ds(at(r, k), ROWS)
            centre = part(centres, k, ROWS, 0)
            total = jnp.zeros((ROWS, LANES), F32)
            squares = jnp.zeros((ROWS, LANES), F32)
            crossed = jnp.zeros((ROWS, LANES), F32)
            for b in range(blocks):
                if b == 0:
                    a = act_two[rows, lanes(b)]
                else:
                    a = depth_rows(at(r, k), ROWS, b)
                    act_two[rows, lanes(b)] = a
                d = a - centre
                total = total + d
                squares = squares + d * d
                crossed = crossed + params[4:5, lanes(b)] * mixed_grad[rows, lanes(b)] * d
            put_seg(at(r, k, HALO), ROWS, 0, total)
            put_seg(at(r, k, HALO), ROWS, 1, squares)
            put_seg(at(r, k, HALO), ROWS, 3, crossed)

    total, squares, q_sum, crossed = item_sums(4)
    mean, spread = local_moments(shift, total, squares)
    crossed = crossed - (mean - shift) * q_sum
    tile_two[...] = pack_tile([mean * my_count, spread, mean, q_sum, crossed])
    exchange(tile_two, stats_two, 8)

    for r in (HALO - DILATION, HALO + frames):
        for b in range(blocks):
            act_two[pl.ds(r, DILATION), lanes(b)] = depth_rows(r, DILATION, b)

    arrived(stats_two, 8)
    tiles, plain, mean_two, scale_two = combined(tile_two, stats_two)
    cross_sum = lane_of(plain, 4)
    for t in tiles:
        cross_sum = cross_sum + (lane_of(t, 2) - mean_two) * lane_of(t, 3)
    put_table(0, mean_two)
    put_table(1, scale_two)
    put_table(2, scale_two * lane_of(plain, 3) / elements)
    put_table(3, scale_two * scale_two * cross_sum / elements)

    def second_back(r, n, size, add):
        values = rows_of(r, n, 4)
        for k in range(0, n, size):
            rows = pl.ds(at(r, k), size)
            mean, scale, q_mean, cross_mean = [part(values, k, size, j) for j in range(4)]
            for b in range(blocks):
                a = act_two[rows, lanes(b)]
                y = mixed_grad[rows, lanes(b)]
                xhat = (a - mean) * scale
                g = (params[4:5, lanes(b)] * y) * scale - q_mean - xhat * cross_mean
                act_two[rows, lanes(b)] = rounded(g * jnp.where(a > 0, 1.0, slope_two))
                if add:
                    mixed[pl.ds(at(r, k, HALO), size), lanes(b)] = (
                        params[4:5, lanes(b)] * xhat + params[5:6, lanes(b)]
                    ).astype(BF16)
                    column[GAIN_TWO, :, lanes(b)] += fold_rows(y * xhat)
                    column[SLOPE_TWO, :, lanes(b)] += fold_rows(g * jnp.minimum(a, 0.0))

    @own_loop()
    def _(r):
        second_back(r, BLOCK, ROWS, True)

    for r in (HALO - DILATION, HALO + frames):
        second_back(r, DILATION, DILATION, False)

    @functools.partial(loop, HALO, 2 * ROWS, frames // (2 * ROWS))
    def _(r):
        for k in range(0, 2 * ROWS, ROWS):
            rows = pl.ds(at(r, k), ROWS)
            low, high = mask_low[rows, :], mask_high[rows, :]
            total = jnp.zeros((ROWS, LANES), F32)
            crossed = jnp.zeros((ROWS, LANES), F32)
            for b in range(blocks):
                later = high * act_two[pl.ds(at(r, k + DILATION), ROWS), lanes(b)]
                here = act_two[rows, lanes(b)]
                earlier = low * act_two[pl.ds(at(r, k - DILATION), ROWS), lanes(b)]
                n = normed[rows, lanes(b)]
                column[TAP_A, :, lanes(b)] += fold_rows(later * n)
                column[TAP_B, :, lanes(b)] += fold_rows(here * n)
                column[TAP_C, :, lanes(b)] += fold_rows(earlier * n)
                column[DEPTH_BIAS, :, lanes(b)] += fold_rows(here)
                y = (
                    params[6:7, lanes(b)] * later
                    + params[7:8, lanes(b)] * here
                    + params[8:9, lanes(b)] * earlier
                )
                column[SHIFT_ONE, :, lanes(b)] += fold_rows(y)
                xhat = xhat_one[rows, lanes(b)]
                column[GAIN_ONE, :, lanes(b)] += fold_rows(y * xhat)
                q = params[1:2, lanes(b)] * y
                mixed_grad[rows, lanes(b)] = q
                total = total + q
                crossed = crossed + q * xhat
            put_seg(at(r, k, HALO), ROWS, 0, total)
            put_seg(at(r, k, HALO), ROWS, 1, crossed)

    total, crossed = item_sums(2)
    tile_three[...] = pack_tile([total, crossed])
    exchange(tile_three, stats_three, 9)

    @own_loop()
    def _(r):
        product = dot(mixed[pl.ds(at(r, 0, HALO), BLOCK), :], w_project[...])
        for k in range(0, BLOCK, ROWS):
            rows = pl.ds(at(r, k, HALO), ROWS)
            inputs = x[pl.ds(at(r, k), ROWS), :].astype(F32)
            block_out[rows, :] = (
                inputs + part(product, k, ROWS, 0) + biases_ref[0:1, :]
            ).astype(BF16)
            skip_out[rows, :] = (part(product, k, ROWS, 1) + biases_ref[1:2, :]).astype(BF16)

    stores = [
        pltpu.make_async_copy(block_out, block_ref, out_sem.at[0]),
        pltpu.make_async_copy(skip_out, skip_ref, out_sem.at[1]),
    ]
    for store in stores:
        store.start()

    step = 512
    total = jnp.zeros((2 * LANES, hidden), F32)
    for k in range(frames // step):
        total = total + dot_frames(
            cots[pl.ds(HALO + k * step, step), :], mixed[pl.ds(k * step, step), :]
        )
    project_part[...] = total

    def column_sum(which):
        return jnp.sum(column[which], axis=0, keepdims=True)

    early_rows = {
        1: column_sum(GAIN_ONE),
        2: column_sum(SHIFT_ONE),
        3: column_sum(DEPTH_BIAS),
        4: column_sum(GAIN_TWO),
        5: column_sum(SHIFT_TWO),
        TAP_ROW: column_sum(TAP_A),
        TAP_ROW + 1: column_sum(TAP_B),
        TAP_ROW + 2: column_sum(TAP_C),
    }
    slope_two_row = column_sum(SLOPE_TWO)
    slope_two_row = (slope_two_row[:, 0:half] + slope_two_row[:, half:hidden]) / slope_two
    for c in range(2):
        small_part[c] = jnp.zeros((16, half), F32)
        for row, v in early_rows.items():
            small_part[c, row : row + 1, :] = v[:, c * half : (c + 1) * half]
        small_part[c, BIAS_ROW : BIAS_ROW + 1, :] = bias_sum
        small_part[c, SLOPE_TWO_ROW : SLOPE_TWO_ROW + 1, :] = slope_two_row

    reducers = 2 * PIECES
    piece = lax.div(tm, stride)
    place = piece * 2 + chan

    def when_reducer(body):
        if stride == 1:
            body()
        else:
            pl.when(lax.rem(tm, stride) == 0)(body)

    def reducer_device(q):
        return lax.rem(q, 2), lax.div(q, 2) * stride

    def to_reducers(send):
        def one(k, carry):
            q = lax.rem(place + k, reducers)
            c, t = reducer_device(q)
            if stride == 1:
                send(q, {"chan": c, "tm": t})
            else:

                @pl.when(t * 2 + c != me)
                def _():
                    send(q, {"chan": c, "tm": t})

            return carry

        lax.fori_loop(1 if stride == 1 else 0, reducers, one, 0)

    def project_piece(q):
        rows = pl.ds(pl.multiple_of(lax.div(q, 2) * 16, 16), 16)
        return rows, pl.ds(pl.multiple_of(lax.rem(q, 2) * half, half), half)

    def expand_piece(q):
        j, c = lax.div(q, 2), lax.rem(q, 2)
        rows = pl.ds(pl.multiple_of(lax.div(j, 2) * 16, 16), 16)
        at = c * half + lax.rem(j, 2) * LANES
        return rows, pl.ds(pl.multiple_of(at, LANES), LANES)

    def send_project(q, target):
        rows, cols = project_piece(q)
        remote(project_part.at[rows, cols], project_in.at[me], 10, target).start()

    to_reducers(send_project)
    for c in range(2):

        @pl.when((tm != 0) | (chan != c))
        def _(c=c):
            remote(small_part.at[c], small_in.at[me], 11, {"chan": c, "tm": 0}).start()

    arrived(stats_three, 9)
    plain = tile_three[...]
    for slot in range(len(offsets)):
        plain = plain + stats_three[slot]
    put_table(0, lane_of(plain, 0) / elements)
    put_table(1, lane_of(plain, 1) / elements)
    put_table(2, scale_one)

    @own_loop()
    def _(r):
        values = rows_of(r, BLOCK, 3)
        for k in range(0, BLOCK, ROWS):
            rows, local = pl.ds(at(r, k), ROWS), pl.ds(at(r, k, HALO), ROWS)
            q_mean, cross_mean, scale = [part(values, k, ROWS, j) for j in range(3)]
            for b in range(blocks):
                a = act_one[rows, lanes(b)]
                g = (mixed_grad[rows, lanes(b)] - q_mean - xhat_one[rows, lanes(b)] * cross_mean) * scale
                column[SLOPE_ONE, :, lanes(b)] += fold_rows(g * jnp.minimum(a, 0.0))
                hidden_grad[local, lanes(b)] = (g * jnp.where(a > 0, 1.0, slope_one)).astype(BF16)

    total = jnp.zeros((LANES, hidden), F32)
    for k in range(frames // step):
        total = total + dot_frames(
            x[pl.ds(HALO + k * step, step), :], hidden_grad[pl.ds(k * step, step), :]
        )
    expand_part[...] = total
    bias_one = dot(jnp.ones((16, frames), BF16), hidden_grad[...])[0:1]
    slope_row = column_sum(SLOPE_ONE)
    slope_row = (slope_row[:, 0:half] + slope_row[:, half:hidden]) / slope_one
    for c in range(2):
        late_part[c] = jnp.zeros((8, half), F32)
        late_part[c, 0:1, :] = bias_one[:, c * half : (c + 1) * half]
        late_part[c, 1:2, :] = slope_row

    def send_expand(q, target):
        rows, cols = expand_piece(q)
        remote(expand_part.at[rows, cols], expand_in.at[me], 12, target).start()

    to_reducers(send_expand)
    for c in range(2):

        @pl.when((tm != 0) | (chan != c))
        def _(c=c):
            remote(late_part.at[c], late_in.at[me], 13, {"chan": c, "tm": 0}).start()

    def to_group(send):
        def one(k, carry):
            send({"chan": chan, "tm": lax.rem(tm + k, tm_size)})
            return carry

        lax.fori_loop(1, tm_size, one, 0)

    my_sum_rows = pl.ds(pl.multiple_of(piece * 16, 16), 16)

    def sum_project():
        rows, cols = project_piece(place)
        wait_bytes(project_in.at[pl.ds(0, devices - 1)], recv_sem.at[10])
        project_in[me] = project_part[rows, cols]

        def add(k, total):
            return total + project_in[k]

        total = lax.fori_loop(0, devices, add, jnp.zeros((16, half), F32))
        project_sum[my_sum_rows, :] = total
        squares = jnp.sum(total * total, axis=0, keepdims=True)
        square_part[...] = squares[:, 0:LANES] + squares[:, LANES:half]

        def send(target):
            remote(project_sum.at[my_sum_rows, :], project_sum.at[my_sum_rows, :], 14, target).start()

        to_group(send)

    when_reducer(sum_project)

    @pl.when(tm == 0)
    def _():
        wait_bytes(small_in.at[pl.ds(0, devices - 1)], recv_sem.at[11])
        small_in[me] = small_part[chan]

        def add(k, total):
            return total + small_in[k]

        total = lax.fori_loop(0, devices, add, jnp.zeros((16, half), F32))
        small_sum[...] = total
        squares = jnp.sum((total * total)[0:BIAS_ROW], axis=0, keepdims=True)
        square_part[...] += squares[:, 0:LANES] + squares[:, LANES:half]

        def send(target):
            remote(small_sum, small_sum, 15, target).start()

        to_group(send)

    @own_loop()
    def _(r):
        product = dot_rows(hidden_grad[pl.ds(at(r, 0, HALO), BLOCK), :], w_expand[...])
        for k in range(0, BLOCK, ROWS):
            above = cots[pl.ds(at(r, k), ROWS), 0:LANES].astype(F32)
            input_out[pl.ds(at(r, k, HALO), ROWS), :] = above + part(product, k, ROWS, 0)

    stores.append(pltpu.make_async_copy(input_out, input_grad_ref, out_sem.at[2]))
    stores[2].start()

    def sum_piece(q):
        j = lax.div(q, 2)
        rows = pl.ds(pl.multiple_of(lax.div(j, 2) * 16, 16), 16)
        return rows, pl.ds(pl.multiple_of(lax.rem(j, 2) * LANES, LANES), LANES)

    @pl.when(tm == 0)
    def _():
        wait_bytes(late_in.at[pl.ds(0, devices - 1)], recv_sem.at[13])
        late_in[me] = late_part[chan]

        def add(k, total):
            return total + late_in[k]

        total = lax.fori_loop(0, devices, add, jnp.zeros((8, half), F32))
        late_sum[...] = total
        squares = (total * total)[0:1]
        square_part[...] += squares[:, 0:LANES] + squares[:, LANES:half]

        def send(target):
            remote(late_sum, late_sum, 16, target).start()

        to_group(send)

    def sum_expand():
        wait_bytes(expand_in.at[pl.ds(0, devices - 1)], recv_sem.at[12])
        rows, cols = expand_piece(place)
        expand_in[me] = expand_part[rows, cols]

        def add(k, total):
            return total + expand_in[k]

        total = lax.fori_loop(0, devices, add, jnp.zeros((16, LANES), F32))
        rows, cols = sum_piece(place)
        expand_sum[rows, cols] = total
        square_part[...] += jnp.sum(total * total, axis=0, keepdims=True)
        square_in[place] = square_part[...]

        def send(target):
            remote(expand_sum.at[rows, cols], expand_sum.at[rows, cols], 17, target).start()

        to_group(send)

        def send_square(k, carry):
            target = device(lax.rem(me + k, devices))
            remote(square_part, square_in.at[place], 18, target).start()
            return carry

        lax.fori_loop(1, devices, send_square, 0)

    when_reducer(sum_expand)

    def wait_group(ref, phase, mine):
        rows = ref.shape[0] // PIECES

        def some(count):
            wait_bytes(ref.at[pl.ds(0, count * rows)], recv_sem.at[phase])

        if stride == 1:
            some(PIECES - 1)
        else:
            is_reducer = lax.rem(tm, stride) == 0
            pl.when(is_reducer)(lambda: some(PIECES - 1))
            pl.when(jnp.logical_not(is_reducer))(lambda: some(PIECES))

    wait_group(project_sum, 14, None)
    for k in range(2):
        project_grad_ref[k] = project_sum[k * LANES : (k + 1) * LANES, :].T

    @pl.when(tm != 0)
    def _():
        wait_bytes(small_sum, recv_sem.at[15])
        wait_bytes(late_sum, recv_sem.at[16])

    small_grad_ref[...] = small_sum[...]
    small_grad_ref[0:1, :] = late_sum[0:1, :]
    small_grad_ref[SLOPE_ONE_ROW : SLOPE_ONE_ROW + 1, :] = late_sum[1:2, :]
    wait_group(expand_sum, 17, None)
    expand_grad_ref[...] = expand_sum[...]

    def wait_squares(count):
        wait_bytes(square_in.at[pl.ds(0, count)], recv_sem.at[18])

    if stride == 1:
        wait_squares(reducers - 1)
    else:
        is_reducer = lax.rem(tm, stride) == 0
        pl.when(is_reducer)(lambda: wait_squares(reducers - 1))
        pl.when(jnp.logical_not(is_reducer))(lambda: wait_squares(reducers))
    total = square_in[0]
    for q in range(1, reducers):
        total = total + square_in[q]
    small_grad_ref[SQUARES_ROW : SQUARES_ROW + 1, 0:LANES] = total
    small_grad_ref[SQUARES_ROW : SQUARES_ROW + 1, LANES:half] = jnp.zeros((1, half - LANES), F32)

    for send in sends + edges:
        send.wait_send()
    for phase, stats in ((7, stats_one), (8, stats_two), (9, stats_three)):
        wait_bytes(stats, send_sem.at[phase])

    def sent_to_reducers(ref, phase):
        if stride == 1:
            wait_bytes(ref.at[pl.ds(0, reducers - 1)], send_sem.at[phase])
        else:
            is_reducer = lax.rem(tm, stride) == 0
            pl.when(is_reducer)(
                lambda: wait_bytes(ref.at[pl.ds(0, reducers - 1)], send_sem.at[phase])
            )
            pl.when(jnp.logical_not(is_reducer))(
                lambda: wait_bytes(ref.at[pl.ds(0, reducers)], send_sem.at[phase])
            )

    sent_to_reducers(project_in, 10)
    sent_to_reducers(expand_in, 12)
    for part, phase in ((small_in, 11), (late_in, 13)):
        pl.when(tm == 0)(lambda: wait_bytes(part.at[0], send_sem.at[phase]))
        pl.when(tm != 0)(lambda: wait_bytes(part.at[pl.ds(0, 2)], send_sem.at[phase]))

    def group_bytes(ref, phase):
        def one(k, carry):
            wait_bytes(ref, send_sem.at[phase])
            return carry

        lax.fori_loop(1, tm_size, one, 0)

    def sent_sums():
        group_bytes(project_sum.at[pl.ds(0, 16), :], 14)
        rows, cols = sum_piece(place)
        group_bytes(expand_sum.at[rows, cols], 17)

        def one(k, carry):
            wait_bytes(square_part, send_sem.at[18])
            return carry

        lax.fori_loop(1, devices, one, 0)

    when_reducer(sent_sums)

    @pl.when(tm == 0)
    def _():
        group_bytes(small_sum, 15)
        group_bytes(late_sum, 16)

    for store in stores:
        store.wait()


def adam(weight, moment, square, gradient, scale, step_rate):
    clipped = gradient * scale
    moment_next = beta_first * moment + (1.0 - beta_first) * clipped
    square_next = beta_second * square + (1.0 - beta_second) * clipped * clipped
    update = (
        moment_next
        / (1.0 - beta_first**step_count)
        / (jnp.sqrt(square_next / (1.0 - beta_second**step_count)) + adam_eps)
    )
    return weight - step_rate * (update + decay * weight), moment_next, square_next


def adam_kernel(
    block_in,
    skip_in,
    input_in,
    expand_grad,
    project_grad,
    small_grad,
    *refs,
):
    state, outs = refs[:18], refs[18:40]
    sem = refs[40]
    copies = [
        pltpu.make_async_copy(src, dst, sem.at[k])
        for k, (src, dst) in enumerate(
            zip((block_in, skip_in, input_in), (outs[0], outs[1], outs[2]))
        )
    ]
    for copy in copies:
        copy.start()
    biases = small_grad[BIAS_ROW : BIAS_ROW + 1, :]
    slopes = [
        jnp.sum(small_grad[row : row + 1, :], axis=1, keepdims=True)
        for row in (SLOPE_ONE_ROW, SLOPE_TWO_ROW)
    ]
    total = jnp.sum(small_grad[SQUARES_ROW : SQUARES_ROW + 1, :] + biases * biases, axis=1, keepdims=True)
    total = total + slopes[0] * slopes[0] + slopes[1] * slopes[1]
    grad_norm = jnp.sqrt(total)
    scale = jnp.minimum(1.0, clip_level / grad_norm)
    outs[3][0, 0] = grad_norm[0, 0]

    def update(k, gradient, step_rate, at=...):
        results = adam(
            state[3 * k][at], state[3 * k + 1][at], state[3 * k + 2][at], gradient, scale, step_rate
        )
        for j in range(3):
            outs[4 + 3 * k + j][at] = results[j]

    update(0, expand_grad[...], rate)
    update(1, small_grad[TAP_ROW : TAP_ROW + 3, :], small_rate)
    for k in range(2):
        update(2, project_grad[k], rate, k)
    update(3, small_grad[0:6, :], small_rate)
    lanes = biases.shape[1] // 2
    for k in range(2):
        update(4, biases[:, k * lanes : (k + 1) * lanes], small_rate, slice(k, k + 1))
    for k in range(2):
        results = adam(
            state[15][k], state[16][k], state[17][k], slopes[k], scale, small_rate
        )
        for j in range(3):
            outs[19 + j][k] = results[j][0, 0]
    for copy in copies:
        copy.wait()


def per_device(
    tm_size,
    frames_in,
    item_lengths,
    out_cotangent,
    skip_cotangent,
    expand,
    expand_moment,
    expand_square,
    depthwise,
    depth_moment,
    depth_square,
    project,
    project_moment,
    project_square,
    channel_vectors,
    vector_moment,
    vector_square,
    output_biases,
    bias_moment,
    bias_square,
    prelu_slopes,
    slope_moment,
    slope_square,
):
    frames, inputs = frames_in.shape
    half = expand.shape[1]
    hidden = 2 * half
    items = item_lengths.shape[0]
    item_pad = -(-items // 16) * 16
    width = -(-3 * item_pad // LANES) * LANES
    wide = frames + 2 * HALO
    devices = 2 * tm_size
    reducers = 2 * PIECES
    peers = 2 * (-(-LONGEST_ITEM // frames))
    vmem, smem, anywhere = (
        pl.BlockSpec(memory_space=pltpu.VMEM),
        pl.BlockSpec(memory_space=pltpu.SMEM),
        pl.BlockSpec(memory_space=pl.ANY),
    )
    shape = jax.ShapeDtypeStruct
    scratch = [
        ((wide, inputs), BF16),
        ((wide, 2 * inputs), BF16),
        ((inputs, hidden), BF16),
        ((hidden, 2 * inputs), BF16),
        ((16, hidden), F32),
        ((wide, width), BF16),
        ((item_pad, frames), BF16),
        ((wide, LANES), F32),
        ((wide, LANES), F32),
        ((width, 4 * LANES), BF16),
        ((peers, item_pad, LANES), F32),
        ((wide, hidden), F32),
        ((wide, hidden), F32),
        ((wide, hidden), F32),
        ((wide, hidden), F32),
        ((wide, hidden), F32),
        ((frames, hidden), BF16),
        ((frames, hidden), BF16),
        ((frames, 8 * LANES), BF16),
        ((COLUMN_SUMS, 8, hidden), F32),
        ((frames, inputs), BF16),
        ((frames, inputs), BF16),
        ((frames, inputs), F32),
        ((item_pad, LANES), F32),
        ((item_pad, LANES), F32),
        ((item_pad, LANES), F32),
        ((peers, item_pad, LANES), F32),
        ((peers, item_pad, LANES), F32),
        ((peers, item_pad, LANES), F32),
        ((2 * inputs, hidden), F32),
        ((inputs, hidden), F32),
        ((devices, 16, half), F32),
        ((devices, 16, LANES), F32),
        ((2, 16, half), F32),
        ((devices, 16, half), F32),
        ((2, 8, half), F32),
        ((devices, 8, half), F32),
        ((2 * inputs, half), F32),
        ((inputs, half), F32),
        ((16, half), F32),
        ((8, half), F32),
        ((1, LANES), F32),
        ((reducers, 1, LANES), F32),
    ]
    block_raw, skip_raw, input_raw, expand_grad, project_grad, small_grad = pl.pallas_call(
        functools.partial(block_kernel, tm_size, items, item_pad),
        out_shape=[
            shape((frames, inputs), BF16),
            shape((frames, inputs), BF16),
            shape((frames, inputs), F32),
            shape((inputs, half), F32),
            shape((2, half, inputs), F32),
            shape((16, half), F32),
        ],
        in_specs=[smem, smem] + [anywhere] * 3 + [vmem] * 5,
        out_specs=[anywhere] * 3 + [vmem] * 3,
        scratch_shapes=[pltpu.VMEM(s, t) for s, t in scratch]
        + [
            pltpu.SemaphoreType.DMA((3,)),
            pltpu.SemaphoreType.DMA((3,)),
            pltpu.SemaphoreType.DMA((19,)),
            pltpu.SemaphoreType.DMA((19,)),
        ],
        compiler_params=pltpu.CompilerParams(
            collective_id=0, has_side_effects=True, vmem_limit_bytes=60 * 2**20
        ),
        name="temporal_block",
    )(
        item_lengths,
        prelu_slopes,
        frames_in,
        out_cotangent,
        skip_cotangent,
        expand,
        project,
        depthwise,
        channel_vectors,
        output_biases,
    )
    state = [
        expand,
        expand_moment,
        expand_square,
        depthwise,
        depth_moment,
        depth_square,
        project,
        project_moment,
        project_square,
        channel_vectors,
        vector_moment,
        vector_square,
        output_biases,
        bias_moment,
        bias_square,
        prelu_slopes,
        slope_moment,
        slope_square,
    ]
    results = pl.pallas_call(
        adam_kernel,
        out_shape=[
            shape((frames, inputs), BF16),
            shape((frames, inputs), BF16),
            shape((frames, inputs), F32),
            shape((1, 1), F32),
        ]
        + [shape(v.shape, F32) for v in state],
        in_specs=[anywhere] * 3 + [vmem] * 18 + [smem] * 3,
        out_specs=[anywhere] * 3 + [smem] + [vmem] * 15 + [smem] * 3,
        scratch_shapes=[pltpu.SemaphoreType.DMA((3,))],
        compiler_params=pltpu.CompilerParams(vmem_limit_bytes=32 * 2**20),
        name="adam_step",
    )(block_raw, skip_raw, input_raw, expand_grad, project_grad, small_grad, *state)
    results = list(results)
    results[3] = results[3].reshape(())
    return tuple(results)


def solution(mesh):
    frames = P(("tm", "chan"), None)
    columns = P(None, "chan")
    rows = P(None, "chan", None)
    in_specs = (
        (frames, P(), frames, frames)
        + (columns,) * 3
        + (columns,) * 3
        + (rows,) * 3
        + (columns,) * 3
        + (P(),) * 6
    )
    out_specs = (
        (frames, frames, frames, P())
        + (columns,) * 3
        + (columns,) * 3
        + (rows,) * 3
        + (columns,) * 3
        + (P(),) * 6
    )
    return jax.shard_map(
        functools.partial(per_device, mesh.shape["tm"]),
        mesh=mesh,
        in_specs=in_specs,
        out_specs=out_specs,
        check_vma=False,
    )
```

```python
import functools

import jax
import jax.numpy as jnp
from jax import lax
from jax.experimental import pallas as pl
from jax.experimental.pallas import tpu as pltpu
from jax.sharding import PartitionSpec as P

F32 = jnp.float32
BF16 = jnp.bfloat16
MESH = pl.DeviceIdType.MESH

DILATION = 16
HALO = 2 * DILATION
LONGEST_ITEM = 8192
LANES = 128
ROWS = 64
BLOCK = 512
PIECES = 16

norm_eps = 1e-06
clip_level = 5.0
rate = 0.05
small_rate = 0.5
beta_first = 0.9
beta_second = 0.999
adam_eps = 1e-08
decay = 0.01
step_count = 10.0

TAP_ROW = 6
BIAS_ROW = 9
SLOPE_TWO_ROW = 10
SLOPE_ONE_ROW = 11
SQUARES_ROW = 12

(GAIN_TWO, SHIFT_TWO, TAP_A, TAP_B, TAP_C, DEPTH_BIAS, GAIN_ONE, SHIFT_ONE, SLOPE_TWO, SLOPE_ONE, COLUMN_SUMS) = range(11)


def dot(a, b):
    return lax.dot_general(a, b, (((1,), (0,)), ((), ())), preferred_element_type=F32)


def dot_rows(a, b):
    return lax.dot_general(a, b, (((1,), (1,)), ((), ())), preferred_element_type=F32)


def dot_frames(a, b):
    return lax.dot_general(a, b, (((0,), (0,)), ((), ())), preferred_element_type=F32)


def rounded(v):
    return v.astype(BF16).astype(F32)


def spread_lanes(v):
    return jnp.broadcast_to(jnp.sum(v, axis=1, keepdims=True), (v.shape[0], LANES))


def spots_of(item_pad):
    names = ("sum", "spread", "mean", "crossed")
    if 4 * item_pad <= LANES:
        return 2, {**{n: (0, k * item_pad) for k, n in enumerate(names)}, "q": (1, 2 * item_pad)}
    return 5, {n: (k, 0) for k, n in enumerate(names + ("q",))}


def fold_rows(v):
    return jnp.sum(v.reshape(v.shape[0] // 8, 8, v.shape[1]), axis=0)


def block_kernel(
    tm_size,
    item_count,
    item_pad,
    len_hbm,
    slope_hbm,
    frames_hbm,
    out_cot_hbm,
    skip_cot_hbm,
    expand_hbm,
    project_hbm,
    taps_hbm,
    vectors_hbm,
    biases_hbm,
    block_out,
    skip_out,
    input_out,
    expand_grad_ref,
    project_grad_ref,
    small_grad_ref,
    len_ref,
    slope_ref,
    expand_ref,
    project_ref,
    taps_ref,
    vectors_ref,
    biases_ref,
    x,
    cots,
    w_expand,
    w_project,
    params,
    item_rows,
    item_cols,
    mask_low,
    mask_high,
    table,
    counts,
    act_one,
    xhat_one,
    normed,
    mixed_grad,
    act_two,
    mixed,
    hidden_grad,
    seg,
    column,
    tile_one,
    tile_two,
    tile_three,
    stats_one,
    stats_two,
    stats_three,
    project_part,
    expand_part,
    project_pair,
    expand_pair,
    project_in,
    expand_in,
    small_part,
    small_in,
    late_part,
    late_in,
    project_sum,
    small_sum,
    square_part,
    last_part,
    last_in,
    local_sem,
    send_sem,
    recv_sem,
    near_send,
    near_recv,
):
    frames = block_out.shape[0]
    wide = x.shape[0]
    half = expand_ref.shape[1]
    hidden = 2 * half
    blocks = hidden // LANES
    devices = 2 * tm_size
    stride = tm_size // PIECES
    spans = -(-LONGEST_ITEM // frames)
    chan = lax.axis_index("chan")
    tm = lax.axis_index("tm")
    me = tm * 2 + chan
    other = 1 - chan

    def device(index):
        return {"chan": lax.rem(index, 2), "tm": lax.div(index, 2)}

    def remote(src, dst, phase, target):
        return pltpu.make_async_remote_copy(
            src_ref=src,
            dst_ref=dst,
            send_sem=send_sem.at[phase],
            recv_sem=recv_sem.at[phase],
            device_id=target,
            device_id_type=MESH,
        )

    def wait_bytes(ref, sem):
        pltpu.make_async_copy(ref, ref, sem).wait()

    pending = {}

    def settle(*keys):
        for key in keys:
            pending.pop(key)()

    def started(copy, name, sends=None, receives=None):
        def maybe(condition, body):
            if condition is None:
                body()
            else:
                pl.when(condition)(body)

        maybe(sends, copy.start)
        pending[name, "sent"] = lambda: maybe(sends, copy.wait_send)
        pending[name, "here"] = lambda: maybe(receives, copy.wait_recv)

    own = pl.ds(HALO, frames)
    loads = {
        "expand": (expand_hbm, expand_ref),
        "frames": (frames_hbm, x.at[own, :]),
        "vectors": (vectors_hbm, vectors_ref),
        "taps": (taps_hbm, taps_ref),
        "lengths": (len_hbm, len_ref),
        "slopes": (slope_hbm, slope_ref),
        "project": (project_hbm, project_ref),
        "out": (out_cot_hbm, cots.at[own, pl.ds(0, LANES)]),
        "skip": (skip_cot_hbm, cots.at[own, pl.ds(LANES, LANES)]),
        "biases": (biases_hbm, biases_ref),
    }
    for k, (name, (src, dst)) in enumerate(loads.items()):
        load = pltpu.make_async_copy(src, dst, local_sem.at[k])
        load.start()
        pending["load", name] = load.wait

    def loaded(*names):
        settle(*[("load", name) for name in names])

    for r in (0, HALO + frames):
        x[r : r + HALO, :] = jnp.zeros((HALO, x.shape[1]), BF16)
    for r in (HALO - DILATION, HALO + frames):
        cots[r : r + DILATION, :] = jnp.zeros((DILATION, cots.shape[1]), BF16)
    for stats in (stats_one, stats_two, stats_three):
        stats[...] = jnp.zeros_like(stats)

    barrier = pltpu.get_barrier_semaphore()

    def greet(k, carry):
        pl.semaphore_signal(
            barrier, inc=1, device_id=device(lax.rem(me + k, devices)), device_id_type=MESH
        )
        return carry

    lax.fori_loop(1, devices, greet, 0)

    my_half = pl.ds(pl.multiple_of(chan * half, half), half)
    loaded("expand", "vectors", "taps")
    w_expand[:, my_half] = expand_ref[...].astype(BF16)
    params[0:6, my_half] = vectors_ref[...]
    params[6:9, my_half] = taps_ref[...]
    params[9:16, my_half] = jnp.zeros((7, half), F32)
    loaded("frames")
    pl.semaphore_wait(barrier, devices - 1)

    partner = device(tm * 2 + other)
    left, right = device(me - 1), device(me + 1)
    has_left, has_right = me > 0, me < devices - 1

    def to_left(ref, count, name):
        copy = remote(
            ref.at[pl.ds(HALO, count), :], ref.at[pl.ds(HALO + frames, count), :], name, left
        )
        started(copy, name, has_left, has_right)

    def to_right(ref, count, name):
        copy = remote(
            ref.at[pl.ds(HALO + frames - count, count), :],
            ref.at[pl.ds(HALO - count, count), :],
            name,
            right,
        )
        started(copy, name, has_right, has_left)

    started(remote(w_expand.at[:, my_half], w_expand.at[:, my_half], 0, partner), 0)
    started(remote(params.at[:, my_half], params.at[:, my_half], 1, partner), 1)
    to_left(x, HALO, 2)
    to_right(x, HALO, 3)
    loaded("project", "out", "skip")
    w_project[my_half, 0:LANES] = project_ref[0].astype(BF16)
    w_project[my_half, LANES : 2 * LANES] = project_ref[1].astype(BF16)
    started(remote(w_project.at[my_half, :], w_project.at[my_half, :], 4, partner), 4)
    to_left(cots, DILATION, 5)
    to_right(cots, DILATION, 6)
    loaded("lengths", "slopes", "biases")

    width = table.shape[0]
    lane = lax.broadcasted_iota(jnp.int32, (8, width), 1)
    lane_item = lax.rem(lane, item_pad)
    row_item = lax.broadcasted_iota(jnp.int32, (item_pad, LANES), 0)

    def bounds(j, carry):
        lane_start, lane_end, row_start, row_end = carry
        length = len_ref[j]
        return (
            lane_start + jnp.where(lane_item > j, length, 0),
            lane_end + jnp.where(lane_item >= j, length, 0),
            row_start + jnp.where(row_item > j, length, 0),
            row_end + jnp.where(row_item >= j, length, 0),
        )

    lane_zero, row_zero = jnp.zeros_like(lane), jnp.zeros_like(row_item)
    lane_start, lane_end, row_start, row_end = lax.fori_loop(
        0, item_count, bounds, (lane_zero, lane_zero, row_zero, row_zero)
    )
    lane_end = jnp.where(lane < 3 * item_pad, lane_end, lane_start)
    first = me * frames
    lane_start_row, lane_end_row = lane_start[0:1], lane_end[0:1]
    elements = jnp.maximum((row_end - row_start).astype(F32) * hidden, 1.0)

    def count_of(index):
        low = jnp.maximum(row_start, index * frames)
        high = jnp.minimum(row_end, (index + 1) * frames)
        return jnp.maximum(high - low, 0).astype(F32) * hidden

    my_count = count_of(me)
    my_safe = jnp.maximum(my_count, 1.0)
    offsets = [sign * o for o in range(spans, 0, -1) for sign in (1, -1)]
    spots = spots_of(item_pad)[1]
    tile_lane = lax.broadcasted_iota(jnp.int32, (item_pad, LANES), 1)

    def packed(v, name):
        chosen = tile_lane == spots[name][1] + row_item
        return jnp.sum(jnp.where(chosen, v, 0.0), axis=0, keepdims=True)

    def unpacked(row, name):
        chosen = tile_lane == spots[name][1] + row_item
        return spread_lanes(jnp.where(chosen, jnp.broadcast_to(row, chosen.shape), 0.0))

    counts[len(offsets)] = packed(my_count, "mean")
    for slot, offset in enumerate(offsets):
        counts[slot] = packed(count_of(me - offset), "mean")
    column[...] = jnp.zeros_like(column)

    def put_table(place, v):
        high = v.astype(BF16)
        rest = v - high.astype(F32)
        middle = rest.astype(BF16)
        low = (rest - middle.astype(F32)).astype(BF16)
        where = slice(place * LANES, (place + 1) * LANES)
        table[0:item_pad, where] = high
        table[item_pad : 2 * item_pad, where] = middle
        table[2 * item_pad : 3 * item_pad, where] = low

    def rows_of(r, n, count):
        return dot(item_rows[pl.ds(r, n), :], table[:, 0 : count * LANES])

    def part(values, k, n, b):
        return values[k : k + n, b * LANES : (b + 1) * LANES]

    def put_seg(r, n, place, v, exact=True):
        high = v.astype(BF16)
        seg[pl.ds(r, n), pl.ds(place * LANES, LANES)] = high
        if exact:
            low = (v - high.astype(F32)).astype(BF16)
            seg[pl.ds(r, n), pl.ds((place + 1) * LANES, LANES)] = low

    def item_sums(first, widths):
        sums = dot(item_cols[...], seg[:, first * LANES : (first + sum(widths)) * LANES])
        results, k = [], 0
        for n in widths:
            v = sums[:, k * LANES : (k + 1) * LANES]
            if n == 2:
                v = v + sums[:, (k + 1) * LANES : (k + 2) * LANES]
            results.append(spread_lanes(v))
            k += n
        return results

    def loop(start, size, count, body, rep=1):
        def step(i, carry):
            i = i if rep == 1 else lax.rem(i, count)
            body(pl.multiple_of(start + i * size, 16))
            return carry

        lax.fori_loop(0, count * rep, step, 0)

    def at(r, k, shift=0):
        return pl.multiple_of(r + (k - shift), 16)

    table[...] = jnp.zeros_like(table)
    put_table(0, row_start.astype(F32))
    put_table(1, row_end.astype(F32))

    wide_block = wide // 4
    wide_rows = wide_block // 11

    @functools.partial(loop, 0, wide_block, 4)
    def _(r):
        for k in range(0, wide_block, wide_rows):
            position = first - HALO + r + k + lax.broadcasted_iota(jnp.int32, (wide_rows, width), 0)
            inside = (position >= lane_start_row) & (position < lane_end_row)
            item_rows[pl.ds(at(r, k), wide_rows), :] = inside.astype(F32).astype(BF16)
        ends = rows_of(r, wide_block, 2)
        for k in range(0, wide_block, wide_rows):
            here = first - HALO + r + k + lax.broadcasted_iota(jnp.int32, (wide_rows, LANES), 0)
            here = here.astype(F32)
            after = here - part(ends, k, wide_rows, 0)
            before = part(ends, k, wide_rows, 1) - here
            mask_low[pl.ds(at(r, k), wide_rows), :] = (after >= DILATION).astype(F32)
            mask_high[pl.ds(at(r, k), wide_rows), :] = (before > DILATION).astype(F32)

    for i in range(frames // LANES):
        position = first + i * LANES + lax.broadcasted_iota(jnp.int32, (item_pad, LANES), 1)
        inside = (position >= row_start) & (position < row_end)
        item_cols[:, i * LANES : (i + 1) * LANES] = inside.astype(F32).astype(BF16)

    slope_one, slope_two = slope_ref[0], slope_ref[1]

    def lanes_of(which, b):
        return pl.ds(pl.multiple_of(which * half + b * LANES, LANES), LANES)

    def half_of(which):
        return pl.ds(pl.multiple_of(which * half, half), half)

    def activate(product, k, n, which, b):
        v = part(product, k, n, b) + params[0:1, lanes_of(which, b)]
        return jnp.maximum(v, slope_one * v)

    own_loop = functools.partial(functools.partial, loop, HALO, BLOCK, frames // BLOCK)

    @own_loop()
    def _(r):
        product = dot(x[pl.ds(r, BLOCK), :], w_expand[:, half_of(chan)])
        for k in range(0, BLOCK, ROWS):
            total = jnp.zeros((ROWS, LANES), F32)
            for b in range(blocks // 2):
                a = activate(product, k, ROWS, chan, b)
                act_one[pl.ds(at(r, k), ROWS), lanes_of(chan, b)] = a
                total = total + a
            put_seg(at(r, k, HALO), ROWS, 0, total)

    (total,) = item_sums(0, (2,))
    shift = total / jnp.maximum(my_count * 0.5, 1.0)
    put_table(0, shift)
    settle(*[(k, "here") for k in range(4)])

    @own_loop()
    def _(r):
        centres = rows_of(r, BLOCK, 1)
        product = dot(x[pl.ds(r, BLOCK), :], w_expand[:, half_of(other)])
        for k in range(0, BLOCK, ROWS):
            rows = pl.ds(at(r, k), ROWS)
            centre = part(centres, k, ROWS, 0)
            total = jnp.zeros((ROWS, LANES), F32)
            squares = jnp.zeros((ROWS, LANES), F32)
            for b in range(blocks // 2):
                d = act_one[rows, lanes_of(chan, b)] - centre
                total = total + d
                squares = squares + d * d
                a = activate(product, k, ROWS, other, b)
                act_one[rows, lanes_of(other, b)] = a
                d = a - centre
                total = total + d
                squares = squares + d * d
            put_seg(at(r, k, HALO), ROWS, 0, total)
            put_seg(at(r, k, HALO), ROWS, 2, squares)

    def pack_tile(tile, values):
        for r in range(tile.shape[0]):
            row = jnp.zeros((1, LANES), F32)
            for name, v in values.items():
                if spots[name][0] == r:
                    row = row + packed(v, name)
            tile[r : r + 1, :] = row

    def local_moments(shift, total, squares):
        mean = shift + total / my_safe
        spread = jnp.maximum(squares - total * total / my_safe, 0.0)
        return mean, spread

    def exchange(tile, stats, phase):
        def near(slot, offset):
            return pltpu.make_async_remote_copy(
                src_ref=tile,
                dst_ref=stats.at[slot],
                send_sem=near_send.at[phase, slot],
                recv_sem=near_recv.at[phase, slot],
                device_id=device(me + offset),
                device_id_type=MESH,
            )

        def all_near(source, act):
            for slot, offset in enumerate(offsets):
                index = me - offset if source else me + offset
                pl.when((index >= 0) & (index < devices))(lambda: act(near(slot, offset)))

        all_near(False, lambda copy: copy.start())
        pending["near", phase, "sent"] = lambda: all_near(False, lambda copy: copy.wait_send())
        pending["near", phase, "here"] = lambda: all_near(True, lambda copy: copy.wait_recv())

    def rows_with(name, tile, stats):
        r = spots[name][0]
        return [stats[slot, r : r + 1, :] for slot in range(len(offsets))] + [tile[r : r + 1, :]]

    def sum_of(name, tile, stats):
        total = None
        for row in rows_with(name, tile, stats):
            total = row if total is None else total + row
        return unpacked(total, name)

    def combined(tile, stats):
        mean = sum_of("sum", tile, stats) / elements
        centre = packed(mean, "mean")
        between = jnp.zeros((1, LANES), F32)
        for k, row in enumerate(rows_with("mean", tile, stats)):
            between = between + counts[k] * (row - centre) * (row - centre)
        spread = (sum_of("spread", tile, stats) + unpacked(between, "mean")) / elements
        return mean, centre, lax.rsqrt(spread + norm_eps)

    total, squares = item_sums(0, (2, 2))
    mean, spread = local_moments(shift, total, squares)
    pack_tile(tile_one, {"sum": mean * my_count, "spread": spread, "mean": mean})
    exchange(tile_one, stats_one, 0)

    for r in (0, HALO + frames):
        for which in (chan, other):
            product = dot(x[pl.ds(r, HALO), :], w_expand[:, half_of(which)])
            for b in range(blocks // 2):
                act_one[pl.ds(r, HALO), lanes_of(which, b)] = activate(product, 0, HALO, which, b)

    settle(*[(k, "here") for k in (4, 5, 6)])

    def lanes(b):
        return pl.ds(b * LANES, LANES)

    def mixed_rows(r, n, size, add):
        product = dot_rows(cots[pl.ds(r, n), :], w_project[...])
        for k in range(0, n, size):
            total = jnp.zeros((size, LANES), F32)
            for b in range(blocks):
                y = part(product, k, size, b)
                mixed_grad[pl.ds(at(r, k), size), lanes(b)] = y
                if add:
                    total = total + params[4:5, lanes(b)] * y
                    column[SHIFT_TWO, :, lanes(b)] += fold_rows(y)
            if add:
                put_seg(at(r, k, HALO), size, 4, total)

    @own_loop()
    def _(r):
        mixed_rows(r, BLOCK, ROWS, True)

    for r in (HALO - DILATION, HALO + frames):
        mixed_rows(r, DILATION, DILATION, False)
    bias_sum = dot(jnp.ones((16, frames), BF16), cots[own, :])[0:1]
    (q_sum,) = item_sums(4, (2,))

    settle(("near", 0, "here"))
    mean_one, _, scale_one = combined(tile_one, stats_one)
    put_table(0, mean_one)
    put_table(1, scale_one)

    @functools.partial(loop, 0, wide_block, 4)
    def _(r):
        values = rows_of(r, wide_block, 2)
        for k in range(0, wide_block, wide_rows):
            rows = pl.ds(at(r, k), wide_rows)
            mean, scale = part(values, k, wide_rows, 0), part(values, k, wide_rows, 1)
            for b in range(blocks):
                xhat = (act_one[rows, lanes(b)] - mean) * scale
                xhat_one[rows, lanes(b)] = xhat
                normed[rows, lanes(b)] = rounded(
                    params[1:2, lanes(b)] * xhat + params[2:3, lanes(b)]
                )

    def depth_rows(r, n, b):
        low, high = mask_low[pl.ds(r, n), :], mask_high[pl.ds(r, n), :]
        v = (
            params[3:4, lanes(b)]
            + params[6:7, lanes(b)] * (low * normed[pl.ds(r - DILATION, n), lanes(b)])
            + params[7:8, lanes(b)] * normed[pl.ds(r, n), lanes(b)]
            + params[8:9, lanes(b)] * (high * normed[pl.ds(r + DILATION, n), lanes(b)])
        )
        return jnp.maximum(v, slope_two * v)

    @own_loop()
    def _(r):
        for k in range(0, BLOCK, ROWS):
            a = depth_rows(at(r, k), ROWS, 0)
            act_two[pl.ds(at(r, k), ROWS), lanes(0)] = a
            put_seg(at(r, k, HALO), ROWS, 0, a)

    (total,) = item_sums(0, (2,))
    shift = total / jnp.maximum(my_count * (1.0 / blocks), 1.0)
    put_table(0, shift)

    @own_loop()
    def _(r):
        centres = rows_of(r, BLOCK, 1)
        for k in range(0, BLOCK, ROWS):
            rows = pl.ds(at(r, k), ROWS)
            centre = part(centres, k, ROWS, 0)
            total = jnp.zeros((ROWS, LANES), F32)
            squares = jnp.zeros((ROWS, LANES), F32)
            crossed = jnp.zeros((ROWS, LANES), F32)
            for b in range(blocks):
                if b == 0:
                    a = act_two[rows, lanes(b)]
                else:
                    a = depth_rows(at(r, k), ROWS, b)
                    act_two[rows, lanes(b)] = a
                d = a - centre
                total = total + d
                squares = squares + d * d
                crossed = crossed + params[4:5, lanes(b)] * mixed_grad[rows, lanes(b)] * d
            put_seg(at(r, k, HALO), ROWS, 0, total)
            put_seg(at(r, k, HALO), ROWS, 2, squares, exact=False)
            put_seg(at(r, k, HALO), ROWS, 3, crossed, exact=False)

    total, squares, crossed = item_sums(0, (2, 1, 1))
    mean, spread = local_moments(shift, total, squares)
    crossed = crossed - (mean - shift) * q_sum
    values = {"sum": mean * my_count, "spread": spread, "mean": mean, "crossed": crossed, "q": q_sum}
    pack_tile(tile_two, values)
    exchange(tile_two, stats_two, 1)

    for r in (HALO - DILATION, HALO + frames):
        for b in range(blocks):
            act_two[pl.ds(r, DILATION), lanes(b)] = depth_rows(r, DILATION, b)

    settle(("near", 1, "here"))
    mean_two, centre, scale_two = combined(tile_two, stats_two)
    between = jnp.zeros((1, LANES), F32)
    for row, q_row in zip(rows_with("mean", tile_two, stats_two), rows_with("q", tile_two, stats_two)):
        between = between + (row - centre) * q_row
    cross_sum = sum_of("crossed", tile_two, stats_two) + unpacked(between, "mean")
    put_table(0, mean_two)
    put_table(1, scale_two)
    put_table(2, scale_two * sum_of("q", tile_two, stats_two) / elements)
    put_table(3, scale_two * scale_two * cross_sum / elements)

    def second_back(r, n, size, add):
        values = rows_of(r, n, 4)
        for k in range(0, n, size):
            rows = pl.ds(at(r, k), size)
            mean, scale, q_mean, cross_mean = [part(values, k, size, j) for j in range(4)]
            for b in range(blocks):
                a = act_two[rows, lanes(b)]
                y = mixed_grad[rows, lanes(b)]
                xhat = (a - mean) * scale
                g = (params[4:5, lanes(b)] * y) * scale - q_mean - xhat * cross_mean
                act_two[rows, lanes(b)] = rounded(g * jnp.where(a > 0, 1.0, slope_two))
                if add:
                    mixed[pl.ds(at(r, k, HALO), size), lanes(b)] = (
                        params[4:5, lanes(b)] * xhat + params[5:6, lanes(b)]
                    ).astype(BF16)
                    column[GAIN_TWO, :, lanes(b)] += fold_rows(y * xhat)
                    column[SLOPE_TWO, :, lanes(b)] += fold_rows(g * jnp.minimum(a, 0.0))

    @own_loop()
    def _(r):
        second_back(r, BLOCK, ROWS, True)

    for r in (HALO - DILATION, HALO + frames):
        second_back(r, DILATION, DILATION, False)

    @functools.partial(loop, HALO, 2 * ROWS, frames // (2 * ROWS))
    def _(r):
        for k in range(0, 2 * ROWS, ROWS):
            rows = pl.ds(at(r, k), ROWS)
            low, high = mask_low[rows, :], mask_high[rows, :]
            total = jnp.zeros((ROWS, LANES), F32)
            crossed = jnp.zeros((ROWS, LANES), F32)
            for b in range(blocks):
                later = high * act_two[pl.ds(at(r, k + DILATION), ROWS), lanes(b)]
                here = act_two[rows, lanes(b)]
                earlier = low * act_two[pl.ds(at(r, k - DILATION), ROWS), lanes(b)]
                n = normed[rows, lanes(b)]
                column[TAP_A, :, lanes(b)] += fold_rows(later * n)
                column[TAP_B, :, lanes(b)] += fold_rows(here * n)
                column[TAP_C, :, lanes(b)] += fold_rows(earlier * n)
                column[DEPTH_BIAS, :, lanes(b)] += fold_rows(here)
                y = (
                    params[6:7, lanes(b)] * later
                    + params[7:8, lanes(b)] * here
                    + params[8:9, lanes(b)] * earlier
                )
                column[SHIFT_ONE, :, lanes(b)] += fold_rows(y)
                xhat = xhat_one[rows, lanes(b)]
                column[GAIN_ONE, :, lanes(b)] += fold_rows(y * xhat)
                q = params[1:2, lanes(b)] * y
                mixed_grad[rows, lanes(b)] = q
                total = total + q
                crossed = crossed + q * xhat
            put_seg(at(r, k, HALO), ROWS, 0, total)
            put_seg(at(r, k, HALO), ROWS, 2, crossed)

    total, crossed = item_sums(0, (2, 2))
    pack_tile(tile_three, {"sum": total, "crossed": crossed})
    exchange(tile_three, stats_three, 2)

    step = 512
    total = jnp.zeros((2 * LANES, hidden), F32)
    for k in range(frames // step):
        total = total + dot_frames(
            cots[pl.ds(HALO + k * step, step), :], mixed[pl.ds(k * step, step), :]
        )
    project_part[...] = total

    core = lax.rem(tm, 2)
    sibling = {"chan": chan, "tm": tm + 1 - 2 * core}
    mine = pl.ds(pl.multiple_of(core * LANES, LANES), LANES)
    yours = pl.ds(pl.multiple_of((1 - core) * LANES, LANES), LANES)
    started(remote(project_part.at[yours, :], project_pair, 7, sibling), 7)

    def column_sum(which):
        return jnp.sum(column[which], axis=0, keepdims=True)

    early_rows = {
        1: column_sum(GAIN_ONE),
        2: column_sum(SHIFT_ONE),
        3: column_sum(DEPTH_BIAS),
        4: column_sum(GAIN_TWO),
        5: column_sum(SHIFT_TWO),
        TAP_ROW: column_sum(TAP_A),
        TAP_ROW + 1: column_sum(TAP_B),
        TAP_ROW + 2: column_sum(TAP_C),
    }
    slope_two_row = column_sum(SLOPE_TWO)
    slope_two_row = (slope_two_row[:, 0:half] + slope_two_row[:, half:hidden]) / slope_two
    for c in range(2):
        small_part[c] = jnp.zeros((16, half), F32)
        for row, v in early_rows.items():
            small_part[c, row : row + 1, :] = v[:, c * half : (c + 1) * half]
        small_part[c, BIAS_ROW : BIAS_ROW + 1, :] = bias_sum
        small_part[c, SLOPE_TWO_ROW : SLOPE_TWO_ROW + 1, :] = slope_two_row

    chips = tm_size // 2
    chip = lax.div(tm, 2)
    mates = 2 * chips
    mate = chip * 2 + chan
    spot = lax.div(chip, stride)
    reducers = 2 * PIECES
    place = (spot * 2 + core) * 2 + chan
    is_reducer = lax.rem(chip, stride) == 0

    def when_reducer(body):
        if stride == 1:
            body()
        else:
            pl.when(is_reducer)(body)

    def by_role(body, count):
        if stride == 1:
            body(count - 1)
        else:
            pl.when(is_reducer)(lambda: body(count - 1))
            pl.when(jnp.logical_not(is_reducer))(lambda: body(count))

    def to_reducers(source, ref, phase):
        def one(k, carry):
            q = lax.rem(spot * 2 + chan + k, PIECES)
            c, at_spot = lax.rem(q, 2), lax.div(q, 2)
            target = {"chan": c, "tm": at_spot * stride * 2 + core}

            def send():
                remote(source(c, at_spot), ref.at[mate], phase, target).start()

            if stride == 1:
                send()
            else:
                pl.when(at_spot * stride * 2 + c != mate)(send)
            return carry

        lax.fori_loop(1 if stride == 1 else 0, PIECES, one, 0)
        pending[phase, "sent"] = lambda: by_role(
            lambda n: wait_bytes(ref.at[pl.ds(0, n)], send_sem.at[phase]), PIECES
        )
        pending[phase, "here"] = lambda: when_reducer(
            lambda: wait_bytes(ref.at[pl.ds(0, mates - 1)], recv_sem.at[phase])
        )

    def piece_rows(at_spot):
        return pl.ds(pl.multiple_of(at_spot * 16, 16), 16)

    def project_piece(c, at_spot):
        return project_pair.at[piece_rows(at_spot), pl.ds(pl.multiple_of(c * half, half), half)]

    def expand_piece(c, at_spot):
        return expand_pair.at[c, piece_rows(at_spot), :]

    first_of_group = tm == 0

    def to_first(parts, ref, phase):
        for c in range(2):

            @pl.when((tm != 0) | (chan != c))
            def _(c=c):
                remote(parts.at[c], ref.at[me], phase, {"chan": c, "tm": 0}).start()

        def sent():
            pl.when(first_of_group)(lambda: wait_bytes(ref.at[0], send_sem.at[phase]))
            pl.when(jnp.logical_not(first_of_group))(
                lambda: wait_bytes(ref.at[pl.ds(0, 2)], send_sem.at[phase])
            )

        pending[phase, "sent"] = sent
        pending[phase, "here"] = lambda: pl.when(first_of_group)(
            lambda: wait_bytes(ref.at[pl.ds(0, devices - 1)], recv_sem.at[phase])
        )

    to_first(small_part, small_in, 11)
    settle((7, "here"))
    project_pair[...] += project_part[mine, :]
    to_reducers(project_piece, project_in, 10)

    @own_loop()
    def _(r):
        product = dot(mixed[pl.ds(at(r, 0, HALO), BLOCK), :], w_project[...])
        for k in range(0, BLOCK, ROWS):
            rows = pl.ds(at(r, k, HALO), ROWS)
            inputs = x[pl.ds(at(r, k), ROWS), :].astype(F32)
            block_out[rows, :] = (
                inputs + part(product, k, ROWS, 0) + biases_ref[0:1, :]
            ).astype(BF16)
            skip_out[rows, :] = (part(product, k, ROWS, 1) + biases_ref[1:2, :]).astype(BF16)

    settle(("near", 2, "here"))
    put_table(0, sum_of("sum", tile_three, stats_three) / elements)
    put_table(1, sum_of("crossed", tile_three, stats_three) / elements)
    put_table(2, scale_one)

    @own_loop()
    def _(r):
        values = rows_of(r, BLOCK, 3)
        for k in range(0, BLOCK, ROWS):
            rows, local = pl.ds(at(r, k), ROWS), pl.ds(at(r, k, HALO), ROWS)
            q_mean, cross_mean, scale = [part(values, k, ROWS, j) for j in range(3)]
            for b in range(blocks):
                a = act_one[rows, lanes(b)]
                g = (mixed_grad[rows, lanes(b)] - q_mean - xhat_one[rows, lanes(b)] * cross_mean) * scale
                column[SLOPE_ONE, :, lanes(b)] += fold_rows(g * jnp.minimum(a, 0.0))
                hidden_grad[local, lanes(b)] = (g * jnp.where(a > 0, 1.0, slope_one)).astype(BF16)

    total = jnp.zeros((LANES, hidden), F32)
    for k in range(frames // step):
        total = total + dot_frames(
            x[pl.ds(HALO + k * step, step), :], hidden_grad[pl.ds(k * step, step), :]
        )
    expand_part[...] = total
    for c in range(2):
        source = pl.ds(pl.multiple_of(c * half + (1 - core) * LANES, LANES), LANES)
        started(remote(expand_part.at[:, source], expand_pair.at[c], 8 + c, sibling), 8 + c)
    bias_one = dot(jnp.ones((16, frames), BF16), hidden_grad[...])[0:1]
    slope_row = column_sum(SLOPE_ONE)
    slope_row = (slope_row[:, 0:half] + slope_row[:, half:hidden]) / slope_one
    for c in range(2):
        late_part[c, 0:1, :] = bias_one[:, c * half : (c + 1) * half]
        late_part[c, 1:2, :] = slope_row
    to_first(late_part, late_in, 13)
    settle((8, "here"), (9, "here"))
    for c in range(2):
        expand_pair[c] += expand_part[
            :, pl.ds(pl.multiple_of(c * half + core * LANES, LANES), LANES)
        ]
    to_reducers(expand_piece, expand_in, 12)

    def total_of(ref, count, rows, cols):
        return lax.fori_loop(
            0, count, lambda k, total: total + ref[k], jnp.zeros((rows, cols), F32)
        )

    def fold_lanes(v):
        return v[:, 0:LANES] + v[:, LANES:half]

    def to_group(src, dst, phase, targets):
        def one(k, carry):
            target = (
                lax.rem(chip + k, chips) * 2 + core if targets == chips else lax.rem(tm + k, tm_size)
            )
            remote(src, dst, phase, {"chan": chan, "tm": target}).start()
            return carry

        lax.fori_loop(1, targets, one, 0)

    def group_sent(ref, phase, targets):
        def one(k, carry):
            wait_bytes(ref, send_sem.at[phase])
            return carry

        lax.fori_loop(1, targets, one, 0)

    settle((10, "here"))
    sum_rows = pl.ds(pl.multiple_of(core * LANES + spot * 16, 16), 16)

    @when_reducer
    def _():
        project_in[mate] = project_piece(chan, spot)[...]
        total = total_of(project_in, mates, 16, half)
        project_sum[sum_rows, :] = total
        square_part[...] = fold_lanes(jnp.sum(total * total, axis=0, keepdims=True))
        to_group(project_sum.at[sum_rows, :], project_sum.at[sum_rows, :], 14, chips)

    pending[14, "sent"] = lambda: when_reducer(
        lambda: group_sent(project_sum.at[pl.ds(0, 16), :], 14, chips)
    )
    pending[14, "here"] = lambda: by_role(
        lambda n: wait_bytes(project_sum.at[pl.ds(0, 16 * n), :], recv_sem.at[14]), PIECES // 2
    )
    settle((11, "here"))

    @pl.when(first_of_group)
    def _():
        small_in[me] = small_part[chan]
        total = total_of(small_in, devices, 16, half)
        small_sum[...] = total
        square_part[...] += fold_lanes(
            jnp.sum((total * total)[0:BIAS_ROW], axis=0, keepdims=True)
        )
        to_group(small_sum, small_sum, 15, tm_size)

    pending[15, "sent"] = lambda: pl.when(first_of_group)(
        lambda: group_sent(small_sum, 15, tm_size)
    )
    pending[15, "here"] = lambda: pl.when(jnp.logical_not(first_of_group))(
        lambda: wait_bytes(small_sum, recv_sem.at[15])
    )

    @own_loop()
    def _(r):
        product = dot_rows(hidden_grad[pl.ds(at(r, 0, HALO), BLOCK), :], w_expand[...])
        for k in range(0, BLOCK, ROWS):
            above = cots[pl.ds(at(r, k), ROWS), 0:LANES].astype(F32)
            input_out[pl.ds(at(r, k, HALO), ROWS), :] = above + part(product, k, ROWS, 0)

    settle((13, "here"))
    last_part[...] = jnp.zeros_like(last_part)

    @pl.when(first_of_group)
    def _():
        late_in[me] = late_part[chan]
        total = total_of(late_in, devices, 2, half)
        last_part[17:19, :] = total[:, 0:LANES]
        last_part[19:21, :] = total[:, LANES:half]
        squares = (total * total)[0:1]
        square_part[...] += fold_lanes(squares)

    settle((12, "here"))

    @when_reducer
    def _():
        expand_in[mate] = expand_piece(chan, spot)[...]
        total = total_of(expand_in, mates, 16, LANES)
        last_part[0:16, :] = total
        last_part[16:17, :] = square_part[...] + jnp.sum(total * total, axis=0, keepdims=True)
        last_in[place] = last_part[...]
        to_group(last_part, last_in.at[place], 17, tm_size)
        tail = pl.ds(16, 8)

        def send_tail(k, carry):
            target = {"chan": other, "tm": lax.rem(tm + k, tm_size)}
            remote(last_part.at[tail, :], last_in.at[place, tail, :], 18, target).start()
            return carry

        lax.fori_loop(0, tm_size, send_tail, 0)

    def tails(count, sem):
        wait_bytes(last_in.at[pl.ds(0, count), pl.ds(16, 8), :], sem)

    def tails_sent():
        for _ in range(tm_size // PIECES):
            tails(PIECES, send_sem.at[18])

    pending[17, "sent"] = lambda: when_reducer(lambda: group_sent(last_part, 17, tm_size))
    pending[17, "here"] = lambda: by_role(
        lambda n: wait_bytes(last_in.at[pl.ds(0, n)], recv_sem.at[17]), PIECES
    )
    pending[18, "sent"] = lambda: when_reducer(tails_sent)
    pending[18, "here"] = lambda: tails(PIECES, recv_sem.at[18])

    settle((14, "here"))
    started(remote(project_sum.at[mine, :], project_sum.at[mine, :], 16, sibling), 16)
    settle((15, "here"), (16, "here"))
    for k in range(2):
        project_grad_ref[k] = project_sum[k * LANES : (k + 1) * LANES, :].T
    small_grad_ref[...] = small_sum[...]
    settle((17, "here"), (18, "here"))
    for j in range(PIECES):
        rows, lanes_here = slice(j // 2 * 16, j // 2 * 16 + 16), slice(j % 2 * LANES, (j % 2 + 1) * LANES)
        expand_grad_ref[rows, lanes_here] = last_in[j * 2 + chan, 0:16, :]
    for k in range(2):
        where = slice(k * LANES, (k + 1) * LANES)
        late = last_in[chan, 17 + 2 * k : 19 + 2 * k, :]
        small_grad_ref[0:1, where] = late[0:1]
        small_grad_ref[SLOPE_ONE_ROW : SLOPE_ONE_ROW + 1, where] = late[1:2]
    total = last_in[0, 16:17, :]
    for q in range(1, reducers):
        total = total + last_in[q, 16:17, :]
    small_grad_ref[SQUARES_ROW : SQUARES_ROW + 1, 0:LANES] = total
    small_grad_ref[SQUARES_ROW : SQUARES_ROW + 1, LANES:half] = jnp.zeros((1, half - LANES), F32)

    settle(*list(pending))


def adam(weight, moment, square, gradient, scale, step_rate):
    clipped = gradient * scale
    moment_next = beta_first * moment + (1.0 - beta_first) * clipped
    square_next = beta_second * square + (1.0 - beta_second) * clipped * clipped
    update = (
        moment_next
        / (1.0 - beta_first**step_count)
        / (jnp.sqrt(square_next / (1.0 - beta_second**step_count)) + adam_eps)
    )
    return weight - step_rate * (update + decay * weight), moment_next, square_next


def adam_kernel(
    block_in,
    skip_in,
    input_in,
    expand_grad,
    project_grad,
    small_grad,
    *refs,
):
    state, outs = refs[:18], refs[18:40]
    sem = refs[40]
    copies = [
        pltpu.make_async_copy(src, dst, sem.at[k])
        for k, (src, dst) in enumerate(
            zip((block_in, skip_in, input_in), (outs[0], outs[1], outs[2]))
        )
    ]
    for copy in copies:
        copy.start()
    biases = small_grad[BIAS_ROW : BIAS_ROW + 1, :]
    slopes = [
        jnp.sum(small_grad[row : row + 1, :], axis=1, keepdims=True)
        for row in (SLOPE_ONE_ROW, SLOPE_TWO_ROW)
    ]
    total = jnp.sum(small_grad[SQUARES_ROW : SQUARES_ROW + 1, :] + biases * biases, axis=1, keepdims=True)
    total = total + slopes[0] * slopes[0] + slopes[1] * slopes[1]
    grad_norm = jnp.sqrt(total)
    scale = jnp.minimum(1.0, clip_level / grad_norm)
    outs[3][0, 0] = grad_norm[0, 0]

    def update(k, gradient, step_rate, at=...):
        results = adam(
            state[3 * k][at], state[3 * k + 1][at], state[3 * k + 2][at], gradient, scale, step_rate
        )
        for j in range(3):
            outs[4 + 3 * k + j][at] = results[j]

    update(0, expand_grad[...], rate)
    update(1, small_grad[TAP_ROW : TAP_ROW + 3, :], small_rate)
    for k in range(2):
        update(2, project_grad[k], rate, k)
    update(3, small_grad[0:6, :], small_rate)
    lanes = biases.shape[1] // 2
    for k in range(2):
        update(4, biases[:, k * lanes : (k + 1) * lanes], small_rate, slice(k, k + 1))
    for k in range(2):
        results = adam(
            state[15][k], state[16][k], state[17][k], slopes[k], scale, small_rate
        )
        for j in range(3):
            outs[19 + j][k] = results[j][0, 0]
    for copy in copies:
        copy.wait()


def per_device(
    tm_size,
    frames_in,
    item_lengths,
    out_cotangent,
    skip_cotangent,
    expand,
    expand_moment,
    expand_square,
    depthwise,
    depth_moment,
    depth_square,
    project,
    project_moment,
    project_square,
    channel_vectors,
    vector_moment,
    vector_square,
    output_biases,
    bias_moment,
    bias_square,
    prelu_slopes,
    slope_moment,
    slope_square,
):
    frames, inputs = frames_in.shape
    half = expand.shape[1]
    hidden = 2 * half
    items = item_lengths.shape[0]
    item_pad = -(-items // 16) * 16
    width = -(-3 * item_pad // LANES) * LANES
    wide = frames + 2 * HALO
    devices = 2 * tm_size
    reducers = 2 * PIECES
    peers = 2 * (-(-LONGEST_ITEM // frames))
    tile_rows = spots_of(item_pad)[0]
    vmem, smem, anywhere, hbm = (
        pl.BlockSpec(memory_space=space)
        for space in (pltpu.VMEM, pltpu.SMEM, pl.ANY, pltpu.HBM)
    )
    shape = jax.ShapeDtypeStruct
    scratch = [
        ((inputs, half), F32),
        ((2, half, inputs), F32),
        ((3, half), F32),
        ((6, half), F32),
        ((2, inputs), F32),
        ((wide, inputs), BF16),
        ((wide, 2 * inputs), BF16),
        ((inputs, hidden), BF16),
        ((hidden, 2 * inputs), BF16),
        ((16, hidden), F32),
        ((wide, width), BF16),
        ((item_pad, frames), BF16),
        ((wide, LANES), F32),
        ((wide, LANES), F32),
        ((width, 4 * LANES), BF16),
        ((peers + 1, 1, LANES), F32),
        ((wide, hidden), F32),
        ((wide, hidden), F32),
        ((wide, hidden), F32),
        ((wide, hidden), F32),
        ((wide, hidden), F32),
        ((frames, hidden), BF16),
        ((frames, hidden), BF16),
        ((frames, 8 * LANES), BF16),
        ((COLUMN_SUMS, 8, hidden), F32),
        ((tile_rows, LANES), F32),
        ((tile_rows, LANES), F32),
        ((tile_rows, LANES), F32),
        ((peers, tile_rows, LANES), F32),
        ((peers, tile_rows, LANES), F32),
        ((peers, tile_rows, LANES), F32),
        ((2 * inputs, hidden), F32),
        ((inputs, hidden), F32),
        ((inputs, hidden), F32),
        ((2, inputs, LANES), F32),
        ((tm_size, 16, half), F32),
        ((tm_size, 16, LANES), F32),
        ((2, 16, half), F32),
        ((devices, 16, half), F32),
        ((2, 2, half), F32),
        ((devices, 2, half), F32),
        ((2 * inputs, half), F32),
        ((16, half), F32),
        ((1, LANES), F32),
        ((24, LANES), F32),
        ((reducers, 24, LANES), F32),
    ]
    block_raw, skip_raw, input_raw, expand_grad, project_grad, small_grad = pl.pallas_call(
        functools.partial(block_kernel, tm_size, items, item_pad),
        out_shape=[
            shape((frames, inputs), BF16),
            shape((frames, inputs), BF16),
            shape((frames, inputs), F32),
            shape((inputs, half), F32),
            shape((2, half, inputs), F32),
            shape((16, half), F32),
        ],
        in_specs=[hbm] * 10,
        out_specs=[vmem] * 6,
        scratch_shapes=[pltpu.SMEM((items,), jnp.int32), pltpu.SMEM((2,), F32)]
        + [pltpu.VMEM(s, t) for s, t in scratch]
        + [
            pltpu.SemaphoreType.DMA((10,)),
            pltpu.SemaphoreType.DMA((19,)),
            pltpu.SemaphoreType.DMA((19,)),
            pltpu.SemaphoreType.DMA((3, peers)),
            pltpu.SemaphoreType.DMA((3, peers)),
        ],
        compiler_params=pltpu.CompilerParams(
            collective_id=0, has_side_effects=True, vmem_limit_bytes=52 * 2**20
        ),
        name="temporal_block",
    )(
        *[
            pltpu.with_memory_space_constraint(v, pltpu.HBM)
            for v in (
                item_lengths,
                prelu_slopes,
                frames_in,
                out_cotangent,
                skip_cotangent,
                expand,
                project,
                depthwise,
                channel_vectors,
                output_biases,
            )
        ]
    )
    state = [
        expand,
        expand_moment,
        expand_square,
        depthwise,
        depth_moment,
        depth_square,
        project,
        project_moment,
        project_square,
        channel_vectors,
        vector_moment,
        vector_square,
        output_biases,
        bias_moment,
        bias_square,
        prelu_slopes,
        slope_moment,
        slope_square,
    ]
    results = pl.pallas_call(
        adam_kernel,
        out_shape=[
            shape((frames, inputs), BF16),
            shape((frames, inputs), BF16),
            shape((frames, inputs), F32),
            shape((1, 1), F32),
        ]
        + [shape(v.shape, F32) for v in state],
        in_specs=[anywhere] * 3 + [vmem] * 18 + [smem] * 3,
        out_specs=[anywhere] * 3 + [smem] + [vmem] * 15 + [smem] * 3,
        scratch_shapes=[pltpu.SemaphoreType.DMA((3,))],
        compiler_params=pltpu.CompilerParams(vmem_limit_bytes=32 * 2**20),
        name="adam_step",
    )(block_raw, skip_raw, input_raw, expand_grad, project_grad, small_grad, *state)
    results = list(results)
    results[3] = results[3].reshape(())
    return tuple(results)


def solution(mesh):
    frames = P(("tm", "chan"), None)
    columns = P(None, "chan")
    rows = P(None, "chan", None)
    in_specs = (
        (frames, P(), frames, frames)
        + (columns,) * 3
        + (columns,) * 3
        + (rows,) * 3
        + (columns,) * 3
        + (P(),) * 6
    )
    out_specs = (
        (frames, frames, frames, P())
        + (columns,) * 3
        + (columns,) * 3
        + (rows,) * 3
        + (columns,) * 3
        + (P(),) * 6
    )
    return jax.shard_map(
        functools.partial(per_device, mesh.shape["tm"]),
        mesh=mesh,
        in_specs=in_specs,
        out_specs=out_specs,
        check_vma=False,
    )
```

```python
import functools

import jax
import jax.numpy as jnp
from jax import lax
from jax.experimental import pallas as pl
from jax.experimental.pallas import tpu as pltpu
from jax.sharding import PartitionSpec as P

F32 = jnp.float32
BF16 = jnp.bfloat16
MESH = pl.DeviceIdType.MESH

DILATION = 16
HALO = 2 * DILATION
LONGEST_ITEM = 8192
LANES = 128
ROWS = 64
BLOCK = 512
PIECES = 16

norm_eps = 1e-06
clip_level = 5.0
rate = 0.05
small_rate = 0.5
beta_first = 0.9
beta_second = 0.999
adam_eps = 1e-08
decay = 0.01
step_count = 10.0

TAP_ROW = 6
BIAS_ROW = 9
SLOPE_TWO_ROW = 10
SLOPE_ONE_ROW = 11
SQUARES_ROW = 12

(GAIN_TWO, SHIFT_TWO, TAP_A, TAP_B, TAP_C, DEPTH_BIAS, GAIN_ONE, SHIFT_ONE, SLOPE_TWO, SLOPE_ONE, COLUMN_SUMS) = range(11)


def dot(a, b):
    return lax.dot_general(a, b, (((1,), (0,)), ((), ())), preferred_element_type=F32)


def dot_rows(a, b):
    return lax.dot_general(a, b, (((1,), (1,)), ((), ())), preferred_element_type=F32)


def dot_frames(a, b):
    return lax.dot_general(a, b, (((0,), (0,)), ((), ())), preferred_element_type=F32)


def rounded(v):
    return v.astype(BF16).astype(F32)


def spread_lanes(v):
    return jnp.broadcast_to(jnp.sum(v, axis=1, keepdims=True), (v.shape[0], LANES))


def in_hbm(arrays):
    return [pltpu.with_memory_space_constraint(v, pltpu.HBM) for v in arrays]


def spots_of(item_pad):
    names = ("sum", "spread", "mean", "crossed")
    if 4 * item_pad <= LANES:
        return 2, {**{n: (0, k * item_pad) for k, n in enumerate(names)}, "q": (1, 2 * item_pad)}
    return 5, {n: (k, 0) for k, n in enumerate(names + ("q",))}


def fold_rows(v):
    return jnp.sum(v.reshape(v.shape[0] // 8, 8, v.shape[1]), axis=0)


def block_kernel(
    tm_size,
    item_count,
    item_pad,
    len_hbm,
    slope_hbm,
    frames_hbm,
    out_cot_hbm,
    skip_cot_hbm,
    *refs,
):
    state_hbm, refs = refs[:15], refs[15:]
    block_out, skip_out, input_out, expand_grad_ref, project_grad_ref, small_grad_ref = refs[:6]
    state_refs, refs = refs[6:21], refs[21:]
    expand_ref, taps_ref, project_ref, vectors_ref, biases_ref = state_refs[::3]
    (
    len_ref,
    slope_ref,
    x,
    cots,
    w_expand,
    w_project,
    params,
    item_rows,
    item_cols,
    mask_low,
    mask_high,
    table,
    counts,
    act_one,
    xhat_one,
    normed,
    mixed_grad,
    act_two,
    mixed,
    hidden_grad,
    seg,
    column,
    tile_one,
    tile_two,
    tile_three,
    stats_one,
    stats_two,
    stats_three,
    project_part,
    expand_part,
    project_pair,
    expand_pair,
    project_in,
    expand_in,
    small_part,
    small_pair,
    small_in,
    late_part,
    late_in,
    project_sum,
    small_sum,
    square_part,
    last_part,
    last_in,
    tail_in,
    local_sem,
    send_sem,
    recv_sem,
    near_send,
    near_recv,
    ) = refs
    frames = block_out.shape[0]
    wide = x.shape[0]
    half = expand_ref.shape[1]
    hidden = 2 * half
    blocks = hidden // LANES
    devices = 2 * tm_size
    stride = tm_size // PIECES
    spans = -(-LONGEST_ITEM // frames)
    chan = lax.axis_index("chan")
    tm = lax.axis_index("tm")
    me = tm * 2 + chan
    other = 1 - chan

    def device(index):
        return {"chan": lax.rem(index, 2), "tm": lax.div(index, 2)}

    def remote(src, dst, phase, target):
        return pltpu.make_async_remote_copy(
            src_ref=src,
            dst_ref=dst,
            send_sem=send_sem.at[phase],
            recv_sem=recv_sem.at[phase],
            device_id=target,
            device_id_type=MESH,
        )

    def wait_bytes(ref, sem):
        pltpu.make_async_copy(ref, ref, sem).wait()

    pending = {}

    def settle(*keys):
        for key in keys:
            pending.pop(key)()

    def started(copy, name, sends=None, receives=None):
        def maybe(condition, body):
            if condition is None:
                body()
            else:
                pl.when(condition)(body)

        maybe(sends, copy.start)
        pending[name, "sent"] = lambda: maybe(sends, copy.wait_send)
        pending[name, "here"] = lambda: maybe(receives, copy.wait_recv)

    own = pl.ds(HALO, frames)
    loads = {
        "expand": (state_hbm[0], expand_ref),
        "frames": (frames_hbm, x.at[own, :]),
        "vectors": (state_hbm[9], vectors_ref),
        "taps": (state_hbm[3], taps_ref),
        "lengths": (len_hbm, len_ref),
        "slopes": (slope_hbm, slope_ref),
        "project": (state_hbm[6], project_ref),
        "out": (out_cot_hbm, cots.at[own, pl.ds(0, LANES)]),
        "skip": (skip_cot_hbm, cots.at[own, pl.ds(LANES, LANES)]),
        "biases": (state_hbm[12], biases_ref),
    }
    for k, (name, (src, dst)) in enumerate(loads.items()):
        load = pltpu.make_async_copy(src, dst, local_sem.at[k])
        load.start()
        pending["load", name] = load.wait

    def loaded(*names):
        settle(*[("load", name) for name in names])

    for r in (0, HALO + frames):
        x[r : r + HALO, :] = jnp.zeros((HALO, x.shape[1]), BF16)
    for r in (HALO - DILATION, HALO + frames):
        cots[r : r + DILATION, :] = jnp.zeros((DILATION, cots.shape[1]), BF16)
    for stats in (stats_one, stats_two, stats_three):
        stats[...] = jnp.zeros_like(stats)

    barrier = pltpu.get_barrier_semaphore()

    def greet(k, carry):
        pl.semaphore_signal(
            barrier, inc=1, device_id=device(lax.rem(me + k, devices)), device_id_type=MESH
        )
        return carry

    lax.fori_loop(1, devices, greet, 0)

    my_half = pl.ds(pl.multiple_of(chan * half, half), half)
    loaded("expand", "vectors", "taps")
    w_expand[:, my_half] = expand_ref[...].astype(BF16)
    params[0:6, my_half] = vectors_ref[...]
    params[6:9, my_half] = taps_ref[...]
    params[9:12, my_half] = vectors_ref[1:2, :] * taps_ref[...]
    params[12:16, my_half] = jnp.zeros((4, half), F32)
    loaded("frames")
    pl.semaphore_wait(barrier, devices - 1)

    partner = device(tm * 2 + other)
    left, right = device(me - 1), device(me + 1)
    has_left, has_right = me > 0, me < devices - 1

    def to_left(ref, count, name):
        copy = remote(
            ref.at[pl.ds(HALO, count), :], ref.at[pl.ds(HALO + frames, count), :], name, left
        )
        started(copy, name, has_left, has_right)

    def to_right(ref, count, name):
        copy = remote(
            ref.at[pl.ds(HALO + frames - count, count), :],
            ref.at[pl.ds(HALO - count, count), :],
            name,
            right,
        )
        started(copy, name, has_right, has_left)

    started(remote(w_expand.at[:, my_half], w_expand.at[:, my_half], 0, partner), 0)
    started(remote(params.at[:, my_half], params.at[:, my_half], 1, partner), 1)
    to_left(x, HALO, 2)
    to_right(x, HALO, 3)
    loaded("project", "out", "skip")
    w_project[my_half, 0:LANES] = project_ref[0].astype(BF16)
    w_project[my_half, LANES : 2 * LANES] = project_ref[1].astype(BF16)
    started(remote(w_project.at[my_half, :], w_project.at[my_half, :], 4, partner), 4)
    to_left(cots, DILATION, 5)
    to_right(cots, DILATION, 6)
    loaded("lengths", "slopes", "biases")
    moments = [k for k in range(15) if k % 3]
    for k in moments:
        load = pltpu.make_async_copy(state_hbm[k], state_refs[k], local_sem.at[10 + k])
        load.start()
        pending["load", k] = load.wait

    width = table.shape[0]
    lane = lax.broadcasted_iota(jnp.int32, (8, width), 1)
    lane_item = lax.rem(lane, item_pad)
    row_item = lax.broadcasted_iota(jnp.int32, (item_pad, LANES), 0)

    def bounds(j, carry):
        lane_start, lane_end, row_start, row_end = carry
        length = len_ref[j]
        return (
            lane_start + jnp.where(lane_item > j, length, 0),
            lane_end + jnp.where(lane_item >= j, length, 0),
            row_start + jnp.where(row_item > j, length, 0),
            row_end + jnp.where(row_item >= j, length, 0),
        )

    lane_zero, row_zero = jnp.zeros_like(lane), jnp.zeros_like(row_item)
    lane_start, lane_end, row_start, row_end = lax.fori_loop(
        0, item_count, bounds, (lane_zero, lane_zero, row_zero, row_zero)
    )
    lane_end = jnp.where(lane < 3 * item_pad, lane_end, lane_start)
    first = me * frames
    lane_start_row, lane_end_row = lane_start[0:1], lane_end[0:1]
    elements = jnp.maximum((row_end - row_start).astype(F32) * hidden, 1.0)

    def count_of(index):
        low = jnp.maximum(row_start, index * frames)
        high = jnp.minimum(row_end, (index + 1) * frames)
        return jnp.maximum(high - low, 0).astype(F32) * hidden

    my_count = count_of(me)
    my_safe = jnp.maximum(my_count, 1.0)
    offsets = [sign * o for o in range(spans, 0, -1) for sign in (1, -1)]
    spots = spots_of(item_pad)[1]
    tile_lane = lax.broadcasted_iota(jnp.int32, (item_pad, LANES), 1)

    def packed(v, name):
        chosen = tile_lane == spots[name][1] + row_item
        return jnp.sum(jnp.where(chosen, v, 0.0), axis=0, keepdims=True)

    def unpacked(row, name):
        chosen = tile_lane == spots[name][1] + row_item
        return spread_lanes(jnp.where(chosen, jnp.broadcast_to(row, chosen.shape), 0.0))

    counts[len(offsets)] = packed(my_count, "mean")
    for slot, offset in enumerate(offsets):
        counts[slot] = packed(count_of(me - offset), "mean")
    column[...] = jnp.zeros_like(column)

    def put_table(place, v):
        high = v.astype(BF16)
        rest = v - high.astype(F32)
        middle = rest.astype(BF16)
        low = (rest - middle.astype(F32)).astype(BF16)
        where = slice(place * LANES, (place + 1) * LANES)
        table[0:item_pad, where] = high
        table[item_pad : 2 * item_pad, where] = middle
        table[2 * item_pad : 3 * item_pad, where] = low

    def rows_of(r, n, count):
        return dot(item_rows[pl.ds(r, n), :], table[:, 0 : count * LANES])

    def part(values, k, n, b):
        return values[k : k + n, b * LANES : (b + 1) * LANES]

    def put_seg(r, n, place, v, exact=True):
        high = v.astype(BF16)
        seg[pl.ds(r, n), pl.ds(place * LANES, LANES)] = high
        if exact:
            low = (v - high.astype(F32)).astype(BF16)
            seg[pl.ds(r, n), pl.ds((place + 1) * LANES, LANES)] = low

    def item_sums(first, widths):
        sums = dot(item_cols[...], seg[:, first * LANES : (first + sum(widths)) * LANES])
        results, k = [], 0
        for n in widths:
            v = sums[:, k * LANES : (k + 1) * LANES]
            if n == 2:
                v = v + sums[:, (k + 1) * LANES : (k + 2) * LANES]
            results.append(spread_lanes(v))
            k += n
        return results

    def loop(start, size, count, body, rep=1):
        def step(i, carry):
            i = i if rep == 1 else lax.rem(i, count)
            body(pl.multiple_of(start + i * size, 16))
            return carry

        lax.fori_loop(0, count * rep, step, 0)

    def at(r, k, shift=0):
        return pl.multiple_of(r + (k - shift), 16)

    table[...] = jnp.zeros_like(table)
    put_table(0, row_start.astype(F32))
    put_table(1, row_end.astype(F32))

    wide_block = wide // 4
    wide_rows = wide_block // 11

    @functools.partial(loop, 0, wide_block, 4)
    def _(r):
        for k in range(0, wide_block, wide_rows):
            position = first - HALO + r + k + lax.broadcasted_iota(jnp.int32, (wide_rows, width), 0)
            inside = (position >= lane_start_row) & (position < lane_end_row)
            item_rows[pl.ds(at(r, k), wide_rows), :] = inside.astype(F32).astype(BF16)
        ends = rows_of(r, wide_block, 2)
        for k in range(0, wide_block, wide_rows):
            here = first - HALO + r + k + lax.broadcasted_iota(jnp.int32, (wide_rows, LANES), 0)
            here = here.astype(F32)
            after = here - part(ends, k, wide_rows, 0)
            before = part(ends, k, wide_rows, 1) - here
            mask_low[pl.ds(at(r, k), wide_rows), :] = (after >= DILATION).astype(F32)
            mask_high[pl.ds(at(r, k), wide_rows), :] = (before > DILATION).astype(F32)

    for i in range(frames // LANES):
        position = first + i * LANES + lax.broadcasted_iota(jnp.int32, (item_pad, LANES), 1)
        inside = (position >= row_start) & (position < row_end)
        item_cols[:, i * LANES : (i + 1) * LANES] = inside.astype(F32).astype(BF16)

    slope_one, slope_two = slope_ref[0], slope_ref[1]

    def lanes_of(which, b):
        return pl.ds(pl.multiple_of(which * half + b * LANES, LANES), LANES)

    def half_of(which):
        return pl.ds(pl.multiple_of(which * half, half), half)

    def activate(product, k, n, which, b):
        v = part(product, k, n, b) + params[0:1, lanes_of(which, b)]
        return jnp.maximum(v, slope_one * v)

    own_loop = functools.partial(functools.partial, loop, HALO, BLOCK, frames // BLOCK)

    @own_loop()
    def _(r):
        product = dot(x[pl.ds(r, BLOCK), :], w_expand[:, half_of(chan)])
        for k in range(0, BLOCK, ROWS):
            total = jnp.zeros((ROWS, LANES), F32)
            for b in range(blocks // 2):
                a = activate(product, k, ROWS, chan, b)
                act_one[pl.ds(at(r, k), ROWS), lanes_of(chan, b)] = a
                total = total + a
            put_seg(at(r, k, HALO), ROWS, 0, total)

    (total,) = item_sums(0, (2,))
    shift = total / jnp.maximum(my_count * 0.5, 1.0)
    put_table(0, shift)
    settle(*[(k, "here") for k in range(4)])

    @own_loop()
    def _(r):
        centres = rows_of(r, BLOCK, 1)
        product = dot(x[pl.ds(r, BLOCK), :], w_expand[:, half_of(other)])
        for k in range(0, BLOCK, ROWS):
            rows = pl.ds(at(r, k), ROWS)
            centre = part(centres, k, ROWS, 0)
            total = jnp.zeros((ROWS, LANES), F32)
            squares = jnp.zeros((ROWS, LANES), F32)
            for b in range(blocks // 2):
                d = act_one[rows, lanes_of(chan, b)] - centre
                total = total + d
                squares = squares + d * d
                a = activate(product, k, ROWS, other, b)
                act_one[rows, lanes_of(other, b)] = a
                d = a - centre
                total = total + d
                squares = squares + d * d
            put_seg(at(r, k, HALO), ROWS, 0, total)
            put_seg(at(r, k, HALO), ROWS, 2, squares)

    def pack_tile(tile, values):
        for r in range(tile.shape[0]):
            row = jnp.zeros((1, LANES), F32)
            for name, v in values.items():
                if spots[name][0] == r:
                    row = row + packed(v, name)
            tile[r : r + 1, :] = row

    def local_moments(shift, total, squares):
        mean = shift + total / my_safe
        spread = jnp.maximum(squares - total * total / my_safe, 0.0)
        return mean, spread

    def exchange(tile, stats, phase):
        def near(slot, offset):
            return pltpu.make_async_remote_copy(
                src_ref=tile,
                dst_ref=stats.at[slot],
                send_sem=near_send.at[phase, slot],
                recv_sem=near_recv.at[phase, slot],
                device_id=device(me + offset),
                device_id_type=MESH,
            )

        def all_near(source, act):
            for slot, offset in enumerate(offsets):
                index = me - offset if source else me + offset
                pl.when((index >= 0) & (index < devices))(lambda: act(near(slot, offset)))

        all_near(False, lambda copy: copy.start())
        pending["near", phase, "sent"] = lambda: all_near(False, lambda copy: copy.wait_send())
        pending["near", phase, "here"] = lambda: all_near(True, lambda copy: copy.wait_recv())

    def rows_with(name, tile, stats):
        r = spots[name][0]
        return [stats[slot, r : r + 1, :] for slot in range(len(offsets))] + [tile[r : r + 1, :]]

    def sum_of(name, tile, stats):
        total = None
        for row in rows_with(name, tile, stats):
            total = row if total is None else total + row
        return unpacked(total, name)

    def combined(tile, stats):
        mean = sum_of("sum", tile, stats) / elements
        centre = packed(mean, "mean")
        between = jnp.zeros((1, LANES), F32)
        for k, row in enumerate(rows_with("mean", tile, stats)):
            between = between + counts[k] * (row - centre) * (row - centre)
        spread = (sum_of("spread", tile, stats) + unpacked(between, "mean")) / elements
        return mean, centre, lax.rsqrt(spread + norm_eps)

    total, squares = item_sums(0, (2, 2))
    mean, spread = local_moments(shift, total, squares)
    pack_tile(tile_one, {"sum": mean * my_count, "spread": spread, "mean": mean})
    exchange(tile_one, stats_one, 0)

    for r in (0, HALO + frames):
        for which in (chan, other):
            product = dot(x[pl.ds(r, HALO), :], w_expand[:, half_of(which)])
            for b in range(blocks // 2):
                act_one[pl.ds(r, HALO), lanes_of(which, b)] = activate(product, 0, HALO, which, b)

    settle(*[(k, "here") for k in (4, 5, 6)])

    def lanes(b):
        return pl.ds(b * LANES, LANES)

    def mixed_rows(r, n, size, add):
        product = dot_rows(cots[pl.ds(r, n), :], w_project[...])
        for k in range(0, n, size):
            total = jnp.zeros((size, LANES), F32)
            for b in range(blocks):
                q = params[4:5, lanes(b)] * part(product, k, size, b)
                mixed_grad[pl.ds(at(r, k), size), lanes(b)] = q
                if add:
                    total = total + q
                    column[SHIFT_TWO, :, lanes(b)] += fold_rows(q)
            if add:
                put_seg(at(r, k, HALO), size, 4, total)

    @own_loop()
    def _(r):
        mixed_rows(r, BLOCK, ROWS, True)

    for r in (HALO - DILATION, HALO + frames):
        mixed_rows(r, DILATION, DILATION, False)
    bias_sum = dot(jnp.ones((16, frames), BF16), cots[own, :])[0:1]
    (q_sum,) = item_sums(4, (2,))

    settle(("near", 0, "here"))
    mean_one, _, scale_one = combined(tile_one, stats_one)
    put_table(0, mean_one)
    put_table(1, scale_one)

    @functools.partial(loop, 0, wide_block, 4)
    def _(r):
        values = rows_of(r, wide_block, 2)
        for k in range(0, wide_block, wide_rows):
            rows = pl.ds(at(r, k), wide_rows)
            mean, scale = part(values, k, wide_rows, 0), part(values, k, wide_rows, 1)
            for b in range(blocks):
                xhat = (act_one[rows, lanes(b)] - mean) * scale
                xhat_one[rows, lanes(b)] = xhat
                normed[rows, lanes(b)] = rounded(
                    params[1:2, lanes(b)] * xhat + params[2:3, lanes(b)]
                )

    def depth_rows(r, n, b):
        low, high = mask_low[pl.ds(r, n), :], mask_high[pl.ds(r, n), :]
        v = (
            params[3:4, lanes(b)]
            + params[6:7, lanes(b)] * (low * normed[pl.ds(r - DILATION, n), lanes(b)])
            + params[7:8, lanes(b)] * normed[pl.ds(r, n), lanes(b)]
            + params[8:9, lanes(b)] * (high * normed[pl.ds(r + DILATION, n), lanes(b)])
        )
        return jnp.maximum(v, slope_two * v)

    @own_loop()
    def _(r):
        for k in range(0, BLOCK, ROWS):
            a = depth_rows(at(r, k), ROWS, 0)
            act_two[pl.ds(at(r, k), ROWS), lanes(0)] = a
            put_seg(at(r, k, HALO), ROWS, 0, a)

    (total,) = item_sums(0, (2,))
    shift = total / jnp.maximum(my_count * (1.0 / blocks), 1.0)
    put_table(0, shift)

    @own_loop()
    def _(r):
        centres = rows_of(r, BLOCK, 1)
        for k in range(0, BLOCK, ROWS):
            rows = pl.ds(at(r, k), ROWS)
            centre = part(centres, k, ROWS, 0)
            total = jnp.zeros((ROWS, LANES), F32)
            squares = jnp.zeros((ROWS, LANES), F32)
            crossed = jnp.zeros((ROWS, LANES), F32)
            for b in range(blocks):
                if b == 0:
                    a = act_two[rows, lanes(b)]
                else:
                    a = depth_rows(at(r, k), ROWS, b)
                    act_two[rows, lanes(b)] = a
                d = a - centre
                total = total + d
                squares = squares + d * d
                crossed = crossed + mixed_grad[rows, lanes(b)] * d
            put_seg(at(r, k, HALO), ROWS, 0, total)
            put_seg(at(r, k, HALO), ROWS, 2, squares, exact=False)
            put_seg(at(r, k, HALO), ROWS, 3, crossed, exact=False)

    total, squares, crossed = item_sums(0, (2, 1, 1))
    mean, spread = local_moments(shift, total, squares)
    crossed = crossed - (mean - shift) * q_sum
    values = {"sum": mean * my_count, "spread": spread, "mean": mean, "crossed": crossed, "q": q_sum}
    pack_tile(tile_two, values)
    exchange(tile_two, stats_two, 1)

    for r in (HALO - DILATION, HALO + frames):
        for b in range(blocks):
            act_two[pl.ds(r, DILATION), lanes(b)] = depth_rows(r, DILATION, b)

    settle(("near", 1, "here"))
    mean_two, centre, scale_two = combined(tile_two, stats_two)
    between = jnp.zeros((1, LANES), F32)
    for row, q_row in zip(rows_with("mean", tile_two, stats_two), rows_with("q", tile_two, stats_two)):
        between = between + (row - centre) * q_row
    cross_sum = sum_of("crossed", tile_two, stats_two) + unpacked(between, "mean")
    put_table(0, mean_two)
    put_table(1, scale_two)
    put_table(2, scale_two * sum_of("q", tile_two, stats_two) / elements)
    put_table(3, scale_two * scale_two * cross_sum / elements)

    def second_back(r, n, size, add):
        values = rows_of(r, n, 4)
        for k in range(0, n, size):
            rows = pl.ds(at(r, k), size)
            mean, scale, q_mean, cross_mean = [part(values, k, size, j) for j in range(4)]
            for b in range(blocks):
                a = act_two[rows, lanes(b)]
                q = mixed_grad[rows, lanes(b)]
                xhat = (a - mean) * scale
                g = q * scale - q_mean - xhat * cross_mean
                act_two[rows, lanes(b)] = rounded(g * jnp.where(a > 0, 1.0, slope_two))
                if add:
                    mixed[pl.ds(at(r, k, HALO), size), lanes(b)] = (
                        params[4:5, lanes(b)] * xhat + params[5:6, lanes(b)]
                    ).astype(BF16)
                    column[GAIN_TWO, :, lanes(b)] += fold_rows(q * xhat)
                    column[SLOPE_TWO, :, lanes(b)] += fold_rows(g * jnp.minimum(a, 0.0))

    @own_loop()
    def _(r):
        second_back(r, BLOCK, ROWS, True)

    for r in (HALO - DILATION, HALO + frames):
        second_back(r, DILATION, DILATION, False)

    @functools.partial(loop, HALO, 2 * ROWS, frames // (2 * ROWS))
    def _(r):
        for k in range(0, 2 * ROWS, ROWS):
            rows = pl.ds(at(r, k), ROWS)
            low, high = mask_low[rows, :], mask_high[rows, :]
            total = jnp.zeros((ROWS, LANES), F32)
            crossed = jnp.zeros((ROWS, LANES), F32)
            for b in range(blocks):
                later = high * act_two[pl.ds(at(r, k + DILATION), ROWS), lanes(b)]
                here = act_two[rows, lanes(b)]
                earlier = low * act_two[pl.ds(at(r, k - DILATION), ROWS), lanes(b)]
                n = normed[rows, lanes(b)]
                column[TAP_A, :, lanes(b)] += fold_rows(later * n)
                column[TAP_B, :, lanes(b)] += fold_rows(here * n)
                column[TAP_C, :, lanes(b)] += fold_rows(earlier * n)
                column[DEPTH_BIAS, :, lanes(b)] += fold_rows(here)
                q = (
                    params[9:10, lanes(b)] * later
                    + params[10:11, lanes(b)] * here
                    + params[11:12, lanes(b)] * earlier
                )
                mixed_grad[rows, lanes(b)] = q
                column[SHIFT_ONE, :, lanes(b)] += fold_rows(q)
                q_xhat = q * xhat_one[rows, lanes(b)]
                column[GAIN_ONE, :, lanes(b)] += fold_rows(q_xhat)
                total = total + q
                crossed = crossed + q_xhat
            put_seg(at(r, k, HALO), ROWS, 0, total)
            put_seg(at(r, k, HALO), ROWS, 2, crossed)

    total, crossed = item_sums(0, (2, 2))
    pack_tile(tile_three, {"sum": total, "crossed": crossed})
    exchange(tile_three, stats_three, 2)

    step = 512
    total = jnp.zeros((2 * LANES, hidden), F32)
    for k in range(frames // step):
        total = total + dot_frames(
            cots[pl.ds(HALO + k * step, step), :], mixed[pl.ds(k * step, step), :]
        )
    project_part[...] = total

    core = lax.rem(tm, 2)
    sibling = {"chan": chan, "tm": tm + 1 - 2 * core}
    mine = pl.ds(pl.multiple_of(core * LANES, LANES), LANES)
    yours = pl.ds(pl.multiple_of((1 - core) * LANES, LANES), LANES)
    started(remote(project_part.at[yours, :], project_pair, 7, sibling), 7)

    def column_sum(which):
        return jnp.sum(column[which], axis=0, keepdims=True)

    early_rows = {
        1: column_sum(GAIN_ONE) / params[1:2, :],
        2: column_sum(SHIFT_ONE) / params[1:2, :],
        3: column_sum(DEPTH_BIAS),
        4: column_sum(GAIN_TWO) / params[4:5, :],
        5: column_sum(SHIFT_TWO) / params[4:5, :],
        TAP_ROW: column_sum(TAP_A),
        TAP_ROW + 1: column_sum(TAP_B),
        TAP_ROW + 2: column_sum(TAP_C),
    }
    slope_two_row = column_sum(SLOPE_TWO)
    slope_two_row = (slope_two_row[:, 0:half] + slope_two_row[:, half:hidden]) / slope_two
    for c in range(2):
        small_part[c] = jnp.zeros((16, half), F32)
        for row, v in early_rows.items():
            small_part[c, row : row + 1, :] = v[:, c * half : (c + 1) * half]
        small_part[c, BIAS_ROW : BIAS_ROW + 1, :] = bias_sum
        small_part[c, SLOPE_TWO_ROW : SLOPE_TWO_ROW + 1, :] = slope_two_row

    chips = tm_size // 2
    chip = lax.div(tm, 2)
    mates = 2 * chips
    mate = chip * 2 + chan
    spot = lax.div(chip, stride)
    is_reducer = lax.rem(chip, stride) == 0

    def when_reducer(body):
        if stride == 1:
            body()
        else:
            pl.when(is_reducer)(body)

    def by_role(body, count):
        if stride == 1:
            body(count - 1)
        else:
            pl.when(is_reducer)(lambda: body(count - 1))
            pl.when(jnp.logical_not(is_reducer))(lambda: body(count))

    def to_reducers(source, ref, phase):
        def one(k, carry):
            q = lax.rem(spot * 2 + chan + k, PIECES)
            c, at_spot = lax.rem(q, 2), lax.div(q, 2)
            target = {"chan": c, "tm": at_spot * stride * 2 + core}

            def send():
                remote(source(c, at_spot), ref.at[mate], phase, target).start()

            if stride == 1:
                send()
            else:
                pl.when(at_spot * stride * 2 + c != mate)(send)
            return carry

        lax.fori_loop(1 if stride == 1 else 0, PIECES, one, 0)
        pending[phase, "sent"] = lambda: by_role(
            lambda n: wait_bytes(ref.at[pl.ds(0, n)], send_sem.at[phase]), PIECES
        )
        pending[phase, "here"] = lambda: when_reducer(
            lambda: wait_bytes(ref.at[pl.ds(0, mates - 1)], recv_sem.at[phase])
        )

    def piece_rows(at_spot):
        return pl.ds(pl.multiple_of(at_spot * 16, 16), 16)

    def project_piece(c, at_spot):
        return project_pair.at[piece_rows(at_spot), pl.ds(pl.multiple_of(c * half, half), half)]

    def expand_piece(c, at_spot):
        return expand_pair.at[c, piece_rows(at_spot), :]

    keeper = chips // 2 // stride * stride * 2
    is_keeper = tm == keeper

    def to_keepers(parts, ref, slot, count, phase, sends):
        def each(act):
            for c in range(2):
                copy = remote(parts.at[c], ref.at[slot], phase + c, {"chan": c, "tm": keeper})
                pl.when(sends & ((tm != keeper) | (chan != c)))(lambda: act(copy))

        each(lambda copy: copy.start())
        pending[phase, "sent"] = lambda: each(lambda copy: copy.wait_send())
        pending[phase, "here"] = lambda: [
            pl.when(is_keeper & (chan == c))(
                lambda: wait_bytes(ref.at[pl.ds(0, count - 1)], recv_sem.at[phase + c])
            )
            for c in range(2)
        ]

    pair = remote(small_part, small_pair, 10, sibling)
    started(pair, 10, core == 1, core == 0)
    settle((7, "here"))
    project_pair[...] += project_part[mine, :]
    to_reducers(project_piece, project_in, 11)
    settle((10, "here"))

    @pl.when(core == 0)
    def _():
        small_part[...] += small_pair[...]

    to_keepers(small_part, small_in, mate, mates, 12, core == 0)

    @own_loop()
    def _(r):
        product = dot(mixed[pl.ds(at(r, 0, HALO), BLOCK), :], w_project[...])
        for k in range(0, BLOCK, ROWS):
            rows = pl.ds(at(r, k, HALO), ROWS)
            inputs = x[pl.ds(at(r, k), ROWS), :].astype(F32)
            block_out[rows, :] = (
                inputs + part(product, k, ROWS, 0) + biases_ref[0:1, :]
            ).astype(BF16)
            skip_out[rows, :] = (part(product, k, ROWS, 1) + biases_ref[1:2, :]).astype(BF16)

    settle(("near", 2, "here"))
    put_table(0, sum_of("sum", tile_three, stats_three) / elements)
    put_table(1, sum_of("crossed", tile_three, stats_three) / elements)
    put_table(2, scale_one)

    @own_loop()
    def _(r):
        values = rows_of(r, BLOCK, 3)
        for k in range(0, BLOCK, ROWS):
            rows, local = pl.ds(at(r, k), ROWS), pl.ds(at(r, k, HALO), ROWS)
            q_mean, cross_mean, scale = [part(values, k, ROWS, j) for j in range(3)]
            for b in range(blocks):
                a = act_one[rows, lanes(b)]
                g = (mixed_grad[rows, lanes(b)] - q_mean - xhat_one[rows, lanes(b)] * cross_mean) * scale
                column[SLOPE_ONE, :, lanes(b)] += fold_rows(g * jnp.minimum(a, 0.0))
                hidden_grad[local, lanes(b)] = (g * jnp.where(a > 0, 1.0, slope_one)).astype(BF16)

    total = jnp.zeros((LANES, hidden), F32)
    for k in range(frames // step):
        total = total + dot_frames(
            x[pl.ds(HALO + k * step, step), :], hidden_grad[pl.ds(k * step, step), :]
        )
    expand_part[...] = total
    for c in range(2):
        source = pl.ds(pl.multiple_of(c * half + (1 - core) * LANES, LANES), LANES)
        started(remote(expand_part.at[:, source], expand_pair.at[c], 8 + c, sibling), 8 + c)
    bias_one = dot(jnp.ones((16, frames), BF16), hidden_grad[...])[0:1]
    slope_row = column_sum(SLOPE_ONE)
    slope_row = (slope_row[:, 0:half] + slope_row[:, half:hidden]) / slope_one
    for c in range(2):
        late_part[c, 0:1, :] = bias_one[:, c * half : (c + 1) * half]
        late_part[c, 1:2, :] = slope_row
    to_keepers(late_part, late_in, me, devices, 14, tm >= 0)
    settle((8, "here"), (9, "here"))
    for c in range(2):
        expand_pair[c] += expand_part[
            :, pl.ds(pl.multiple_of(c * half + core * LANES, LANES), LANES)
        ]
    to_reducers(expand_piece, expand_in, 16)

    def total_of(ref, count, rows, cols):
        return lax.fori_loop(
            0, count, lambda k, total: total + ref[k], jnp.zeros((rows, cols), F32)
        )

    def fold_lanes(v):
        return v[:, 0:LANES] + v[:, LANES:half]

    def to_group(src, dst, phase, targets):
        def one(k, carry):
            target = (
                lax.rem(chip + k, chips) * 2 + core if targets == chips else lax.rem(tm + k, tm_size)
            )
            remote(src, dst, phase, {"chan": chan, "tm": target}).start()
            return carry

        lax.fori_loop(1, targets, one, 0)

    def group_sent(ref, phase, targets):
        def one(k, carry):
            wait_bytes(ref, send_sem.at[phase])
            return carry

        lax.fori_loop(1, targets, one, 0)

    settle((11, "here"))
    sum_rows = pl.ds(pl.multiple_of(core * LANES + spot * 16, 16), 16)

    @when_reducer
    def _():
        project_in[mate] = project_piece(chan, spot)[...]
        total = total_of(project_in, mates, 16, half)
        project_sum[sum_rows, :] = total
        square_part[...] = fold_lanes(jnp.sum(total * total, axis=0, keepdims=True))
        to_group(project_sum.at[sum_rows, :], project_sum.at[sum_rows, :], 17, chips)

    pending[17, "sent"] = lambda: when_reducer(
        lambda: group_sent(project_sum.at[pl.ds(0, 16), :], 17, chips)
    )
    pending[17, "here"] = lambda: by_role(
        lambda n: wait_bytes(project_sum.at[pl.ds(0, 16 * n), :], recv_sem.at[17]), PIECES // 2
    )
    settle((12, "here"))

    @pl.when(is_keeper)
    def _():
        small_in[mate] = small_part[chan]
        total = total_of(small_in, mates, 16, half)
        small_sum[...] = total
        square_part[...] += fold_lanes(
            jnp.sum((total * total)[0:BIAS_ROW], axis=0, keepdims=True)
        )
        to_group(small_sum, small_sum, 18, tm_size)

    pending[18, "sent"] = lambda: pl.when(is_keeper)(lambda: group_sent(small_sum, 18, tm_size))
    pending[18, "here"] = lambda: pl.when(jnp.logical_not(is_keeper))(
        lambda: wait_bytes(small_sum, recv_sem.at[18])
    )

    @own_loop()
    def _(r):
        product = dot_rows(hidden_grad[pl.ds(at(r, 0, HALO), BLOCK), :], w_expand[...])
        for k in range(0, BLOCK, ROWS):
            above = cots[pl.ds(at(r, k), ROWS), 0:LANES].astype(F32)
            input_out[pl.ds(at(r, k, HALO), ROWS), :] = above + part(product, k, ROWS, 0)

    last_part[...] = jnp.zeros_like(last_part)
    settle((14, "here"))

    @pl.when(is_keeper)
    def _():
        late_in[me] = late_part[chan]
        total = total_of(late_in, devices, 2, half)
        last_part[17:19, :] = total[:, 0:LANES]
        last_part[19:21, :] = total[:, LANES:half]
        squares = (total * total)[0:1]
        square_part[...] += fold_lanes(squares)

    settle((16, "here"))

    @when_reducer
    def _():
        expand_in[mate] = expand_piece(chan, spot)[...]
        total = total_of(expand_in, mates, 16, LANES)
        squares = square_part[...] + jnp.sum(total * total, axis=0, keepdims=True)
        square_part[...] = squares
        last_part[0:16, :] = total
        last_part[16:17, :] = squares
        last_in[core, spot] = last_part[...]

        def send_tail(k, carry):
            target = {"chan": other, "tm": lax.rem(chip + k, chips) * 2 + core}
            remote(square_part, tail_in.at[core, spot], 20, target).start()
            return carry

        to_group(last_part, last_in.at[core, spot], 19, chips)
        lax.fori_loop(0, chips, send_tail, 0)

    def tails_sent():
        for _ in range(stride):
            wait_bytes(tail_in.at[0], send_sem.at[20])

    pending[19, "sent"] = lambda: when_reducer(lambda: group_sent(last_part, 19, chips))
    pending[19, "here"] = lambda: by_role(
        lambda n: wait_bytes(last_in.at[0, pl.ds(0, n)], recv_sem.at[19]), PIECES // 2
    )
    pending[20, "sent"] = lambda: when_reducer(tails_sent)
    pending[20, "here"] = lambda: wait_bytes(tail_in.at[0], recv_sem.at[20])

    settle((17, "here"))
    started(remote(project_sum.at[mine, :], project_sum.at[mine, :], 21, sibling), 21)
    settle((19, "here"))
    started(remote(last_in.at[core], last_in.at[core], 22, sibling), 22)
    settle((20, "here"))
    started(remote(tail_in.at[core], tail_in.at[core], 23, sibling), 23)
    settle((18, "here"), (21, "here"))
    for k in range(2):
        project_grad_ref[k] = project_sum[k * LANES : (k + 1) * LANES, :].T
    small_grad_ref[...] = small_sum[...]
    settle((22, "here"), (23, "here"))
    for c in range(2):
        for j in range(PIECES // 2):
            expand_grad_ref[j * 16 : j * 16 + 16, c * LANES : (c + 1) * LANES] = last_in[c, j, 0:16]
    keeper_spot = keeper // 2 // stride
    for k in range(2):
        where = slice(k * LANES, (k + 1) * LANES)
        late = last_in[0, keeper_spot, 17 + 2 * k : 19 + 2 * k, :]
        small_grad_ref[0:1, where] = late[0:1]
        small_grad_ref[SLOPE_ONE_ROW : SLOPE_ONE_ROW + 1, where] = late[1:2]
    own_total, other_total = last_in[0, 0, 16:17, :], tail_in[0, 0]
    for q in range(1, PIECES):
        c, j = q // (PIECES // 2), q % (PIECES // 2)
        own_total = own_total + last_in[c, j, 16:17, :]
        other_total = other_total + tail_in[c, j]
    small_grad_ref[SQUARES_ROW : SQUARES_ROW + 1, 0:LANES] = own_total + other_total
    small_grad_ref[SQUARES_ROW : SQUARES_ROW + 1, LANES:half] = jnp.zeros((1, half - LANES), F32)

    settle(*list(pending))


def adam(weight, moment, square, gradient, scale, step_rate):
    clipped = gradient * scale
    moment_next = beta_first * moment + (1.0 - beta_first) * clipped
    square_next = beta_second * square + (1.0 - beta_second) * clipped * clipped
    update = (
        moment_next
        / (1.0 - beta_first**step_count)
        / (jnp.sqrt(square_next / (1.0 - beta_second**step_count)) + adam_eps)
    )
    return weight - step_rate * (update + decay * weight), moment_next, square_next


def adam_kernel(
    block_in,
    skip_in,
    input_in,
    expand_grad,
    project_grad,
    small_grad,
    *refs,
):
    state, outs, slope_refs = list(refs[:15]), refs[18:40], refs[40:43]
    sem = refs[43]
    slope_loads = [
        pltpu.make_async_copy(refs[15 + k], slope_refs[k], sem.at[3 + k]) for k in range(3)
    ]
    for load in slope_loads:
        load.start()
    state += slope_refs
    copies = [
        pltpu.make_async_copy(src, dst, sem.at[k])
        for k, (src, dst) in enumerate(
            zip((block_in, skip_in, input_in), (outs[0], outs[1], outs[2]))
        )
    ]
    for copy in copies:
        copy.start()
    biases = small_grad[BIAS_ROW : BIAS_ROW + 1, :]
    slopes = [
        jnp.sum(small_grad[row : row + 1, :], axis=1, keepdims=True)
        for row in (SLOPE_ONE_ROW, SLOPE_TWO_ROW)
    ]
    total = jnp.sum(small_grad[SQUARES_ROW : SQUARES_ROW + 1, :] + biases * biases, axis=1, keepdims=True)
    total = total + slopes[0] * slopes[0] + slopes[1] * slopes[1]
    grad_norm = jnp.sqrt(total)
    scale = jnp.minimum(1.0, clip_level / grad_norm)
    outs[3][0, 0] = grad_norm[0, 0]

    def update(k, gradient, step_rate, at=...):
        results = adam(
            state[3 * k][at], state[3 * k + 1][at], state[3 * k + 2][at], gradient, scale, step_rate
        )
        for j in range(3):
            outs[4 + 3 * k + j][at] = results[j]

    update(0, expand_grad[...], rate)
    update(1, small_grad[TAP_ROW : TAP_ROW + 3, :], small_rate)
    for k in range(2):
        update(2, project_grad[k], rate, k)
    update(3, small_grad[0:6, :], small_rate)
    lanes = biases.shape[1] // 2
    for k in range(2):
        update(4, biases[:, k * lanes : (k + 1) * lanes], small_rate, slice(k, k + 1))
    for load in slope_loads:
        load.wait()
    for k in range(2):
        results = adam(
            state[15][k], state[16][k], state[17][k], slopes[k], scale, small_rate
        )
        for j in range(3):
            outs[19 + j][k] = results[j][0, 0]
    for copy in copies:
        copy.wait()


def per_device(
    tm_size,
    frames_in,
    item_lengths,
    out_cotangent,
    skip_cotangent,
    expand,
    expand_moment,
    expand_square,
    depthwise,
    depth_moment,
    depth_square,
    project,
    project_moment,
    project_square,
    channel_vectors,
    vector_moment,
    vector_square,
    output_biases,
    bias_moment,
    bias_square,
    prelu_slopes,
    slope_moment,
    slope_square,
):
    frames, inputs = frames_in.shape
    half = expand.shape[1]
    hidden = 2 * half
    items = item_lengths.shape[0]
    item_pad = -(-items // 16) * 16
    width = -(-3 * item_pad // LANES) * LANES
    wide = frames + 2 * HALO
    devices = 2 * tm_size
    peers = 2 * (-(-LONGEST_ITEM // frames))
    tile_rows = spots_of(item_pad)[0]
    vmem, smem, anywhere, hbm = (
        pl.BlockSpec(memory_space=space)
        for space in (pltpu.VMEM, pltpu.SMEM, pl.ANY, pltpu.HBM)
    )
    shape = jax.ShapeDtypeStruct
    scratch = [
        ((wide, inputs), BF16),
        ((wide, 2 * inputs), BF16),
        ((inputs, hidden), BF16),
        ((hidden, 2 * inputs), BF16),
        ((16, hidden), F32),
        ((wide, width), BF16),
        ((item_pad, frames), BF16),
        ((wide, LANES), F32),
        ((wide, LANES), F32),
        ((width, 4 * LANES), BF16),
        ((peers + 1, 1, LANES), F32),
        ((wide, hidden), F32),
        ((wide, hidden), F32),
        ((wide, hidden), F32),
        ((wide, hidden), F32),
        ((wide, hidden), F32),
        ((frames, hidden), BF16),
        ((frames, hidden), BF16),
        ((frames, 8 * LANES), BF16),
        ((COLUMN_SUMS, 8, hidden), F32),
        ((tile_rows, LANES), F32),
        ((tile_rows, LANES), F32),
        ((tile_rows, LANES), F32),
        ((peers, tile_rows, LANES), F32),
        ((peers, tile_rows, LANES), F32),
        ((peers, tile_rows, LANES), F32),
        ((2 * inputs, hidden), F32),
        ((inputs, hidden), F32),
        ((inputs, hidden), F32),
        ((2, inputs, LANES), F32),
        ((tm_size, 16, half), F32),
        ((tm_size, 16, LANES), F32),
        ((2, 16, half), F32),
        ((2, 16, half), F32),
        ((tm_size, 16, half), F32),
        ((2, 2, half), F32),
        ((devices, 2, half), F32),
        ((2 * inputs, half), F32),
        ((16, half), F32),
        ((1, LANES), F32),
        ((24, LANES), F32),
        ((2, PIECES // 2, 24, LANES), F32),
        ((2, PIECES // 2, 1, LANES), F32),
    ]
    state = [
        expand,
        expand_moment,
        expand_square,
        depthwise,
        depth_moment,
        depth_square,
        project,
        project_moment,
        project_square,
        channel_vectors,
        vector_moment,
        vector_square,
        output_biases,
        bias_moment,
        bias_square,
    ]
    state = in_hbm(state)
    slopes = in_hbm([prelu_slopes, slope_moment, slope_square])
    arrays = in_hbm([item_lengths, frames_in, out_cotangent, skip_cotangent])
    kept = pl.pallas_call(
        functools.partial(block_kernel, tm_size, items, item_pad),
        out_shape=[
            shape((frames, inputs), BF16),
            shape((frames, inputs), BF16),
            shape((frames, inputs), F32),
            shape((inputs, half), F32),
            shape((2, half, inputs), F32),
            shape((16, half), F32),
        ]
        + [shape(v.shape, F32) for v in state],
        in_specs=[hbm] * 20,
        out_specs=[vmem] * 21,
        scratch_shapes=[pltpu.SMEM((items,), jnp.int32), pltpu.SMEM((2,), F32)]
        + [pltpu.VMEM(s, t) for s, t in scratch]
        + [
            pltpu.SemaphoreType.DMA((25,)),
            pltpu.SemaphoreType.DMA((24,)),
            pltpu.SemaphoreType.DMA((24,)),
            pltpu.SemaphoreType.DMA((3, peers)),
            pltpu.SemaphoreType.DMA((3, peers)),
        ],
        compiler_params=pltpu.CompilerParams(
            collective_id=0, has_side_effects=True, vmem_limit_bytes=48 * 2**20
        ),
        name="temporal_block",
    )(arrays[0], slopes[0], *arrays[1:], *state)
    results = pl.pallas_call(
        adam_kernel,
        out_shape=[
            shape((frames, inputs), BF16),
            shape((frames, inputs), BF16),
            shape((frames, inputs), F32),
            shape((1, 1), F32),
        ]
        + [shape(v.shape, F32) for v in state + slopes],
        in_specs=[anywhere] * 3 + [vmem] * 18 + [hbm] * 3,
        out_specs=[anywhere] * 3 + [smem] + [vmem] * 15 + [smem] * 3,
        scratch_shapes=[pltpu.SMEM((2,), F32)] * 3 + [pltpu.SemaphoreType.DMA((6,))],
        compiler_params=pltpu.CompilerParams(vmem_limit_bytes=8 * 2**20),
        name="adam_step",
    )(*kept, *slopes)
    results = list(results)
    results[3] = results[3].reshape(())
    return tuple(results)


def solution(mesh):
    frames = P(("tm", "chan"), None)
    columns = P(None, "chan")
    rows = P(None, "chan", None)
    in_specs = (
        (frames, P(), frames, frames)
        + (columns,) * 3
        + (columns,) * 3
        + (rows,) * 3
        + (columns,) * 3
        + (P(),) * 6
    )
    out_specs = (
        (frames, frames, frames, P())
        + (columns,) * 3
        + (columns,) * 3
        + (rows,) * 3
        + (columns,) * 3
        + (P(),) * 6
    )
    return jax.shard_map(
        functools.partial(per_device, mesh.shape["tm"]),
        mesh=mesh,
        in_specs=in_specs,
        out_specs=out_specs,
        check_vma=False,
    )
```

```python
import functools

import jax
import jax.numpy as jnp
from jax import lax
from jax.experimental import pallas as pl
from jax.experimental.pallas import tpu as pltpu
from jax.sharding import PartitionSpec as P

F32 = jnp.float32
BF16 = jnp.bfloat16
MESH = pl.DeviceIdType.MESH

DILATION = 16
HALO = 2 * DILATION
LONGEST_ITEM = 8192
LANES = 128
ROWS = 64
BLOCK = 512
PIECES = 16

norm_eps = 1e-06
clip_level = 5.0
rate = 0.05
small_rate = 0.5
beta_first = 0.9
beta_second = 0.999
adam_eps = 1e-08
decay = 0.01
step_count = 10.0

TAP_ROW = 6
BIAS_ROW = 9
SLOPE_TWO_ROW = 10
SLOPE_ONE_ROW = 11
SQUARES_ROW = 12

(GAIN_TWO, SHIFT_TWO, TAP_A, TAP_B, TAP_C, DEPTH_BIAS, GAIN_ONE, SHIFT_ONE, SLOPE_TWO, SLOPE_ONE, COLUMN_SUMS) = range(11)


def dot(a, b):
    return lax.dot_general(a, b, (((1,), (0,)), ((), ())), preferred_element_type=F32)


def dot_rows(a, b):
    return lax.dot_general(a, b, (((1,), (1,)), ((), ())), preferred_element_type=F32)


def dot_frames(a, b):
    return lax.dot_general(a, b, (((0,), (0,)), ((), ())), preferred_element_type=F32)


def rounded(v):
    return v.astype(BF16).astype(F32)


def spread_lanes(v):
    return jnp.broadcast_to(jnp.sum(v, axis=1, keepdims=True), (v.shape[0], LANES))


def in_hbm(arrays):
    return [pltpu.with_memory_space_constraint(v, pltpu.HBM) for v in arrays]


def spots_of(item_pad):
    names = ("sum", "spread", "mean", "crossed")
    if 4 * item_pad <= LANES:
        return 2, {**{n: (0, k * item_pad) for k, n in enumerate(names)}, "q": (1, 2 * item_pad)}
    return 5, {n: (k, 0) for k, n in enumerate(names + ("q",))}


def fold_rows(v):
    return jnp.sum(v.reshape(v.shape[0] // 8, 8, v.shape[1]), axis=0)


def block_kernel(
    tm_size,
    item_count,
    item_pad,
    len_hbm,
    slope_hbm,
    frames_hbm,
    out_cot_hbm,
    skip_cot_hbm,
    *refs,
):
    state_hbm, refs = refs[:15], refs[15:]
    block_out, skip_out, input_out, expand_grad_ref, project_grad_ref, small_grad_ref = refs[:6]
    state_refs, refs = refs[6:21], refs[21:]
    expand_ref, taps_ref, project_ref, vectors_ref, biases_ref = state_refs[::3]
    (
    len_ref,
    slope_ref,
    x,
    cots,
    w_expand,
    w_project,
    params,
    item_rows,
    item_cols,
    mask_low,
    mask_high,
    table,
    counts,
    act_one,
    xhat_one,
    normed,
    mixed_grad,
    act_two,
    mixed,
    hidden_grad,
    seg,
    column,
    tile_one,
    tile_two,
    tile_three,
    stats_one,
    stats_two,
    stats_three,
    project_part,
    expand_part,
    project_pair,
    expand_pair,
    project_in,
    expand_in,
    small_part,
    small_pair,
    small_in,
    late_part,
    late_in,
    project_sum,
    small_sum,
    square_part,
    extra,
    last_part,
    last_in,
    tail_in,
    local_sem,
    send_sem,
    recv_sem,
    near_send,
    near_recv,
    ) = refs
    frames = block_out.shape[0]
    wide = x.shape[0]
    half = expand_ref.shape[1]
    hidden = 2 * half
    blocks = hidden // LANES
    devices = 2 * tm_size
    stride = tm_size // PIECES
    spans = -(-LONGEST_ITEM // frames)
    chan = lax.axis_index("chan")
    tm = lax.axis_index("tm")
    me = tm * 2 + chan
    other = 1 - chan

    def device(index):
        return {"chan": lax.rem(index, 2), "tm": lax.div(index, 2)}

    def remote(src, dst, phase, target):
        return pltpu.make_async_remote_copy(
            src_ref=src,
            dst_ref=dst,
            send_sem=send_sem.at[phase],
            recv_sem=recv_sem.at[phase],
            device_id=target,
            device_id_type=MESH,
        )

    def wait_bytes(ref, sem):
        pltpu.make_async_copy(ref, ref, sem).wait()

    pending = {}

    def settle(*keys):
        for key in keys:
            pending.pop(key)()

    def started(copy, name, sends=None, receives=None):
        def maybe(condition, body):
            if condition is None:
                body()
            else:
                pl.when(condition)(body)

        maybe(sends, copy.start)
        pending[name, "sent"] = lambda: maybe(sends, copy.wait_send)
        pending[name, "here"] = lambda: maybe(receives, copy.wait_recv)

    own = pl.ds(HALO, frames)
    loads = {
        "expand": (state_hbm[0], expand_ref),
        "frames": (frames_hbm, x.at[own, :]),
        "vectors": (state_hbm[9], vectors_ref),
        "taps": (state_hbm[3], taps_ref),
        "lengths": (len_hbm, len_ref),
        "slopes": (slope_hbm, slope_ref),
        "project": (state_hbm[6], project_ref),
        "out": (out_cot_hbm, cots.at[own, pl.ds(0, LANES)]),
        "skip": (skip_cot_hbm, cots.at[own, pl.ds(LANES, LANES)]),
        "biases": (state_hbm[12], biases_ref),
    }
    def load_some(first, last):
        for k, (name, (src, dst)) in list(enumerate(loads.items()))[first:last]:
            load = pltpu.make_async_copy(src, dst, local_sem.at[k])
            load.start()
            pending["load", name] = load.wait

    load_some(0, 2)

    def loaded(*names):
        settle(*[("load", name) for name in names])

    for r in (0, HALO + frames):
        x[r : r + HALO, :] = jnp.zeros((HALO, x.shape[1]), BF16)
    for r in (HALO - DILATION, HALO + frames):
        cots[r : r + DILATION, :] = jnp.zeros((DILATION, cots.shape[1]), BF16)
    for stats in (stats_one, stats_two, stats_three):
        stats[...] = jnp.zeros_like(stats)

    barrier = pltpu.get_barrier_semaphore()

    def wrapped(v, size):
        return jnp.where(v >= size, v - size, v)

    def greet(k, carry):
        t = wrapped(tm + k, tm_size)
        for c in range(2):
            pl.semaphore_signal(
                barrier, inc=1, device_id={"chan": c, "tm": t}, device_id_type=MESH
            )
        return carry

    pl.semaphore_signal(barrier, inc=1, device_id={"chan": other, "tm": tm}, device_id_type=MESH)
    if tm_size <= 16:
        for k in range(1, tm_size):
            greet(k, 0)
    else:
        lax.fori_loop(1, tm_size, greet, 0)

    load_some(2, len(loads))

    my_half = pl.ds(pl.multiple_of(chan * half, half), half)
    loaded("expand")
    w_expand[:, my_half] = expand_ref[...].astype(BF16)
    pl.semaphore_wait(barrier, devices - 1)

    partner = device(tm * 2 + other)
    left, right = device(me - 1), device(me + 1)
    has_left, has_right = me > 0, me < devices - 1

    def to_left(ref, count, name):
        copy = remote(
            ref.at[pl.ds(HALO, count), :], ref.at[pl.ds(HALO + frames, count), :], name, left
        )
        started(copy, name, has_left, has_right)

    def to_right(ref, count, name):
        copy = remote(
            ref.at[pl.ds(HALO + frames - count, count), :],
            ref.at[pl.ds(HALO - count, count), :],
            name,
            right,
        )
        started(copy, name, has_right, has_left)

    started(remote(w_expand.at[:, my_half], w_expand.at[:, my_half], 0, partner), 0)
    loaded("vectors", "taps")
    params[0:6, my_half] = vectors_ref[...]
    params[6:9, my_half] = taps_ref[...]
    params[9:12, my_half] = vectors_ref[1:2, :] * taps_ref[...]
    params[12:16, my_half] = jnp.zeros((4, half), F32)
    started(remote(params.at[:, my_half], params.at[:, my_half], 1, partner), 1)
    loaded("frames")
    to_left(x, HALO, 2)
    to_right(x, HALO, 3)
    loaded("project", "out", "skip")
    w_project[my_half, 0:LANES] = project_ref[0].astype(BF16)
    w_project[my_half, LANES : 2 * LANES] = project_ref[1].astype(BF16)
    started(remote(w_project.at[my_half, :], w_project.at[my_half, :], 4, partner), 4)
    to_left(cots, DILATION, 5)
    to_right(cots, DILATION, 6)
    loaded("lengths", "slopes", "biases")
    moments = [k for k in range(15) if k % 3]
    for k in moments:
        load = pltpu.make_async_copy(state_hbm[k], state_refs[k], local_sem.at[10 + k])
        load.start()
        pending["load", k] = load.wait

    width = table.shape[0]
    lane = lax.broadcasted_iota(jnp.int32, (8, width), 1)
    lane_item = lax.rem(lane, item_pad)
    row_item = lax.broadcasted_iota(jnp.int32, (item_pad, LANES), 0)

    def bounds(j, carry):
        lane_start, lane_end, row_start, row_end = carry
        length = len_ref[j]
        return (
            lane_start + jnp.where(lane_item > j, length, 0),
            lane_end + jnp.where(lane_item >= j, length, 0),
            row_start + jnp.where(row_item > j, length, 0),
            row_end + jnp.where(row_item >= j, length, 0),
        )

    lane_zero, row_zero = jnp.zeros_like(lane), jnp.zeros_like(row_item)
    lane_start, lane_end, row_start, row_end = lax.fori_loop(
        0, item_count, bounds, (lane_zero, lane_zero, row_zero, row_zero)
    )
    lane_end = jnp.where(lane < 3 * item_pad, lane_end, lane_start)
    first = me * frames
    lane_start_row, lane_end_row = lane_start[0:1], lane_end[0:1]
    elements = jnp.maximum((row_end - row_start).astype(F32) * hidden, 1.0)

    def count_of(index):
        low = jnp.maximum(row_start, index * frames)
        high = jnp.minimum(row_end, (index + 1) * frames)
        return jnp.maximum(high - low, 0).astype(F32) * hidden

    my_count = count_of(me)
    my_safe = jnp.maximum(my_count, 1.0)
    offsets = [sign * o for o in range(spans, 0, -1) for sign in (1, -1)]
    spots = spots_of(item_pad)[1]
    tile_lane = lax.broadcasted_iota(jnp.int32, (item_pad, LANES), 1)

    def packed(v, name):
        chosen = tile_lane == spots[name][1] + row_item
        return jnp.sum(jnp.where(chosen, v, 0.0), axis=0, keepdims=True)

    def unpacked(row, name):
        chosen = tile_lane == spots[name][1] + row_item
        return spread_lanes(jnp.where(chosen, jnp.broadcast_to(row, chosen.shape), 0.0))

    counts[len(offsets)] = packed(my_count, "mean")
    for slot, offset in enumerate(offsets):
        counts[slot] = packed(count_of(me - offset), "mean")
    column[...] = jnp.zeros_like(column)

    def put_table(place, v):
        high = v.astype(BF16)
        rest = v - high.astype(F32)
        middle = rest.astype(BF16)
        low = (rest - middle.astype(F32)).astype(BF16)
        where = slice(place * LANES, (place + 1) * LANES)
        table[0:item_pad, where] = high
        table[item_pad : 2 * item_pad, where] = middle
        table[2 * item_pad : 3 * item_pad, where] = low

    def rows_of(r, n, count):
        return dot(item_rows[pl.ds(r, n), :], table[:, 0 : count * LANES])

    def part(values, k, n, b):
        return values[k : k + n, b * LANES : (b + 1) * LANES]

    def put_seg(r, n, place, v, exact=True):
        high = v.astype(BF16)
        seg[pl.ds(r, n), pl.ds(place * LANES, LANES)] = high
        if exact:
            low = (v - high.astype(F32)).astype(BF16)
            seg[pl.ds(r, n), pl.ds((place + 1) * LANES, LANES)] = low

    def item_sums(first, widths):
        sums = dot(item_cols[...], seg[:, first * LANES : (first + sum(widths)) * LANES])
        results, k = [], 0
        for n in widths:
            v = sums[:, k * LANES : (k + 1) * LANES]
            if n == 2:
                v = v + sums[:, (k + 1) * LANES : (k + 2) * LANES]
            results.append(spread_lanes(v))
            k += n
        return results

    def loop(start, size, count, body, rep=1):
        def step(i, carry):
            i = i if rep == 1 else lax.rem(i, count)
            body(pl.multiple_of(start + i * size, 16))
            return carry

        lax.fori_loop(0, count * rep, step, 0)

    def at(r, k, shift=0):
        return pl.multiple_of(r + (k - shift), 16)

    table[...] = jnp.zeros_like(table)
    put_table(0, row_start.astype(F32))
    put_table(1, row_end.astype(F32))

    wide_block = wide // 4
    wide_rows = wide_block // 11

    @functools.partial(loop, 0, wide_block, 4)
    def _(r):
        for k in range(0, wide_block, wide_rows):
            position = first - HALO + r + k + lax.broadcasted_iota(jnp.int32, (wide_rows, width), 0)
            inside = (position >= lane_start_row) & (position < lane_end_row)
            item_rows[pl.ds(at(r, k), wide_rows), :] = inside.astype(F32).astype(BF16)
        ends = rows_of(r, wide_block, 2)
        for k in range(0, wide_block, wide_rows):
            here = first - HALO + r + k + lax.broadcasted_iota(jnp.int32, (wide_rows, LANES), 0)
            here = here.astype(F32)
            after = here - part(ends, k, wide_rows, 0)
            before = part(ends, k, wide_rows, 1) - here
            mask_low[pl.ds(at(r, k), wide_rows), :] = (after >= DILATION).astype(F32)
            mask_high[pl.ds(at(r, k), wide_rows), :] = (before > DILATION).astype(F32)

    for i in range(frames // LANES):
        position = first + i * LANES + lax.broadcasted_iota(jnp.int32, (item_pad, LANES), 1)
        inside = (position >= row_start) & (position < row_end)
        item_cols[:, i * LANES : (i + 1) * LANES] = inside.astype(F32).astype(BF16)

    slope_one, slope_two = slope_ref[0], slope_ref[1]

    def lanes_of(which, b):
        return pl.ds(pl.multiple_of(which * half + b * LANES, LANES), LANES)

    def half_of(which):
        return pl.ds(pl.multiple_of(which * half, half), half)

    def activate(product, k, n, which, b):
        v = part(product, k, n, b) + params[0:1, lanes_of(which, b)]
        return jnp.maximum(v, slope_one * v)

    own_loop = functools.partial(functools.partial, loop, HALO, BLOCK, frames // BLOCK)

    @own_loop()
    def _(r):
        product = dot(x[pl.ds(r, BLOCK), :], w_expand[:, half_of(chan)])
        for k in range(0, BLOCK, ROWS):
            total = jnp.zeros((ROWS, LANES), F32)
            for b in range(blocks // 2):
                a = activate(product, k, ROWS, chan, b)
                act_one[pl.ds(at(r, k), ROWS), lanes_of(chan, b)] = a
                total = total + a
            put_seg(at(r, k, HALO), ROWS, 0, total)

    (total,) = item_sums(0, (2,))
    shift = total / jnp.maximum(my_count * 0.5, 1.0)
    put_table(0, shift)
    settle(*[(k, "here") for k in range(4)])

    @own_loop()
    def _(r):
        centres = rows_of(r, BLOCK, 1)
        product = dot(x[pl.ds(r, BLOCK), :], w_expand[:, half_of(other)])
        for k in range(0, BLOCK, ROWS):
            rows = pl.ds(at(r, k), ROWS)
            centre = part(centres, k, ROWS, 0)
            total = jnp.zeros((ROWS, LANES), F32)
            squares = jnp.zeros((ROWS, LANES), F32)
            for b in range(blocks // 2):
                d = act_one[rows, lanes_of(chan, b)] - centre
                total = total + d
                squares = squares + d * d
                a = activate(product, k, ROWS, other, b)
                act_one[rows, lanes_of(other, b)] = a
                d = a - centre
                total = total + d
                squares = squares + d * d
            put_seg(at(r, k, HALO), ROWS, 0, total)
            put_seg(at(r, k, HALO), ROWS, 2, squares)

    def pack_tile(tile, values):
        for r in range(tile.shape[0]):
            row = jnp.zeros((1, LANES), F32)
            for name, v in values.items():
                if spots[name][0] == r:
                    row = row + packed(v, name)
            tile[r : r + 1, :] = row

    def local_moments(shift, total, squares):
        mean = shift + total / my_safe
        spread = jnp.maximum(squares - total * total / my_safe, 0.0)
        return mean, spread

    def exchange(tile, stats, phase):
        def near(slot, offset):
            return pltpu.make_async_remote_copy(
                src_ref=tile,
                dst_ref=stats.at[slot],
                send_sem=near_send.at[phase, slot],
                recv_sem=near_recv.at[phase, slot],
                device_id=device(me + offset),
                device_id_type=MESH,
            )

        def all_near(source, act):
            for slot, offset in enumerate(offsets):
                index = me - offset if source else me + offset
                pl.when((index >= 0) & (index < devices))(lambda: act(near(slot, offset)))

        all_near(False, lambda copy: copy.start())
        pending["near", phase, "sent"] = lambda: all_near(False, lambda copy: copy.wait_send())
        pending["near", phase, "here"] = lambda: all_near(True, lambda copy: copy.wait_recv())

    def rows_with(name, tile, stats):
        r = spots[name][0]
        return [stats[slot, r : r + 1, :] for slot in range(len(offsets))] + [tile[r : r + 1, :]]

    def sum_of(name, tile, stats):
        total = None
        for row in rows_with(name, tile, stats):
            total = row if total is None else total + row
        return unpacked(total, name)

    def combined(tile, stats):
        mean = sum_of("sum", tile, stats) / elements
        centre = packed(mean, "mean")
        between = jnp.zeros((1, LANES), F32)
        for k, row in enumerate(rows_with("mean", tile, stats)):
            between = between + counts[k] * (row - centre) * (row - centre)
        spread = (sum_of("spread", tile, stats) + unpacked(between, "mean")) / elements
        return mean, centre, lax.rsqrt(spread + norm_eps)

    total, squares = item_sums(0, (2, 2))
    mean, spread = local_moments(shift, total, squares)
    pack_tile(tile_one, {"sum": mean * my_count, "spread": spread, "mean": mean})
    exchange(tile_one, stats_one, 0)

    for r in (0, HALO + frames):
        for which in (chan, other):
            product = dot(x[pl.ds(r, HALO), :], w_expand[:, half_of(which)])
            for b in range(blocks // 2):
                act_one[pl.ds(r, HALO), lanes_of(which, b)] = activate(product, 0, HALO, which, b)

    settle(*[(k, "here") for k in (4, 5, 6)])

    def lanes(b):
        return pl.ds(b * LANES, LANES)

    def mixed_rows(r, n, size, add):
        product = dot_rows(cots[pl.ds(r, n), :], w_project[...])
        for k in range(0, n, size):
            total = jnp.zeros((size, LANES), F32)
            for b in range(blocks):
                q = params[4:5, lanes(b)] * part(product, k, size, b)
                mixed_grad[pl.ds(at(r, k), size), lanes(b)] = q
                if add:
                    total = total + q
                    column[SHIFT_TWO, :, lanes(b)] += fold_rows(q)
            if add:
                put_seg(at(r, k, HALO), size, 4, total)

    @own_loop()
    def _(r):
        mixed_rows(r, BLOCK, ROWS, True)

    for r in (HALO - DILATION, HALO + frames):
        mixed_rows(r, DILATION, DILATION, False)
    bias_sum = dot(jnp.ones((16, frames), BF16), cots[own, :])[0:1]
    (q_sum,) = item_sums(4, (2,))

    settle(("near", 0, "here"))
    mean_one, _, scale_one = combined(tile_one, stats_one)
    put_table(0, mean_one)
    put_table(1, scale_one)

    @functools.partial(loop, 0, wide_block, 4)
    def _(r):
        values = rows_of(r, wide_block, 2)
        for k in range(0, wide_block, wide_rows):
            rows = pl.ds(at(r, k), wide_rows)
            mean, scale = part(values, k, wide_rows, 0), part(values, k, wide_rows, 1)
            for b in range(blocks):
                xhat = (act_one[rows, lanes(b)] - mean) * scale
                xhat_one[rows, lanes(b)] = xhat
                normed[rows, lanes(b)] = rounded(
                    params[1:2, lanes(b)] * xhat + params[2:3, lanes(b)]
                )

    def depth_rows(r, n, b):
        low, high = mask_low[pl.ds(r, n), :], mask_high[pl.ds(r, n), :]
        v = (
            params[3:4, lanes(b)]
            + params[6:7, lanes(b)] * (low * normed[pl.ds(r - DILATION, n), lanes(b)])
            + params[7:8, lanes(b)] * normed[pl.ds(r, n), lanes(b)]
            + params[8:9, lanes(b)] * (high * normed[pl.ds(r + DILATION, n), lanes(b)])
        )
        return jnp.maximum(v, slope_two * v)

    @own_loop()
    def _(r):
        for k in range(0, BLOCK, ROWS):
            a = depth_rows(at(r, k), ROWS, 0)
            act_two[pl.ds(at(r, k), ROWS), lanes(0)] = a
            put_seg(at(r, k, HALO), ROWS, 0, a)

    (total,) = item_sums(0, (2,))
    shift = total / jnp.maximum(my_count * (1.0 / blocks), 1.0)
    put_table(0, shift)

    @own_loop()
    def _(r):
        centres = rows_of(r, BLOCK, 1)
        for k in range(0, BLOCK, ROWS):
            rows = pl.ds(at(r, k), ROWS)
            centre = part(centres, k, ROWS, 0)
            total = jnp.zeros((ROWS, LANES), F32)
            squares = jnp.zeros((ROWS, LANES), F32)
            crossed = jnp.zeros((ROWS, LANES), F32)
            for b in range(blocks):
                if b == 0:
                    a = act_two[rows, lanes(b)]
                else:
                    a = depth_rows(at(r, k), ROWS, b)
                    act_two[rows, lanes(b)] = a
                d = a - centre
                total = total + d
                squares = squares + d * d
                crossed = crossed + mixed_grad[rows, lanes(b)] * d
            put_seg(at(r, k, HALO), ROWS, 0, total)
            put_seg(at(r, k, HALO), ROWS, 2, squares, exact=False)
            put_seg(at(r, k, HALO), ROWS, 3, crossed, exact=False)

    total, squares, crossed = item_sums(0, (2, 1, 1))
    mean, spread = local_moments(shift, total, squares)
    crossed = crossed - (mean - shift) * q_sum
    values = {"sum": mean * my_count, "spread": spread, "mean": mean, "crossed": crossed, "q": q_sum}
    pack_tile(tile_two, values)
    exchange(tile_two, stats_two, 1)

    for r in (HALO - DILATION, HALO + frames):
        for b in range(blocks):
            act_two[pl.ds(r, DILATION), lanes(b)] = depth_rows(r, DILATION, b)

    settle(("near", 1, "here"))
    mean_two, centre, scale_two = combined(tile_two, stats_two)
    between = jnp.zeros((1, LANES), F32)
    for row, q_row in zip(rows_with("mean", tile_two, stats_two), rows_with("q", tile_two, stats_two)):
        between = between + (row - centre) * q_row
    cross_sum = sum_of("crossed", tile_two, stats_two) + unpacked(between, "mean")
    put_table(0, mean_two)
    put_table(1, scale_two)
    put_table(2, scale_two * sum_of("q", tile_two, stats_two) / elements)
    put_table(3, scale_two * scale_two * cross_sum / elements)

    def second_back(r, n, size, add):
        values = rows_of(r, n, 4)
        for k in range(0, n, size):
            rows = pl.ds(at(r, k), size)
            mean, scale, q_mean, cross_mean = [part(values, k, size, j) for j in range(4)]
            for b in range(blocks):
                a = act_two[rows, lanes(b)]
                q = mixed_grad[rows, lanes(b)]
                xhat = (a - mean) * scale
                g = q * scale - q_mean - xhat * cross_mean
                act_two[rows, lanes(b)] = rounded(g * jnp.where(a > 0, 1.0, slope_two))
                if add:
                    mixed[pl.ds(at(r, k, HALO), size), lanes(b)] = (
                        params[4:5, lanes(b)] * xhat + params[5:6, lanes(b)]
                    ).astype(BF16)
                    column[GAIN_TWO, :, lanes(b)] += fold_rows(q * xhat)
                    column[SLOPE_TWO, :, lanes(b)] += fold_rows(g * jnp.minimum(a, 0.0))

    @own_loop()
    def _(r):
        second_back(r, BLOCK, ROWS, True)

    chips = tm_size // 2
    chip = lax.div(tm, 2)
    mates = 2 * chips
    mate = chip * 2 + chan
    spot = lax.div(chip, stride)
    is_reducer = lax.rem(chip, stride) == 0

    def when_reducer(body):
        if stride == 1:
            body()
        else:
            pl.when(is_reducer)(body)

    def by_role(body, count):
        if stride == 1:
            body(count - 1)
        else:
            pl.when(is_reducer)(lambda: body(count - 1))
            pl.when(jnp.logical_not(is_reducer))(lambda: body(count))

    spots_here = PIECES // 2

    def send_pieces(source, ref, phase, c):
        for k in range(spots_here):
            at_spot = wrapped(spot + k, spots_here)
            target = {"chan": c, "tm": at_spot * (2 * stride) + core}
            copy = remote(source(c, at_spot), ref.at[mate], phase, target)
            if k == 0:
                pl.when(jnp.logical_not(is_reducer & (chan == c)))(copy.start)
            else:
                copy.start()

    def pieces_pending(ref, phase):
        pending[phase, "sent"] = lambda: by_role(
            lambda n: wait_bytes(ref.at[pl.ds(0, n)], send_sem.at[phase]), PIECES
        )
        pending[phase, "here"] = lambda: when_reducer(
            lambda: wait_bytes(ref.at[pl.ds(0, mates - 1)], recv_sem.at[phase])
        )

    def piece_rows(at_spot):
        return pl.ds(pl.multiple_of(at_spot * 16, 16), 16)

    def project_piece(c, at_spot):
        return project_pair.at[piece_rows(at_spot), pl.ds(pl.multiple_of(c * half, half), half)]

    def expand_piece(c, at_spot):
        return expand_pair.at[c, piece_rows(at_spot), :]

    def total_of(ref, count, rows, cols):
        if count <= 32:
            total = ref[0]
            for k in range(1, count):
                total = total + ref[k]
            return total
        return lax.fori_loop(
            0, count, lambda k, total: total + ref[k], jnp.zeros((rows, cols), F32)
        )

    def fold_lanes(v):
        return v[:, 0:LANES] + v[:, LANES:half]

    def to_group(src, dst, phase, targets):
        def one(k, carry):
            if targets == chips:
                t = wrapped(chip + k, chips) * 2 + core
            else:
                t = wrapped(tm + k, tm_size)
            remote(src, dst, phase, {"chan": chan, "tm": t}).start()
            return carry

        if targets <= 16:
            for k in range(1, targets):
                one(k, 0)
        else:
            lax.fori_loop(1, targets, one, 0)

    def group_sent(ref, phase, targets):
        def one(k, carry):
            wait_bytes(ref, send_sem.at[phase])
            return carry

        lax.fori_loop(1, targets, one, 0)

    step = 512
    total = jnp.zeros((2 * LANES, hidden), F32)
    for k in range(frames // step):
        total = total + dot_frames(
            cots[pl.ds(HALO + k * step, step), :], mixed[pl.ds(k * step, step), :]
        )
    project_part[...] = total

    core = lax.rem(tm, 2)
    sibling = {"chan": chan, "tm": tm + 1 - 2 * core}
    mine = pl.ds(pl.multiple_of(core * LANES, LANES), LANES)
    yours = pl.ds(pl.multiple_of((1 - core) * LANES, LANES), LANES)
    started(remote(project_part.at[yours, :], project_pair, 7, sibling), 7)

    for r in (HALO - DILATION, HALO + frames):
        second_back(r, DILATION, DILATION, False)

    settle((7, "here"))
    project_pair[...] += project_part[mine, :]
    for c in range(2):
        send_pieces(project_piece, project_in, 11, c)
    pieces_pending(project_in, 11)

    @functools.partial(loop, HALO, 2 * ROWS, frames // (2 * ROWS))
    def _(r):
        for k in range(0, 2 * ROWS, ROWS):
            rows = pl.ds(at(r, k), ROWS)
            low, high = mask_low[rows, :], mask_high[rows, :]
            total = jnp.zeros((ROWS, LANES), F32)
            crossed = jnp.zeros((ROWS, LANES), F32)
            for b in range(blocks):
                later = high * act_two[pl.ds(at(r, k + DILATION), ROWS), lanes(b)]
                here = act_two[rows, lanes(b)]
                earlier = low * act_two[pl.ds(at(r, k - DILATION), ROWS), lanes(b)]
                n = normed[rows, lanes(b)]
                column[TAP_A, :, lanes(b)] += fold_rows(later * n)
                column[TAP_B, :, lanes(b)] += fold_rows(here * n)
                column[TAP_C, :, lanes(b)] += fold_rows(earlier * n)
                column[DEPTH_BIAS, :, lanes(b)] += fold_rows(here)
                q = (
                    params[9:10, lanes(b)] * later
                    + params[10:11, lanes(b)] * here
                    + params[11:12, lanes(b)] * earlier
                )
                mixed_grad[rows, lanes(b)] = q
                column[SHIFT_ONE, :, lanes(b)] += fold_rows(q)
                q_xhat = q * xhat_one[rows, lanes(b)]
                column[GAIN_ONE, :, lanes(b)] += fold_rows(q_xhat)
                total = total + q
                crossed = crossed + q_xhat
            put_seg(at(r, k, HALO), ROWS, 0, total)
            put_seg(at(r, k, HALO), ROWS, 2, crossed)

    total, crossed = item_sums(0, (2, 2))
    pack_tile(tile_three, {"sum": total, "crossed": crossed})
    exchange(tile_three, stats_three, 2)

    def column_sum(which):
        return jnp.sum(column[which], axis=0, keepdims=True)

    early_rows = {
        1: column_sum(GAIN_ONE) / params[1:2, :],
        2: column_sum(SHIFT_ONE) / params[1:2, :],
        3: column_sum(DEPTH_BIAS),
        4: column_sum(GAIN_TWO) / params[4:5, :],
        5: column_sum(SHIFT_TWO) / params[4:5, :],
        TAP_ROW: column_sum(TAP_A),
        TAP_ROW + 1: column_sum(TAP_B),
        TAP_ROW + 2: column_sum(TAP_C),
    }
    slope_two_row = column_sum(SLOPE_TWO)
    slope_two_row = (slope_two_row[:, 0:half] + slope_two_row[:, half:hidden]) / slope_two
    for c in range(2):
        small_part[c] = jnp.zeros((16, half), F32)
        for row, v in early_rows.items():
            small_part[c, row : row + 1, :] = v[:, c * half : (c + 1) * half]
        small_part[c, BIAS_ROW : BIAS_ROW + 1, :] = bias_sum
        small_part[c, SLOPE_TWO_ROW : SLOPE_TWO_ROW + 1, :] = slope_two_row

    keeper = chips // 2 // stride * stride * 2
    is_keeper = tm == keeper

    def to_keepers(parts, ref, slot, count, phase, sends):
        def each(act):
            for c in range(2):
                copy = remote(parts.at[c], ref.at[slot], phase + c, {"chan": c, "tm": keeper})
                pl.when(sends & ((tm != keeper) | (chan != c)))(lambda: act(copy))

        each(lambda copy: copy.start())
        pending[phase, "sent"] = lambda: each(lambda copy: copy.wait_send())
        pending[phase, "here"] = lambda: [
            pl.when(is_keeper & (chan == c))(
                lambda: wait_bytes(ref.at[pl.ds(0, count - 1)], recv_sem.at[phase + c])
            )
            for c in range(2)
        ]

    pair = remote(small_part, small_pair, 10, sibling)
    started(pair, 10, core == 1, core == 0)
    @own_loop()
    def _(r):
        product = dot(mixed[pl.ds(at(r, 0, HALO), BLOCK), :], w_project[...])
        for k in range(0, BLOCK, ROWS):
            rows = pl.ds(at(r, k, HALO), ROWS)
            inputs = x[pl.ds(at(r, k), ROWS), :].astype(F32)
            block_out[rows, :] = (
                inputs + part(product, k, ROWS, 0) + biases_ref[0:1, :]
            ).astype(BF16)
            skip_out[rows, :] = (part(product, k, ROWS, 1) + biases_ref[1:2, :]).astype(BF16)

    settle((10, "here"))

    @pl.when(core == 0)
    def _():
        small_part[...] += small_pair[...]

    to_keepers(small_part, small_in, mate, mates, 12, core == 0)
    settle((11, "here"))
    sum_rows = pl.ds(pl.multiple_of(core * LANES + spot * 16, 16), 16)

    @when_reducer
    def _():
        project_in[mate] = project_piece(chan, spot)[...]
        total = total_of(project_in, mates, 16, half)
        project_sum[sum_rows, :] = total
        square_part[...] = fold_lanes(jnp.sum(total * total, axis=0, keepdims=True))
        to_group(project_sum.at[sum_rows, :], project_sum.at[sum_rows, :], 17, chips)

    pending[17, "sent"] = lambda: when_reducer(
        lambda: group_sent(project_sum.at[pl.ds(0, 16), :], 17, chips)
    )
    pending[17, "here"] = lambda: by_role(
        lambda n: wait_bytes(project_sum.at[pl.ds(0, 16 * n), :], recv_sem.at[17]), PIECES // 2
    )

    settle(("near", 2, "here"))
    put_table(0, sum_of("sum", tile_three, stats_three) / elements)
    put_table(1, sum_of("crossed", tile_three, stats_three) / elements)
    put_table(2, scale_one)


    for c in range(2):

        @own_loop()
        def _(r, c=c):
            if c == 0:
                values = rows_of(r, BLOCK, 3)
                act_two[pl.ds(r, BLOCK), 0 : 3 * LANES] = values
            for k in range(0, BLOCK, ROWS):
                rows, local = pl.ds(at(r, k), ROWS), pl.ds(at(r, k, HALO), ROWS)
                if c == 0:
                    q_mean, cross_mean, scale = [part(values, k, ROWS, j) for j in range(3)]
                else:
                    q_mean, cross_mean, scale = [act_two[rows, lanes(j)] for j in range(3)]
                for b in range(c * blocks // 2, (c + 1) * blocks // 2):
                    a = act_one[rows, lanes(b)]
                    g = mixed_grad[rows, lanes(b)] - q_mean
                    g = (g - xhat_one[rows, lanes(b)] * cross_mean) * scale
                    column[SLOPE_ONE, :, lanes(b)] += fold_rows(g * jnp.minimum(a, 0.0))
                    hidden_grad[local, lanes(b)] = (g * jnp.where(a > 0, 1.0, slope_one)).astype(
                        BF16
                    )

        total = jnp.zeros((LANES, half), F32)
        for k in range(frames // step):
            total = total + dot_frames(
                x[pl.ds(HALO + k * step, step), :],
                hidden_grad[pl.ds(k * step, step), c * half : (c + 1) * half],
            )
        expand_part[:, c * half : (c + 1) * half] = total
        source = pl.ds(pl.multiple_of(c * half + (1 - core) * LANES, LANES), LANES)
        started(remote(expand_part.at[:, source], expand_pair.at[c], 8 + c, sibling), 8 + c)

    def send_expand(c):
        settle((8 + c, "here"))
        expand_pair[c] += expand_part[
            :, pl.ds(pl.multiple_of(c * half + core * LANES, LANES), LANES)
        ]
        send_pieces(expand_piece, expand_in, 16, c)

    send_expand(0)
    bias_one = dot(jnp.ones((16, frames), BF16), hidden_grad[...])[0:1]
    slope_row = column_sum(SLOPE_ONE)
    slope_row = (slope_row[:, 0:half] + slope_row[:, half:hidden]) / slope_one
    for c in range(2):
        late_part[c, 0:1, :] = bias_one[:, c * half : (c + 1) * half]
        late_part[c, 1:2, :] = slope_row
    to_keepers(late_part, late_in, me, devices, 14, tm >= 0)
    send_expand(1)
    pieces_pending(expand_in, 16)

    settle((12, "here"))

    @pl.when(is_keeper)
    def _():
        small_in[mate] = small_part[chan]
        total = total_of(small_in, mates, 16, half)
        small_sum[...] = total
        square_part[...] += fold_lanes(
            jnp.sum((total * total)[0:BIAS_ROW], axis=0, keepdims=True)
        )
        to_group(small_sum, small_sum, 18, tm_size)

    pending[18, "sent"] = lambda: pl.when(is_keeper)(lambda: group_sent(small_sum, 18, tm_size))
    pending[18, "here"] = lambda: pl.when(jnp.logical_not(is_keeper))(
        lambda: wait_bytes(small_sum, recv_sem.at[18])
    )

    @own_loop()
    def _(r):
        product = dot_rows(hidden_grad[pl.ds(at(r, 0, HALO), BLOCK), :], w_expand[...])
        for k in range(0, BLOCK, ROWS):
            above = cots[pl.ds(at(r, k), ROWS), 0:LANES].astype(F32)
            input_out[pl.ds(at(r, k, HALO), ROWS), :] = above + part(product, k, ROWS, 0)

    extra[...] = jnp.zeros_like(extra)

    def put_extra(k, v):
        high = rounded(v)
        middle = rounded(v - high)
        for j, p in enumerate((high, middle, v - high - middle)):
            extra[3 * k + j : 3 * k + j + 1, :] = p

    settle((14, "here"))

    @pl.when(is_keeper)
    def _():
        late_in[me] = late_part[chan]
        total = total_of(late_in, devices, 2, half)
        for k in range(2):
            for j in range(2):
                put_extra(1 + 2 * k + j, total[j : j + 1, k * LANES : (k + 1) * LANES])
        squares = (total * total)[0:1]
        square_part[...] += fold_lanes(squares)

    settle((16, "here"))

    @when_reducer
    def _():
        expand_in[mate] = expand_piece(chan, spot)[...]
        total = total_of(expand_in, mates, 16, LANES)
        squares = square_part[...] + jnp.sum(total * total, axis=0, keepdims=True)
        square_part[...] = squares
        put_extra(0, squares)
        last_part[0:16, :] = total.astype(BF16)
        last_part[16:32, :] = extra[...].astype(BF16)
        slot = core * spots_here + spot
        last_in[slot] = last_part[...]
        to_group(last_part, last_in.at[slot], 19, tm_size)

        def send_tail(k, carry):
            target = {"chan": other, "tm": wrapped(tm + k, tm_size)}
            remote(square_part, tail_in.at[slot], 20, target).start()
            return carry

        if tm_size <= 16:
            for k in range(tm_size):
                send_tail(k, 0)
        else:
            lax.fori_loop(0, tm_size, send_tail, 0)

    def tails_sent():
        for _ in range(stride):
            wait_bytes(tail_in, send_sem.at[20])

    def from_reducers(n):
        wait_bytes(last_in.at[pl.ds(0, n)], recv_sem.at[19])

    pending[19, "sent"] = lambda: when_reducer(lambda: group_sent(last_part, 19, tm_size))
    pending[19, "here"] = lambda: by_role(from_reducers, PIECES)
    pending[20, "sent"] = lambda: when_reducer(tails_sent)
    pending[20, "here"] = lambda: wait_bytes(tail_in, recv_sem.at[20])

    settle((17, "here"))
    started(remote(project_sum.at[mine, :], project_sum.at[mine, :], 21, sibling), 21)
    settle((18, "here"), (21, "here"))
    for k in range(2):
        project_grad_ref[k] = project_sum[k * LANES : (k + 1) * LANES, :].T
    small_grad_ref[...] = small_sum[...]
    settle((19, "here"), (20, "here"))
    for c in range(2):
        for j in range(spots_here):
            where = slice(c * LANES, (c + 1) * LANES)
            expand_grad_ref[j * 16 : j * 16 + 16, where] = last_in[c * spots_here + j, 0:16, :].astype(F32)
    keeper_spot = keeper // 2 // stride

    def extras(c, j):
        return last_in[c * spots_here + j, 16:32, :].astype(F32)

    def get_extra(rows, k):
        return rows[3 * k : 3 * k + 1] + rows[3 * k + 1 : 3 * k + 2] + rows[3 * k + 2 : 3 * k + 3]

    late = extras(0, keeper_spot)
    for k in range(2):
        where = slice(k * LANES, (k + 1) * LANES)
        small_grad_ref[0:1, where] = get_extra(late, 1 + 2 * k)
        small_grad_ref[SLOPE_ONE_ROW : SLOPE_ONE_ROW + 1, where] = get_extra(late, 2 + 2 * k)
    own_total, other_total = None, None
    for q in range(PIECES):
        c, j = q // spots_here, q % spots_here
        mine_here, theirs = get_extra(extras(c, j), 0), tail_in[q]
        own_total = mine_here if own_total is None else own_total + mine_here
        other_total = theirs if other_total is None else other_total + theirs
    small_grad_ref[SQUARES_ROW : SQUARES_ROW + 1, 0:LANES] = own_total + other_total
    small_grad_ref[SQUARES_ROW : SQUARES_ROW + 1, LANES:half] = jnp.zeros((1, half - LANES), F32)

    settle(*list(pending))


def adam(weight, moment, square, gradient, scale, step_rate):
    clipped = gradient * scale
    moment_next = beta_first * moment + (1.0 - beta_first) * clipped
    square_next = beta_second * square + (1.0 - beta_second) * clipped * clipped
    update = (
        moment_next
        / (1.0 - beta_first**step_count)
        / (jnp.sqrt(square_next / (1.0 - beta_second**step_count)) + adam_eps)
    )
    return weight - step_rate * (update + decay * weight), moment_next, square_next


def adam_kernel(
    block_in,
    skip_in,
    input_in,
    expand_grad,
    project_grad,
    small_grad,
    *refs,
):
    state, outs, slope_refs = list(refs[:15]), refs[18:40], refs[40:43]
    sem = refs[43]
    slope_loads = [
        pltpu.make_async_copy(refs[15 + k], slope_refs[k], sem.at[3 + k]) for k in range(3)
    ]
    for load in slope_loads:
        load.start()
    state += slope_refs
    copies = [
        pltpu.make_async_copy(src, dst, sem.at[k])
        for k, (src, dst) in enumerate(
            zip((block_in, skip_in, input_in), (outs[0], outs[1], outs[2]))
        )
    ]
    for copy in copies:
        copy.start()
    biases = small_grad[BIAS_ROW : BIAS_ROW + 1, :]
    slopes = [
        jnp.sum(small_grad[row : row + 1, :], axis=1, keepdims=True)
        for row in (SLOPE_ONE_ROW, SLOPE_TWO_ROW)
    ]
    total = jnp.sum(small_grad[SQUARES_ROW : SQUARES_ROW + 1, :] + biases * biases, axis=1, keepdims=True)
    total = total + slopes[0] * slopes[0] + slopes[1] * slopes[1]
    grad_norm = jnp.sqrt(total)
    scale = jnp.minimum(1.0, clip_level / grad_norm)
    outs[3][0, 0] = grad_norm[0, 0]

    def update(k, gradient, step_rate, at=...):
        results = adam(
            state[3 * k][at], state[3 * k + 1][at], state[3 * k + 2][at], gradient, scale, step_rate
        )
        for j in range(3):
            outs[4 + 3 * k + j][at] = results[j]

    update(0, expand_grad[...], rate)
    update(1, small_grad[TAP_ROW : TAP_ROW + 3, :], small_rate)
    for k in range(2):
        update(2, project_grad[k], rate, k)
    update(3, small_grad[0:6, :], small_rate)
    lanes = biases.shape[1] // 2
    for k in range(2):
        update(4, biases[:, k * lanes : (k + 1) * lanes], small_rate, slice(k, k + 1))
    for load in slope_loads:
        load.wait()
    for k in range(2):
        results = adam(
            state[15][k], state[16][k], state[17][k], slopes[k], scale, small_rate
        )
        for j in range(3):
            outs[19 + j][k] = results[j][0, 0]
    for copy in copies:
        copy.wait()


def per_device(
    tm_size,
    frames_in,
    item_lengths,
    out_cotangent,
    skip_cotangent,
    expand,
    expand_moment,
    expand_square,
    depthwise,
    depth_moment,
    depth_square,
    project,
    project_moment,
    project_square,
    channel_vectors,
    vector_moment,
    vector_square,
    output_biases,
    bias_moment,
    bias_square,
    prelu_slopes,
    slope_moment,
    slope_square,
):
    frames, inputs = frames_in.shape
    half = expand.shape[1]
    hidden = 2 * half
    items = item_lengths.shape[0]
    item_pad = -(-items // 16) * 16
    width = -(-3 * item_pad // LANES) * LANES
    wide = frames + 2 * HALO
    devices = 2 * tm_size
    peers = 2 * (-(-LONGEST_ITEM // frames))
    tile_rows = spots_of(item_pad)[0]
    vmem, smem, anywhere, hbm = (
        pl.BlockSpec(memory_space=space)
        for space in (pltpu.VMEM, pltpu.SMEM, pl.ANY, pltpu.HBM)
    )
    shape = jax.ShapeDtypeStruct
    scratch = [
        ((wide, inputs), BF16),
        ((wide, 2 * inputs), BF16),
        ((inputs, hidden), BF16),
        ((hidden, 2 * inputs), BF16),
        ((16, hidden), F32),
        ((wide, width), BF16),
        ((item_pad, frames), BF16),
        ((wide, LANES), F32),
        ((wide, LANES), F32),
        ((width, 4 * LANES), BF16),
        ((peers + 1, 1, LANES), F32),
        ((wide, hidden), F32),
        ((wide, hidden), F32),
        ((wide, hidden), F32),
        ((wide, hidden), F32),
        ((wide, hidden), F32),
        ((frames, hidden), BF16),
        ((frames, hidden), BF16),
        ((frames, 8 * LANES), BF16),
        ((COLUMN_SUMS, 8, hidden), F32),
        ((tile_rows, LANES), F32),
        ((tile_rows, LANES), F32),
        ((tile_rows, LANES), F32),
        ((peers, tile_rows, LANES), F32),
        ((peers, tile_rows, LANES), F32),
        ((peers, tile_rows, LANES), F32),
        ((2 * inputs, hidden), F32),
        ((inputs, hidden), F32),
        ((inputs, hidden), F32),
        ((2, inputs, LANES), F32),
        ((tm_size, 16, half), F32),
        ((tm_size, 16, LANES), F32),
        ((2, 16, half), F32),
        ((2, 16, half), F32),
        ((tm_size, 16, half), F32),
        ((2, 2, half), F32),
        ((devices, 2, half), F32),
        ((2 * inputs, half), F32),
        ((16, half), F32),
        ((1, LANES), F32),
        ((16, LANES), F32),
        ((32, LANES), BF16),
        ((PIECES, 32, LANES), BF16),
        ((PIECES, 1, LANES), F32),
    ]
    state = [
        expand,
        expand_moment,
        expand_square,
        depthwise,
        depth_moment,
        depth_square,
        project,
        project_moment,
        project_square,
        channel_vectors,
        vector_moment,
        vector_square,
        output_biases,
        bias_moment,
        bias_square,
    ]
    state = in_hbm(state)
    slopes = in_hbm([prelu_slopes, slope_moment, slope_square])
    arrays = in_hbm([item_lengths, frames_in, out_cotangent, skip_cotangent])
    kept = pl.pallas_call(
        functools.partial(block_kernel, tm_size, items, item_pad),
        out_shape=[
            shape((frames, inputs), BF16),
            shape((frames, inputs), BF16),
            shape((frames, inputs), F32),
            shape((inputs, half), F32),
            shape((2, half, inputs), F32),
            shape((16, half), F32),
        ]
        + [shape(v.shape, F32) for v in state],
        in_specs=[hbm] * 20,
        out_specs=[vmem] * 21,
        scratch_shapes=[pltpu.SMEM((items,), jnp.int32), pltpu.SMEM((2,), F32)]
        + [pltpu.VMEM(s, t) for s, t in scratch]
        + [
            pltpu.SemaphoreType.DMA((25,)),
            pltpu.SemaphoreType.DMA((24,)),
            pltpu.SemaphoreType.DMA((24,)),
            pltpu.SemaphoreType.DMA((3, peers)),
            pltpu.SemaphoreType.DMA((3, peers)),
        ],
        compiler_params=pltpu.CompilerParams(
            collective_id=0, has_side_effects=True, vmem_limit_bytes=48 * 2**20
        ),
        name="temporal_block",
    )(arrays[0], slopes[0], *arrays[1:], *state)
    results = pl.pallas_call(
        adam_kernel,
        out_shape=[
            shape((frames, inputs), BF16),
            shape((frames, inputs), BF16),
            shape((frames, inputs), F32),
            shape((1, 1), F32),
        ]
        + [shape(v.shape, F32) for v in state + slopes],
        in_specs=[anywhere] * 3 + [vmem] * 18 + [hbm] * 3,
        out_specs=[anywhere] * 3 + [smem] + [vmem] * 15 + [smem] * 3,
        scratch_shapes=[pltpu.SMEM((2,), F32)] * 3 + [pltpu.SemaphoreType.DMA((6,))],
        compiler_params=pltpu.CompilerParams(vmem_limit_bytes=8 * 2**20),
        name="adam_step",
    )(*kept, *slopes)
    results = list(results)
    results[3] = results[3].reshape(())
    return tuple(results)


def solution(mesh):
    frames = P(("tm", "chan"), None)
    columns = P(None, "chan")
    rows = P(None, "chan", None)
    in_specs = (
        (frames, P(), frames, frames)
        + (columns,) * 3
        + (columns,) * 3
        + (rows,) * 3
        + (columns,) * 3
        + (P(),) * 6
    )
    out_specs = (
        (frames, frames, frames, P())
        + (columns,) * 3
        + (columns,) * 3
        + (rows,) * 3
        + (columns,) * 3
        + (P(),) * 6
    )
    return jax.shard_map(
        functools.partial(per_device, mesh.shape["tm"]),
        mesh=mesh,
        in_specs=in_specs,
        out_specs=out_specs,
        check_vma=False,
    )
```

```python
import functools

import jax
import jax.numpy as jnp
from jax import lax
from jax.experimental import pallas as pl
from jax.experimental.pallas import tpu as pltpu
from jax.sharding import PartitionSpec as P

F32 = jnp.float32
BF16 = jnp.bfloat16
MESH = pl.DeviceIdType.MESH

DILATION = 16
HALO = 2 * DILATION
LONGEST_ITEM = 8192
LANES = 128
ROWS = 32
BLOCK = 2048
PIECES = 16

norm_eps = 1e-06
clip_level = 5.0
rate = 0.05
small_rate = 0.5
beta_first = 0.9
beta_second = 0.999
adam_eps = 1e-08
decay = 0.01
step_count = 10.0

TAP_ROW = 6
BIAS_ROW = 9
SLOPE_TWO_ROW = 10
SLOPE_ONE_ROW = 11
SQUARES_ROW = 12

(GAIN_TWO, SHIFT_TWO, TAP_A, TAP_B, TAP_C, DEPTH_BIAS, GAIN_ONE, SHIFT_ONE, SLOPE_TWO, SLOPE_ONE, COLUMN_SUMS) = range(11)


def dot(a, b):
    return lax.dot_general(a, b, (((1,), (0,)), ((), ())), preferred_element_type=F32)


def dot_rows(a, b):
    return lax.dot_general(a, b, (((1,), (1,)), ((), ())), preferred_element_type=F32)


def dot_frames(a, b):
    return lax.dot_general(a, b, (((0,), (0,)), ((), ())), preferred_element_type=F32)


def rounded(v):
    return v.astype(BF16).astype(F32)


def spread_lanes(v):
    return jnp.broadcast_to(jnp.sum(v, axis=1, keepdims=True), (v.shape[0], LANES))


def in_hbm(arrays):
    return [pltpu.with_memory_space_constraint(v, pltpu.HBM) for v in arrays]


def spots_of(item_pad):
    names = ("sum", "spread", "mean", "crossed")
    if 4 * item_pad <= LANES:
        return 2, {**{n: (0, k * item_pad) for k, n in enumerate(names)}, "q": (1, 2 * item_pad)}
    return 5, {n: (k, 0) for k, n in enumerate(names + ("q",))}


def fold_rows(v):
    return jnp.sum(v.reshape(v.shape[0] // 8, 8, v.shape[1]), axis=0)


def block_kernel(
    tm_size,
    item_count,
    item_pad,
    len_hbm,
    slope_hbm,
    frames_hbm,
    out_cot_hbm,
    skip_cot_hbm,
    *refs,
):
    state_hbm, refs = refs[:15], refs[15:]
    block_out, skip_out, input_out, expand_grad_ref, project_grad_ref, small_grad_ref = refs[:6]
    state_refs, refs = refs[6:21], refs[21:]
    expand_ref, taps_ref, project_ref, vectors_ref, biases_ref = state_refs[::3]
    (
    len_ref,
    slope_ref,
    x,
    cots,
    w_expand,
    w_project,
    params,
    item_rows,
    item_cols,
    mask_low,
    mask_high,
    table,
    counts,
    act_one,
    xhat_one,
    normed,
    mixed_grad,
    act_two,
    mixed,
    hidden_grad,
    seg,
    column,
    tile_one,
    tile_two,
    tile_three,
    stats_one,
    stats_two,
    stats_three,
    project_part,
    expand_part,
    project_pair,
    expand_pair,
    project_in,
    expand_in,
    small_part,
    small_pair,
    small_in,
    late_part,
    late_in,
    project_sum,
    small_sum,
    square_part,
    extra,
    last_part,
    last_in,
    tail_in,
    local_sem,
    send_sem,
    recv_sem,
    near_send,
    near_recv,
    ) = refs
    frames = block_out.shape[0]
    wide = x.shape[0]
    half = expand_ref.shape[1]
    hidden = 2 * half
    blocks = hidden // LANES
    devices = 2 * tm_size
    stride = tm_size // PIECES
    spans = -(-LONGEST_ITEM // frames)
    chan = lax.axis_index("chan")
    tm = lax.axis_index("tm")
    me = tm * 2 + chan
    other = 1 - chan

    def device(index):
        return {"chan": lax.rem(index, 2), "tm": lax.div(index, 2)}

    def remote(src, dst, phase, target):
        return pltpu.make_async_remote_copy(
            src_ref=src,
            dst_ref=dst,
            send_sem=send_sem.at[phase],
            recv_sem=recv_sem.at[phase],
            device_id=target,
            device_id_type=MESH,
        )

    def wait_bytes(ref, sem):
        pltpu.make_async_copy(ref, ref, sem).wait()

    pending = {}

    def settle(*keys):
        for key in keys:
            pending.pop(key)()

    def started(copy, name, sends=None, receives=None):
        def maybe(condition, body):
            if condition is None:
                body()
            else:
                pl.when(condition)(body)

        maybe(sends, copy.start)
        pending[name, "sent"] = lambda: maybe(sends, copy.wait_send)
        pending[name, "here"] = lambda: maybe(receives, copy.wait_recv)

    own = pl.ds(HALO, frames)
    loads = {
        "expand": (state_hbm[0], expand_ref),
        "frames": (frames_hbm, x.at[own, :]),
        "vectors": (state_hbm[9], vectors_ref),
        "taps": (state_hbm[3], taps_ref),
        "lengths": (len_hbm, len_ref),
        "slopes": (slope_hbm, slope_ref),
        "project": (state_hbm[6], project_ref),
        "out": (out_cot_hbm, cots.at[own, pl.ds(0, LANES)]),
        "skip": (skip_cot_hbm, cots.at[own, pl.ds(LANES, LANES)]),
        "biases": (state_hbm[12], biases_ref),
    }
    def load_some(first, last):
        for k, (name, (src, dst)) in list(enumerate(loads.items()))[first:last]:
            load = pltpu.make_async_copy(src, dst, local_sem.at[k])
            load.start()
            pending["load", name] = load.wait

    load_some(0, 2)

    def loaded(*names):
        settle(*[("load", name) for name in names])

    for r in (0, HALO + frames):
        x[r : r + HALO, :] = jnp.zeros((HALO, x.shape[1]), BF16)
    for r in (HALO - DILATION, HALO + frames):
        cots[r : r + DILATION, :] = jnp.zeros((DILATION, cots.shape[1]), BF16)
    for stats in (stats_one, stats_two, stats_three):
        stats[...] = jnp.zeros_like(stats)

    barrier = pltpu.get_barrier_semaphore()

    def wrapped(v, size):
        return jnp.where(v >= size, v - size, v)

    def greet(k, carry):
        t = wrapped(tm + k, tm_size)
        for c in range(2):
            pl.semaphore_signal(
                barrier, inc=1, device_id={"chan": c, "tm": t}, device_id_type=MESH
            )
        return carry

    pl.semaphore_signal(barrier, inc=1, device_id={"chan": other, "tm": tm}, device_id_type=MESH)
    if tm_size <= 16:
        for k in range(1, tm_size):
            greet(k, 0)
    else:
        lax.fori_loop(1, tm_size, greet, 0)

    load_some(2, len(loads))

    my_half = pl.ds(pl.multiple_of(chan * half, half), half)
    loaded("expand")
    w_expand[:, my_half] = expand_ref[...].astype(BF16)
    pl.semaphore_wait(barrier, devices - 1)

    partner = device(tm * 2 + other)
    left, right = device(me - 1), device(me + 1)
    has_left, has_right = me > 0, me < devices - 1

    def to_left(ref, count, name):
        copy = remote(
            ref.at[pl.ds(HALO, count), :], ref.at[pl.ds(HALO + frames, count), :], name, left
        )
        started(copy, name, has_left, has_right)

    def to_right(ref, count, name):
        copy = remote(
            ref.at[pl.ds(HALO + frames - count, count), :],
            ref.at[pl.ds(HALO - count, count), :],
            name,
            right,
        )
        started(copy, name, has_right, has_left)

    started(remote(w_expand.at[:, my_half], w_expand.at[:, my_half], 0, partner), 0)
    loaded("vectors", "taps")
    params[0:6, my_half] = vectors_ref[...]
    params[6:9, my_half] = taps_ref[...]
    params[9:12, my_half] = vectors_ref[1:2, :] * taps_ref[...]
    params[12:16, my_half] = jnp.zeros((4, half), F32)
    started(remote(params.at[:, my_half], params.at[:, my_half], 1, partner), 1)
    loaded("frames")
    to_left(x, HALO, 2)
    to_right(x, HALO, 3)
    loaded("project", "out", "skip")
    w_project[my_half, 0:LANES] = project_ref[0].astype(BF16)
    w_project[my_half, LANES : 2 * LANES] = project_ref[1].astype(BF16)
    started(remote(w_project.at[my_half, :], w_project.at[my_half, :], 4, partner), 4)
    to_left(cots, DILATION, 5)
    to_right(cots, DILATION, 6)
    loaded("lengths", "slopes", "biases")
    moments = [k for k in range(15) if k % 3]
    for k in moments:
        load = pltpu.make_async_copy(state_hbm[k], state_refs[k], local_sem.at[10 + k])
        load.start()
        pending["load", k] = load.wait

    width = table.shape[0]
    lane = lax.broadcasted_iota(jnp.int32, (8, width), 1)
    lane_item = lax.rem(lane, item_pad)
    row_item = lax.broadcasted_iota(jnp.int32, (item_pad, LANES), 0)

    def bounds(j, carry):
        lane_start, lane_end, row_start, row_end = carry
        length = len_ref[j]
        return (
            lane_start + jnp.where(lane_item > j, length, 0),
            lane_end + jnp.where(lane_item >= j, length, 0),
            row_start + jnp.where(row_item > j, length, 0),
            row_end + jnp.where(row_item >= j, length, 0),
        )

    lane_zero, row_zero = jnp.zeros_like(lane), jnp.zeros_like(row_item)
    lane_start, lane_end, row_start, row_end = lax.fori_loop(
        0, item_count, bounds, (lane_zero, lane_zero, row_zero, row_zero)
    )
    lane_end = jnp.where(lane < 3 * item_pad, lane_end, lane_start)
    first = me * frames
    lane_start_row, lane_end_row = lane_start[0:1], lane_end[0:1]
    elements = jnp.maximum((row_end - row_start).astype(F32) * hidden, 1.0)

    def count_of(index):
        low = jnp.maximum(row_start, index * frames)
        high = jnp.minimum(row_end, (index + 1) * frames)
        return jnp.maximum(high - low, 0).astype(F32) * hidden

    my_count = count_of(me)
    my_safe = jnp.maximum(my_count, 1.0)
    offsets = [sign * o for o in range(spans, 0, -1) for sign in (1, -1)]
    spots = spots_of(item_pad)[1]
    tile_lane = lax.broadcasted_iota(jnp.int32, (item_pad, LANES), 1)

    def packed(v, name):
        chosen = tile_lane == spots[name][1] + row_item
        return jnp.sum(jnp.where(chosen, v, 0.0), axis=0, keepdims=True)

    def unpacked(row, name):
        chosen = tile_lane == spots[name][1] + row_item
        return spread_lanes(jnp.where(chosen, jnp.broadcast_to(row, chosen.shape), 0.0))

    counts[len(offsets)] = packed(my_count, "mean")
    for slot, offset in enumerate(offsets):
        counts[slot] = packed(count_of(me - offset), "mean")
    column[...] = jnp.zeros_like(column)

    def put_table(place, v):
        high = v.astype(BF16)
        rest = v - high.astype(F32)
        middle = rest.astype(BF16)
        low = (rest - middle.astype(F32)).astype(BF16)
        where = slice(place * LANES, (place + 1) * LANES)
        table[0:item_pad, where] = high
        table[item_pad : 2 * item_pad, where] = middle
        table[2 * item_pad : 3 * item_pad, where] = low

    def rows_of(r, n, count):
        return dot(item_rows[pl.ds(r, n), :], table[:, 0 : count * LANES])

    def part(values, k, n, b):
        return values[k : k + n, b * LANES : (b + 1) * LANES]

    def put_seg(r, n, place, v, exact=True):
        high = v.astype(BF16)
        seg[pl.ds(r, n), pl.ds(place * LANES, LANES)] = high
        if exact:
            low = (v - high.astype(F32)).astype(BF16)
            seg[pl.ds(r, n), pl.ds((place + 1) * LANES, LANES)] = low

    def item_sums(first, widths):
        sums = dot(item_cols[...], seg[:, first * LANES : (first + sum(widths)) * LANES])
        results, k = [], 0
        for n in widths:
            v = sums[:, k * LANES : (k + 1) * LANES]
            if n == 2:
                v = v + sums[:, (k + 1) * LANES : (k + 2) * LANES]
            results.append(spread_lanes(v))
            k += n
        return results

    def loop(start, size, count, body, rep=1):
        def step(i, carry):
            i = i if rep == 1 else lax.rem(i, count)
            body(pl.multiple_of(start + i * size, 16))
            return carry

        lax.fori_loop(0, count * rep, step, 0)

    def at(r, k, shift=0):
        return pl.multiple_of(r + (k - shift), 16)

    table[...] = jnp.zeros_like(table)
    put_table(0, row_start.astype(F32))
    put_table(1, row_end.astype(F32))

    wide_block = wide // 4
    wide_rows = wide_block // 11

    @functools.partial(loop, 0, wide_block, 4)
    def _(r):
        for k in range(0, wide_block, wide_rows):
            position = first - HALO + r + k + lax.broadcasted_iota(jnp.int32, (wide_rows, width), 0)
            inside = (position >= lane_start_row) & (position < lane_end_row)
            item_rows[pl.ds(at(r, k), wide_rows), :] = inside.astype(F32).astype(BF16)
        ends = rows_of(r, wide_block, 2)
        for k in range(0, wide_block, wide_rows):
            here = first - HALO + r + k + lax.broadcasted_iota(jnp.int32, (wide_rows, LANES), 0)
            here = here.astype(F32)
            after = here - part(ends, k, wide_rows, 0)
            before = part(ends, k, wide_rows, 1) - here
            mask_low[pl.ds(at(r, k), wide_rows), :] = (after >= DILATION).astype(F32)
            mask_high[pl.ds(at(r, k), wide_rows), :] = (before > DILATION).astype(F32)

    for i in range(frames // LANES):
        position = first + i * LANES + lax.broadcasted_iota(jnp.int32, (item_pad, LANES), 1)
        inside = (position >= row_start) & (position < row_end)
        item_cols[:, i * LANES : (i + 1) * LANES] = inside.astype(F32).astype(BF16)

    slope_one, slope_two = slope_ref[0], slope_ref[1]

    def lanes_of(which, b):
        return pl.ds(pl.multiple_of(which * half + b * LANES, LANES), LANES)

    def half_of(which):
        return pl.ds(pl.multiple_of(which * half, half), half)

    def activate(product, k, n, which, b):
        v = part(product, k, n, b) + params[0:1, lanes_of(which, b)]
        return jnp.maximum(v, slope_one * v)

    own_loop = functools.partial(functools.partial, loop, HALO, BLOCK, frames // BLOCK)

    @own_loop()
    def _(r):
        product = dot(x[pl.ds(r, BLOCK), :], w_expand[:, half_of(chan)])
        for k in range(0, BLOCK, ROWS):
            total = jnp.zeros((ROWS, LANES), F32)
            for b in range(blocks // 2):
                a = activate(product, k, ROWS, chan, b)
                act_one[pl.ds(at(r, k), ROWS), lanes_of(chan, b)] = a
                total = total + a
            put_seg(at(r, k, HALO), ROWS, 0, total)

    (total,) = item_sums(0, (2,))
    shift = total / jnp.maximum(my_count * 0.5, 1.0)
    put_table(0, shift)
    settle(*[(k, "here") for k in range(4)])

    @own_loop()
    def _(r):
        centres = rows_of(r, BLOCK, 1)
        product = dot(x[pl.ds(r, BLOCK), :], w_expand[:, half_of(other)])
        for k in range(0, BLOCK, ROWS):
            rows = pl.ds(at(r, k), ROWS)
            centre = part(centres, k, ROWS, 0)
            total = jnp.zeros((ROWS, LANES), F32)
            squares = jnp.zeros((ROWS, LANES), F32)
            for b in range(blocks // 2):
                d = act_one[rows, lanes_of(chan, b)] - centre
                total = total + d
                squares = squares + d * d
                a = activate(product, k, ROWS, other, b)
                act_one[rows, lanes_of(other, b)] = a
                d = a - centre
                total = total + d
                squares = squares + d * d
            put_seg(at(r, k, HALO), ROWS, 0, total)
            put_seg(at(r, k, HALO), ROWS, 2, squares)

    def pack_tile(tile, values):
        for r in range(tile.shape[0]):
            row = jnp.zeros((1, LANES), F32)
            for name, v in values.items():
                if spots[name][0] == r:
                    row = row + packed(v, name)
            tile[r : r + 1, :] = row

    def local_moments(shift, total, squares):
        mean = shift + total / my_safe
        spread = jnp.maximum(squares - total * total / my_safe, 0.0)
        return mean, spread

    def exchange(tile, stats, phase):
        def near(slot, offset):
            return pltpu.make_async_remote_copy(
                src_ref=tile,
                dst_ref=stats.at[slot],
                send_sem=near_send.at[phase, slot],
                recv_sem=near_recv.at[phase, slot],
                device_id=device(me + offset),
                device_id_type=MESH,
            )

        def all_near(source, act):
            for slot, offset in enumerate(offsets):
                index = me - offset if source else me + offset
                pl.when((index >= 0) & (index < devices))(lambda: act(near(slot, offset)))

        all_near(False, lambda copy: copy.start())
        pending["near", phase, "sent"] = lambda: all_near(False, lambda copy: copy.wait_send())
        pending["near", phase, "here"] = lambda: all_near(True, lambda copy: copy.wait_recv())

    def rows_with(name, tile, stats):
        r = spots[name][0]
        return [stats[slot, r : r + 1, :] for slot in range(len(offsets))] + [tile[r : r + 1, :]]

    def sum_of(name, tile, stats):
        total = None
        for row in rows_with(name, tile, stats):
            total = row if total is None else total + row
        return unpacked(total, name)

    def combined(tile, stats):
        mean = sum_of("sum", tile, stats) / elements
        centre = packed(mean, "mean")
        between = jnp.zeros((1, LANES), F32)
        for k, row in enumerate(rows_with("mean", tile, stats)):
            between = between + counts[k] * (row - centre) * (row - centre)
        spread = (sum_of("spread", tile, stats) + unpacked(between, "mean")) / elements
        return mean, centre, lax.rsqrt(spread + norm_eps)

    total, squares = item_sums(0, (2, 2))
    mean, spread = local_moments(shift, total, squares)
    pack_tile(tile_one, {"sum": mean * my_count, "spread": spread, "mean": mean})
    exchange(tile_one, stats_one, 0)

    for r in (0, HALO + frames):
        for which in (chan, other):
            product = dot(x[pl.ds(r, HALO), :], w_expand[:, half_of(which)])
            for b in range(blocks // 2):
                act_one[pl.ds(r, HALO), lanes_of(which, b)] = activate(product, 0, HALO, which, b)

    settle(*[(k, "here") for k in (4, 5, 6)])

    def lanes(b):
        return pl.ds(b * LANES, LANES)

    def mixed_rows(r, n, size, add):
        product = dot_rows(cots[pl.ds(r, n), :], w_project[...])
        for k in range(0, n, size):
            total = jnp.zeros((size, LANES), F32)
            for b in range(blocks):
                q = params[4:5, lanes(b)] * part(product, k, size, b)
                mixed_grad[pl.ds(at(r, k), size), lanes(b)] = q
                if add:
                    total = total + q
                    column[SHIFT_TWO, :, lanes(b)] += fold_rows(q)
            if add:
                put_seg(at(r, k, HALO), size, 4, total)

    @own_loop()
    def _(r):
        mixed_rows(r, BLOCK, ROWS, True)

    for r in (HALO - DILATION, HALO + frames):
        mixed_rows(r, DILATION, DILATION, False)
    bias_sum = dot(jnp.ones((16, frames), BF16), cots[own, :])[0:1]
    (q_sum,) = item_sums(4, (2,))

    settle(("near", 0, "here"))
    mean_one, _, scale_one = combined(tile_one, stats_one)
    put_table(0, mean_one)
    put_table(1, scale_one)

    @functools.partial(loop, 0, wide_block, 4)
    def _(r):
        values = rows_of(r, wide_block, 2)
        for k in range(0, wide_block, wide_rows):
            rows = pl.ds(at(r, k), wide_rows)
            mean, scale = part(values, k, wide_rows, 0), part(values, k, wide_rows, 1)
            for b in range(blocks):
                xhat = (act_one[rows, lanes(b)] - mean) * scale
                xhat_one[rows, lanes(b)] = xhat
                normed[rows, lanes(b)] = rounded(
                    params[1:2, lanes(b)] * xhat + params[2:3, lanes(b)]
                )

    def depth_rows(r, n, b):
        low, high = mask_low[pl.ds(r, n), :], mask_high[pl.ds(r, n), :]
        v = (
            params[3:4, lanes(b)]
            + params[6:7, lanes(b)] * (low * normed[pl.ds(r - DILATION, n), lanes(b)])
            + params[7:8, lanes(b)] * normed[pl.ds(r, n), lanes(b)]
            + params[8:9, lanes(b)] * (high * normed[pl.ds(r + DILATION, n), lanes(b)])
        )
        return jnp.maximum(v, slope_two * v)

    @own_loop()
    def _(r):
        for k in range(0, BLOCK, ROWS):
            a = depth_rows(at(r, k), ROWS, 0)
            act_two[pl.ds(at(r, k), ROWS), lanes(0)] = a
            put_seg(at(r, k, HALO), ROWS, 0, a)

    (total,) = item_sums(0, (2,))
    shift = total / jnp.maximum(my_count * (1.0 / blocks), 1.0)
    put_table(0, shift)

    @own_loop()
    def _(r):
        centres = rows_of(r, BLOCK, 1)
        for k in range(0, BLOCK, ROWS):
            rows = pl.ds(at(r, k), ROWS)
            centre = part(centres, k, ROWS, 0)
            total = jnp.zeros((ROWS, LANES), F32)
            squares = jnp.zeros((ROWS, LANES), F32)
            crossed = jnp.zeros((ROWS, LANES), F32)
            for b in range(blocks):
                if b == 0:
                    a = act_two[rows, lanes(b)]
                else:
                    a = depth_rows(at(r, k), ROWS, b)
                    act_two[rows, lanes(b)] = a
                d = a - centre
                total = total + d
                squares = squares + d * d
                crossed = crossed + mixed_grad[rows, lanes(b)] * d
            put_seg(at(r, k, HALO), ROWS, 0, total)
            put_seg(at(r, k, HALO), ROWS, 2, squares, exact=False)
            put_seg(at(r, k, HALO), ROWS, 3, crossed, exact=False)

    total, squares, crossed = item_sums(0, (2, 1, 1))
    mean, spread = local_moments(shift, total, squares)
    crossed = crossed - (mean - shift) * q_sum
    values = {"sum": mean * my_count, "spread": spread, "mean": mean, "crossed": crossed, "q": q_sum}
    pack_tile(tile_two, values)
    exchange(tile_two, stats_two, 1)

    for r in (HALO - DILATION, HALO + frames):
        for b in range(blocks):
            act_two[pl.ds(r, DILATION), lanes(b)] = depth_rows(r, DILATION, b)

    settle(("near", 1, "here"))
    mean_two, centre, scale_two = combined(tile_two, stats_two)
    between = jnp.zeros((1, LANES), F32)
    for row, q_row in zip(rows_with("mean", tile_two, stats_two), rows_with("q", tile_two, stats_two)):
        between = between + (row - centre) * q_row
    cross_sum = sum_of("crossed", tile_two, stats_two) + unpacked(between, "mean")
    put_table(0, mean_two)
    put_table(1, scale_two)
    put_table(2, scale_two * sum_of("q", tile_two, stats_two) / elements)
    put_table(3, scale_two * scale_two * cross_sum / elements)

    def second_back(r, n, size, add):
        values = rows_of(r, n, 4)
        for k in range(0, n, size):
            rows = pl.ds(at(r, k), size)
            mean, scale, q_mean, cross_mean = [part(values, k, size, j) for j in range(4)]
            for b in range(blocks):
                a = act_two[rows, lanes(b)]
                q = mixed_grad[rows, lanes(b)]
                xhat = (a - mean) * scale
                g = q * scale - q_mean - xhat * cross_mean
                act_two[rows, lanes(b)] = rounded(g * jnp.where(a > 0, 1.0, slope_two))
                if add:
                    mixed[pl.ds(at(r, k, HALO), size), lanes(b)] = (
                        params[4:5, lanes(b)] * xhat + params[5:6, lanes(b)]
                    ).astype(BF16)
                    column[GAIN_TWO, :, lanes(b)] += fold_rows(q * xhat)
                    column[SLOPE_TWO, :, lanes(b)] += fold_rows(g * jnp.minimum(a, 0.0))

    @own_loop()
    def _(r):
        second_back(r, BLOCK, ROWS, True)

    chips = tm_size // 2
    chip = lax.div(tm, 2)
    mates = 2 * chips
    mate = chip * 2 + chan
    spot = lax.div(chip, stride)
    is_reducer = lax.rem(chip, stride) == 0

    def when_reducer(body):
        if stride == 1:
            body()
        else:
            pl.when(is_reducer)(body)

    def by_role(body, count):
        if stride == 1:
            body(count - 1)
        else:
            pl.when(is_reducer)(lambda: body(count - 1))
            pl.when(jnp.logical_not(is_reducer))(lambda: body(count))

    spots_here = PIECES // 2

    def send_pieces(source, ref, phase, c):
        for k in range(spots_here):
            at_spot = wrapped(spot + k, spots_here)
            target = {"chan": c, "tm": at_spot * (2 * stride) + core}
            copy = remote(source(c, at_spot), ref.at[mate], phase, target)
            if k == 0:
                pl.when(jnp.logical_not(is_reducer & (chan == c)))(copy.start)
            else:
                copy.start()

    def pieces_pending(ref, phase):
        pending[phase, "sent"] = lambda: by_role(
            lambda n: wait_bytes(ref.at[pl.ds(0, n)], send_sem.at[phase]), PIECES
        )
        pending[phase, "here"] = lambda: when_reducer(
            lambda: wait_bytes(ref.at[pl.ds(0, mates - 1)], recv_sem.at[phase])
        )

    def piece_rows(at_spot):
        return pl.ds(pl.multiple_of(at_spot * 16, 16), 16)

    def project_piece(c, at_spot):
        return project_pair.at[piece_rows(at_spot), pl.ds(pl.multiple_of(c * half, half), half)]

    def expand_piece(c, at_spot):
        return expand_pair.at[c, piece_rows(at_spot), :]

    def total_of(ref, count, rows, cols):
        if count <= 32:
            total = ref[0]
            for k in range(1, count):
                total = total + ref[k]
            return total
        return lax.fori_loop(
            0, count, lambda k, total: total + ref[k], jnp.zeros((rows, cols), F32)
        )

    def fold_lanes(v):
        return v[:, 0:LANES] + v[:, LANES:half]

    def to_group(src, dst, phase, targets):
        def one(k, carry):
            if targets == chips:
                t = wrapped(chip + k, chips) * 2 + core
            else:
                t = wrapped(tm + k, tm_size)
            remote(src, dst, phase, {"chan": chan, "tm": t}).start()
            return carry

        if targets <= 16:
            for k in range(1, targets):
                one(k, 0)
        else:
            lax.fori_loop(1, targets, one, 0)

    def group_sent(ref, phase, targets):
        def one(k, carry):
            wait_bytes(ref, send_sem.at[phase])
            return carry

        lax.fori_loop(1, targets, one, 0)

    step = 512
    total = jnp.zeros((2 * LANES, hidden), F32)
    for k in range(frames // step):
        total = total + dot_frames(
            cots[pl.ds(HALO + k * step, step), :], mixed[pl.ds(k * step, step), :]
        )
    project_part[...] = total

    core = lax.rem(tm, 2)
    sibling = {"chan": chan, "tm": tm + 1 - 2 * core}
    mine = pl.ds(pl.multiple_of(core * LANES, LANES), LANES)
    yours = pl.ds(pl.multiple_of((1 - core) * LANES, LANES), LANES)
    started(remote(project_part.at[yours, :], project_pair, 7, sibling), 7)

    for r in (HALO - DILATION, HALO + frames):
        second_back(r, DILATION, DILATION, False)

    settle((7, "here"))
    project_pair[...] += project_part[mine, :]
    for c in range(2):
        send_pieces(project_piece, project_in, 11, c)
    pieces_pending(project_in, 11)

    @functools.partial(loop, HALO, 2 * ROWS, frames // (2 * ROWS))
    def _(r):
        for k in range(0, 2 * ROWS, ROWS):
            rows = pl.ds(at(r, k), ROWS)
            low, high = mask_low[rows, :], mask_high[rows, :]
            total = jnp.zeros((ROWS, LANES), F32)
            crossed = jnp.zeros((ROWS, LANES), F32)
            for b in range(blocks):
                later = high * act_two[pl.ds(at(r, k + DILATION), ROWS), lanes(b)]
                here = act_two[rows, lanes(b)]
                earlier = low * act_two[pl.ds(at(r, k - DILATION), ROWS), lanes(b)]
                n = normed[rows, lanes(b)]
                column[TAP_A, :, lanes(b)] += fold_rows(later * n)
                column[TAP_B, :, lanes(b)] += fold_rows(here * n)
                column[TAP_C, :, lanes(b)] += fold_rows(earlier * n)
                column[DEPTH_BIAS, :, lanes(b)] += fold_rows(here)
                q = (
                    params[9:10, lanes(b)] * later
                    + params[10:11, lanes(b)] * here
                    + params[11:12, lanes(b)] * earlier
                )
                mixed_grad[rows, lanes(b)] = q
                column[SHIFT_ONE, :, lanes(b)] += fold_rows(q)
                q_xhat = q * xhat_one[rows, lanes(b)]
                column[GAIN_ONE, :, lanes(b)] += fold_rows(q_xhat)
                total = total + q
                crossed = crossed + q_xhat
            put_seg(at(r, k, HALO), ROWS, 0, total)
            put_seg(at(r, k, HALO), ROWS, 2, crossed)

    total, crossed = item_sums(0, (2, 2))
    pack_tile(tile_three, {"sum": total, "crossed": crossed})
    exchange(tile_three, stats_three, 2)

    def column_sum(which):
        return jnp.sum(column[which], axis=0, keepdims=True)

    early_rows = {
        1: column_sum(GAIN_ONE) / params[1:2, :],
        2: column_sum(SHIFT_ONE) / params[1:2, :],
        3: column_sum(DEPTH_BIAS),
        4: column_sum(GAIN_TWO) / params[4:5, :],
        5: column_sum(SHIFT_TWO) / params[4:5, :],
        TAP_ROW: column_sum(TAP_A),
        TAP_ROW + 1: column_sum(TAP_B),
        TAP_ROW + 2: column_sum(TAP_C),
    }
    slope_two_row = column_sum(SLOPE_TWO)
    slope_two_row = (slope_two_row[:, 0:half] + slope_two_row[:, half:hidden]) / slope_two
    for c in range(2):
        small_part[c] = jnp.zeros((16, half), F32)
        for row, v in early_rows.items():
            small_part[c, row : row + 1, :] = v[:, c * half : (c + 1) * half]
        small_part[c, BIAS_ROW : BIAS_ROW + 1, :] = bias_sum
        small_part[c, SLOPE_TWO_ROW : SLOPE_TWO_ROW + 1, :] = slope_two_row

    keeper = chips // 2 // stride * stride * 2
    is_keeper = tm == keeper

    def to_keepers(parts, ref, slot, count, phase, sends):
        def each(act):
            for c in range(2):
                copy = remote(parts.at[c], ref.at[slot], phase + c, {"chan": c, "tm": keeper})
                pl.when(sends & ((tm != keeper) | (chan != c)))(lambda: act(copy))

        each(lambda copy: copy.start())
        pending[phase, "sent"] = lambda: each(lambda copy: copy.wait_send())
        pending[phase, "here"] = lambda: [
            pl.when(is_keeper & (chan == c))(
                lambda: wait_bytes(ref.at[pl.ds(0, count - 1)], recv_sem.at[phase + c])
            )
            for c in range(2)
        ]

    pair = remote(small_part, small_pair, 10, sibling)
    started(pair, 10, core == 1, core == 0)
    @own_loop()
    def _(r):
        product = dot(mixed[pl.ds(at(r, 0, HALO), BLOCK), :], w_project[...])
        for k in range(0, BLOCK, ROWS):
            rows = pl.ds(at(r, k, HALO), ROWS)
            inputs = x[pl.ds(at(r, k), ROWS), :].astype(F32)
            block_out[rows, :] = (
                inputs + part(product, k, ROWS, 0) + biases_ref[0:1, :]
            ).astype(BF16)
            skip_out[rows, :] = (part(product, k, ROWS, 1) + biases_ref[1:2, :]).astype(BF16)

    settle((10, "here"))

    @pl.when(core == 0)
    def _():
        small_part[...] += small_pair[...]

    to_keepers(small_part, small_in, mate, mates, 12, core == 0)
    settle((11, "here"))
    sum_rows = pl.ds(pl.multiple_of(core * LANES + spot * 16, 16), 16)

    @when_reducer
    def _():
        project_in[mate] = project_piece(chan, spot)[...]
        total = total_of(project_in, mates, 16, half)
        project_sum[sum_rows, :] = total
        square_part[...] = fold_lanes(jnp.sum(total * total, axis=0, keepdims=True))
        to_group(project_sum.at[sum_rows, :], project_sum.at[sum_rows, :], 17, chips)

    pending[17, "sent"] = lambda: when_reducer(
        lambda: group_sent(project_sum.at[pl.ds(0, 16), :], 17, chips)
    )
    pending[17, "here"] = lambda: by_role(
        lambda n: wait_bytes(project_sum.at[pl.ds(0, 16 * n), :], recv_sem.at[17]), PIECES // 2
    )

    settle(("near", 2, "here"))
    put_table(0, sum_of("sum", tile_three, stats_three) / elements)
    put_table(1, sum_of("crossed", tile_three, stats_three) / elements)
    put_table(2, scale_one)


    for c in range(2):

        @own_loop()
        def _(r, c=c):
            if c == 0:
                values = rows_of(r, BLOCK, 3)
                act_two[pl.ds(r, BLOCK), 0 : 3 * LANES] = values
            for k in range(0, BLOCK, ROWS):
                rows, local = pl.ds(at(r, k), ROWS), pl.ds(at(r, k, HALO), ROWS)
                if c == 0:
                    q_mean, cross_mean, scale = [part(values, k, ROWS, j) for j in range(3)]
                else:
                    q_mean, cross_mean, scale = [act_two[rows, lanes(j)] for j in range(3)]
                for b in range(c * blocks // 2, (c + 1) * blocks // 2):
                    a = act_one[rows, lanes(b)]
                    g = mixed_grad[rows, lanes(b)] - q_mean
                    g = (g - xhat_one[rows, lanes(b)] * cross_mean) * scale
                    column[SLOPE_ONE, :, lanes(b)] += fold_rows(g * jnp.minimum(a, 0.0))
                    hidden_grad[local, lanes(b)] = (g * jnp.where(a > 0, 1.0, slope_one)).astype(
                        BF16
                    )

        total = jnp.zeros((LANES, half), F32)
        for k in range(frames // step):
            total = total + dot_frames(
                x[pl.ds(HALO + k * step, step), :],
                hidden_grad[pl.ds(k * step, step), c * half : (c + 1) * half],
            )
        expand_part[:, c * half : (c + 1) * half] = total
        source = pl.ds(pl.multiple_of(c * half + (1 - core) * LANES, LANES), LANES)
        started(remote(expand_part.at[:, source], expand_pair.at[c], 8 + c, sibling), 8 + c)

    def send_expand(c):
        settle((8 + c, "here"))
        expand_pair[c] += expand_part[
            :, pl.ds(pl.multiple_of(c * half + core * LANES, LANES), LANES)
        ]
        send_pieces(expand_piece, expand_in, 16, c)

    send_expand(0)
    bias_one = dot(jnp.ones((16, frames), BF16), hidden_grad[...])[0:1]
    slope_row = column_sum(SLOPE_ONE)
    slope_row = (slope_row[:, 0:half] + slope_row[:, half:hidden]) / slope_one
    for c in range(2):
        late_part[c, 0:1, :] = bias_one[:, c * half : (c + 1) * half]
        late_part[c, 1:2, :] = slope_row
    to_keepers(late_part, late_in, me, devices, 14, tm >= 0)
    send_expand(1)
    pieces_pending(expand_in, 16)

    settle((12, "here"))

    @pl.when(is_keeper)
    def _():
        small_in[mate] = small_part[chan]
        total = total_of(small_in, mates, 16, half)
        small_sum[...] = total
        square_part[...] += fold_lanes(
            jnp.sum((total * total)[0:BIAS_ROW], axis=0, keepdims=True)
        )
        to_group(small_sum, small_sum, 18, tm_size)

    pending[18, "sent"] = lambda: pl.when(is_keeper)(lambda: group_sent(small_sum, 18, tm_size))
    pending[18, "here"] = lambda: pl.when(jnp.logical_not(is_keeper))(
        lambda: wait_bytes(small_sum, recv_sem.at[18])
    )

    @own_loop()
    def _(r):
        product = dot_rows(hidden_grad[pl.ds(at(r, 0, HALO), BLOCK), :], w_expand[...])
        for k in range(0, BLOCK, ROWS):
            above = cots[pl.ds(at(r, k), ROWS), 0:LANES].astype(F32)
            input_out[pl.ds(at(r, k, HALO), ROWS), :] = above + part(product, k, ROWS, 0)

    extra[...] = jnp.zeros_like(extra)

    def put_extra(k, v):
        high = rounded(v)
        middle = rounded(v - high)
        for j, p in enumerate((high, middle, v - high - middle)):
            extra[3 * k + j : 3 * k + j + 1, :] = p

    settle((14, "here"))

    @pl.when(is_keeper)
    def _():
        late_in[me] = late_part[chan]
        total = total_of(late_in, devices, 2, half)
        for k in range(2):
            for j in range(2):
                put_extra(1 + 2 * k + j, total[j : j + 1, k * LANES : (k + 1) * LANES])
        squares = (total * total)[0:1]
        square_part[...] += fold_lanes(squares)

    settle((16, "here"))

    @when_reducer
    def _():
        expand_in[mate] = expand_piece(chan, spot)[...]
        total = total_of(expand_in, mates, 16, LANES)
        squares = square_part[...] + jnp.sum(total * total, axis=0, keepdims=True)
        square_part[...] = squares
        put_extra(0, squares)
        last_part[0:16, :] = total.astype(BF16)
        last_part[16:32, :] = extra[...].astype(BF16)
        slot = core * spots_here + spot
        last_in[slot] = last_part[...]
        to_group(last_part, last_in.at[slot], 19, tm_size)

        def send_tail(k, carry):
            target = {"chan": other, "tm": wrapped(tm + k, tm_size)}
            remote(square_part, tail_in.at[slot], 20, target).start()
            return carry

        if tm_size <= 16:
            for k in range(tm_size):
                send_tail(k, 0)
        else:
            lax.fori_loop(0, tm_size, send_tail, 0)

    def tails_sent():
        for _ in range(stride):
            wait_bytes(tail_in, send_sem.at[20])

    def from_reducers(n):
        wait_bytes(last_in.at[pl.ds(0, n)], recv_sem.at[19])

    pending[19, "sent"] = lambda: when_reducer(lambda: group_sent(last_part, 19, tm_size))
    pending[19, "here"] = lambda: by_role(from_reducers, PIECES)
    pending[20, "sent"] = lambda: when_reducer(tails_sent)
    pending[20, "here"] = lambda: wait_bytes(tail_in, recv_sem.at[20])

    settle((17, "here"))
    started(remote(project_sum.at[mine, :], project_sum.at[mine, :], 21, sibling), 21)
    settle((18, "here"), (21, "here"))
    for k in range(2):
        project_grad_ref[k] = project_sum[k * LANES : (k + 1) * LANES, :].T
    small_grad_ref[...] = small_sum[...]
    settle((19, "here"), (20, "here"))
    for c in range(2):
        for j in range(spots_here):
            where = slice(c * LANES, (c + 1) * LANES)
            expand_grad_ref[j * 16 : j * 16 + 16, where] = last_in[c * spots_here + j, 0:16, :].astype(F32)
    keeper_spot = keeper // 2 // stride

    def extras(c, j):
        return last_in[c * spots_here + j, 16:32, :].astype(F32)

    def get_extra(rows, k):
        return rows[3 * k : 3 * k + 1] + rows[3 * k + 1 : 3 * k + 2] + rows[3 * k + 2 : 3 * k + 3]

    late = extras(0, keeper_spot)
    for k in range(2):
        where = slice(k * LANES, (k + 1) * LANES)
        small_grad_ref[0:1, where] = get_extra(late, 1 + 2 * k)
        small_grad_ref[SLOPE_ONE_ROW : SLOPE_ONE_ROW + 1, where] = get_extra(late, 2 + 2 * k)
    own_total, other_total = None, None
    for q in range(PIECES):
        c, j = q // spots_here, q % spots_here
        mine_here, theirs = get_extra(extras(c, j), 0), tail_in[q]
        own_total = mine_here if own_total is None else own_total + mine_here
        other_total = theirs if other_total is None else other_total + theirs
    small_grad_ref[SQUARES_ROW : SQUARES_ROW + 1, 0:LANES] = own_total + other_total
    small_grad_ref[SQUARES_ROW : SQUARES_ROW + 1, LANES:half] = jnp.zeros((1, half - LANES), F32)

    settle(*list(pending))


def adam(weight, moment, square, gradient, scale, step_rate):
    clipped = gradient * scale
    moment_next = beta_first * moment + (1.0 - beta_first) * clipped
    square_next = beta_second * square + (1.0 - beta_second) * clipped * clipped
    update = (
        moment_next
        / (1.0 - beta_first**step_count)
        / (jnp.sqrt(square_next / (1.0 - beta_second**step_count)) + adam_eps)
    )
    return weight - step_rate * (update + decay * weight), moment_next, square_next


def adam_kernel(
    block_in,
    skip_in,
    input_in,
    expand_grad,
    project_grad,
    small_grad,
    *refs,
):
    state, outs, slope_refs = list(refs[:15]), refs[18:40], refs[40:43]
    sem = refs[43]
    slope_loads = [
        pltpu.make_async_copy(refs[15 + k], slope_refs[k], sem.at[3 + k]) for k in range(3)
    ]
    for load in slope_loads:
        load.start()
    state += slope_refs
    copies = [
        pltpu.make_async_copy(src, dst, sem.at[k])
        for k, (src, dst) in enumerate(
            zip((block_in, skip_in, input_in), (outs[0], outs[1], outs[2]))
        )
    ]
    for copy in copies:
        copy.start()
    biases = small_grad[BIAS_ROW : BIAS_ROW + 1, :]
    slopes = [
        jnp.sum(small_grad[row : row + 1, :], axis=1, keepdims=True)
        for row in (SLOPE_ONE_ROW, SLOPE_TWO_ROW)
    ]
    total = jnp.sum(small_grad[SQUARES_ROW : SQUARES_ROW + 1, :] + biases * biases, axis=1, keepdims=True)
    total = total + slopes[0] * slopes[0] + slopes[1] * slopes[1]
    grad_norm = jnp.sqrt(total)
    scale = jnp.minimum(1.0, clip_level / grad_norm)
    outs[3][0, 0] = grad_norm[0, 0]

    def update(k, gradient, step_rate, at=...):
        results = adam(
            state[3 * k][at], state[3 * k + 1][at], state[3 * k + 2][at], gradient, scale, step_rate
        )
        for j in range(3):
            outs[4 + 3 * k + j][at] = results[j]

    update(0, expand_grad[...], rate)
    update(1, small_grad[TAP_ROW : TAP_ROW + 3, :], small_rate)
    for k in range(2):
        update(2, project_grad[k], rate, k)
    update(3, small_grad[0:6, :], small_rate)
    lanes = biases.shape[1] // 2
    for k in range(2):
        update(4, biases[:, k * lanes : (k + 1) * lanes], small_rate, slice(k, k + 1))
    for load in slope_loads:
        load.wait()
    for k in range(2):
        results = adam(
            state[15][k], state[16][k], state[17][k], slopes[k], scale, small_rate
        )
        for j in range(3):
            outs[19 + j][k] = results[j][0, 0]
    for copy in copies:
        copy.wait()


def per_device(
    tm_size,
    frames_in,
    item_lengths,
    out_cotangent,
    skip_cotangent,
    expand,
    expand_moment,
    expand_square,
    depthwise,
    depth_moment,
    depth_square,
    project,
    project_moment,
    project_square,
    channel_vectors,
    vector_moment,
    vector_square,
    output_biases,
    bias_moment,
    bias_square,
    prelu_slopes,
    slope_moment,
    slope_square,
):
    frames, inputs = frames_in.shape
    half = expand.shape[1]
    hidden = 2 * half
    items = item_lengths.shape[0]
    item_pad = -(-items // 16) * 16
    width = -(-3 * item_pad // LANES) * LANES
    wide = frames + 2 * HALO
    devices = 2 * tm_size
    peers = 2 * (-(-LONGEST_ITEM // frames))
    tile_rows = spots_of(item_pad)[0]
    vmem, smem, anywhere, hbm = (
        pl.BlockSpec(memory_space=space)
        for space in (pltpu.VMEM, pltpu.SMEM, pl.ANY, pltpu.HBM)
    )
    shape = jax.ShapeDtypeStruct
    scratch = [
        ((wide, inputs), BF16),
        ((wide, 2 * inputs), BF16),
        ((inputs, hidden), BF16),
        ((hidden, 2 * inputs), BF16),
        ((16, hidden), F32),
        ((wide, width), BF16),
        ((item_pad, frames), BF16),
        ((wide, LANES), F32),
        ((wide, LANES), F32),
        ((width, 4 * LANES), BF16),
        ((peers + 1, 1, LANES), F32),
        ((wide, hidden), F32),
        ((wide, hidden), F32),
        ((wide, hidden), F32),
        ((wide, hidden), F32),
        ((wide, hidden), F32),
        ((frames, hidden), BF16),
        ((frames, hidden), BF16),
        ((frames, 8 * LANES), BF16),
        ((COLUMN_SUMS, 8, hidden), F32),
        ((tile_rows, LANES), F32),
        ((tile_rows, LANES), F32),
        ((tile_rows, LANES), F32),
        ((peers, tile_rows, LANES), F32),
        ((peers, tile_rows, LANES), F32),
        ((peers, tile_rows, LANES), F32),
        ((2 * inputs, hidden), F32),
        ((inputs, hidden), F32),
        ((inputs, hidden), F32),
        ((2, inputs, LANES), F32),
        ((tm_size, 16, half), F32),
        ((tm_size, 16, LANES), F32),
        ((2, 16, half), F32),
        ((2, 16, half), F32),
        ((tm_size, 16, half), F32),
        ((2, 2, half), F32),
        ((devices, 2, half), F32),
        ((2 * inputs, half), F32),
        ((16, half), F32),
        ((1, LANES), F32),
        ((16, LANES), F32),
        ((32, LANES), BF16),
        ((PIECES, 32, LANES), BF16),
        ((PIECES, 1, LANES), F32),
    ]
    state = [
        expand,
        expand_moment,
        expand_square,
        depthwise,
        depth_moment,
        depth_square,
        project,
        project_moment,
        project_square,
        channel_vectors,
        vector_moment,
        vector_square,
        output_biases,
        bias_moment,
        bias_square,
    ]
    state = in_hbm(state)
    slopes = in_hbm([prelu_slopes, slope_moment, slope_square])
    arrays = in_hbm([item_lengths, frames_in, out_cotangent, skip_cotangent])
    kept = pl.pallas_call(
        functools.partial(block_kernel, tm_size, items, item_pad),
        out_shape=[
            shape((frames, inputs), BF16),
            shape((frames, inputs), BF16),
            shape((frames, inputs), F32),
            shape((inputs, half), F32),
            shape((2, half, inputs), F32),
            shape((16, half), F32),
        ]
        + [shape(v.shape, F32) for v in state],
        in_specs=[hbm] * 20,
        out_specs=[vmem] * 21,
        scratch_shapes=[pltpu.SMEM((items,), jnp.int32), pltpu.SMEM((2,), F32)]
        + [pltpu.VMEM(s, t) for s, t in scratch]
        + [
            pltpu.SemaphoreType.DMA((25,)),
            pltpu.SemaphoreType.DMA((24,)),
            pltpu.SemaphoreType.DMA((24,)),
            pltpu.SemaphoreType.DMA((3, peers)),
            pltpu.SemaphoreType.DMA((3, peers)),
        ],
        compiler_params=pltpu.CompilerParams(
            collective_id=0, has_side_effects=True, vmem_limit_bytes=48 * 2**20
        ),
        name="temporal_block",
    )(arrays[0], slopes[0], *arrays[1:], *state)
    results = pl.pallas_call(
        adam_kernel,
        out_shape=[
            shape((frames, inputs), BF16),
            shape((frames, inputs), BF16),
            shape((frames, inputs), F32),
            shape((1, 1), F32),
        ]
        + [shape(v.shape, F32) for v in state + slopes],
        in_specs=[anywhere] * 3 + [vmem] * 18 + [hbm] * 3,
        out_specs=[anywhere] * 3 + [smem] + [vmem] * 15 + [smem] * 3,
        scratch_shapes=[pltpu.SMEM((2,), F32)] * 3 + [pltpu.SemaphoreType.DMA((6,))],
        compiler_params=pltpu.CompilerParams(vmem_limit_bytes=8 * 2**20),
        name="adam_step",
    )(*kept, *slopes)
    results = list(results)
    results[3] = results[3].reshape(())
    return tuple(results)


def solution(mesh):
    frames = P(("tm", "chan"), None)
    columns = P(None, "chan")
    rows = P(None, "chan", None)
    in_specs = (
        (frames, P(), frames, frames)
        + (columns,) * 3
        + (columns,) * 3
        + (rows,) * 3
        + (columns,) * 3
        + (P(),) * 6
    )
    out_specs = (
        (frames, frames, frames, P())
        + (columns,) * 3
        + (columns,) * 3
        + (rows,) * 3
        + (columns,) * 3
        + (P(),) * 6
    )
    return jax.shard_map(
        functools.partial(per_device, mesh.shape["tm"]),
        mesh=mesh,
        in_specs=in_specs,
        out_specs=out_specs,
        check_vma=False,
    )
```

```python
import functools

import jax
import jax.numpy as jnp
from jax import lax
from jax.experimental import pallas as pl
from jax.experimental.pallas import tpu as pltpu
from jax.sharding import PartitionSpec as P

F32 = jnp.float32
BF16 = jnp.bfloat16
MESH = pl.DeviceIdType.MESH

DILATION = 16
HALO = 2 * DILATION
LONGEST_ITEM = 8192
LANES = 128
ROWS = 32
BLOCK = 2048
PIECES = 16

norm_eps = 1e-06
clip_level = 5.0
rate = 0.05
small_rate = 0.5
beta_first = 0.9
beta_second = 0.999
adam_eps = 1e-08
decay = 0.01
step_count = 10.0

TAP_ROW = 6
BIAS_ROW = 9
SLOPE_TWO_ROW = 10
SLOPE_ONE_ROW = 11
SQUARES_ROW = 12

(GAIN_TWO, SHIFT_TWO, TAP_A, TAP_B, TAP_C, DEPTH_BIAS, GAIN_ONE, SHIFT_ONE, SLOPE_TWO, SLOPE_ONE, COLUMN_SUMS) = range(11)


def dot(a, b):
    return lax.dot_general(a, b, (((1,), (0,)), ((), ())), preferred_element_type=F32)


def dot_rows(a, b):
    return lax.dot_general(a, b, (((1,), (1,)), ((), ())), preferred_element_type=F32)


def dot_frames(a, b):
    return lax.dot_general(a, b, (((0,), (0,)), ((), ())), preferred_element_type=F32)


def rounded(v):
    return v.astype(BF16).astype(F32)


def spread_lanes(v):
    return jnp.broadcast_to(jnp.sum(v, axis=1, keepdims=True), (v.shape[0], LANES))


def in_hbm(arrays):
    return [pltpu.with_memory_space_constraint(v, pltpu.HBM) for v in arrays]


def spots_of(item_pad):
    names = ("sum", "spread", "mean", "crossed")
    if 4 * item_pad <= LANES:
        return 2, {**{n: (0, k * item_pad) for k, n in enumerate(names)}, "q": (1, 2 * item_pad)}
    return 5, {n: (k, 0) for k, n in enumerate(names + ("q",))}


def fold_rows(v):
    return jnp.sum(v.reshape(v.shape[0] // 8, 8, v.shape[1]), axis=0)


def block_kernel(
    tm_size,
    item_count,
    item_pad,
    len_hbm,
    slope_hbm,
    frames_hbm,
    out_cot_hbm,
    skip_cot_hbm,
    *refs,
):
    state_hbm, refs = refs[:15], refs[15:]
    block_out, skip_out, input_out, expand_grad_ref, project_grad_ref, small_grad_ref = refs[:6]
    state_refs, refs = refs[6:21], refs[21:]
    expand_ref, taps_ref, project_ref, vectors_ref, biases_ref = state_refs[::3]
    (
    len_ref,
    slope_ref,
    x,
    cots,
    w_expand,
    w_project,
    params,
    item_rows,
    item_cols,
    mask_low,
    mask_high,
    table,
    counts,
    act_one,
    xhat_one,
    normed,
    mixed_grad,
    act_two,
    mixed,
    hidden_grad,
    seg,
    column,
    tile_one,
    tile_two,
    tile_three,
    stats_one,
    stats_two,
    stats_three,
    project_part,
    expand_part,
    project_pair,
    expand_pair,
    project_in,
    expand_in,
    small_part,
    small_pair,
    small_in,
    late_part,
    late_in,
    project_sum,
    small_sum,
    square_part,
    extra,
    last_part,
    last_in,
    tail_in,
    local_sem,
    send_sem,
    recv_sem,
    near_send,
    near_recv,
    ) = refs
    frames = block_out.shape[0]
    wide = x.shape[0]
    half = expand_ref.shape[1]
    hidden = 2 * half
    blocks = hidden // LANES
    devices = 2 * tm_size
    stride = tm_size // PIECES
    spans = -(-LONGEST_ITEM // frames)
    chan = lax.axis_index("chan")
    tm = lax.axis_index("tm")
    me = tm * 2 + chan
    other = 1 - chan

    def device(index):
        return {"chan": lax.rem(index, 2), "tm": lax.div(index, 2)}

    def remote(src, dst, phase, target):
        return pltpu.make_async_remote_copy(
            src_ref=src,
            dst_ref=dst,
            send_sem=send_sem.at[phase],
            recv_sem=recv_sem.at[phase],
            device_id=target,
            device_id_type=MESH,
        )

    def wait_bytes(ref, sem):
        pltpu.make_async_copy(ref, ref, sem).wait()

    pending = {}

    def settle(*keys):
        for key in keys:
            pending.pop(key)()

    def started(copy, name, sends=None, receives=None):
        def maybe(condition, body):
            if condition is None:
                body()
            else:
                pl.when(condition)(body)

        maybe(sends, copy.start)
        pending[name, "sent"] = lambda: maybe(sends, copy.wait_send)
        pending[name, "here"] = lambda: maybe(receives, copy.wait_recv)

    own = pl.ds(HALO, frames)
    loads = {
        "expand": (state_hbm[0], expand_ref),
        "frames": (frames_hbm, x.at[own, :]),
        "vectors": (state_hbm[9], vectors_ref),
        "taps": (state_hbm[3], taps_ref),
        "lengths": (len_hbm, len_ref),
        "slopes": (slope_hbm, slope_ref),
        "project": (state_hbm[6], project_ref),
        "out": (out_cot_hbm, cots.at[own, pl.ds(0, LANES)]),
        "skip": (skip_cot_hbm, cots.at[own, pl.ds(LANES, LANES)]),
        "biases": (state_hbm[12], biases_ref),
    }
    def load_some(first, last):
        for k, (name, (src, dst)) in list(enumerate(loads.items()))[first:last]:
            load = pltpu.make_async_copy(src, dst, local_sem.at[k])
            load.start()
            pending["load", name] = load.wait

    load_some(0, 2)

    def loaded(*names):
        settle(*[("load", name) for name in names])

    for r in (0, HALO + frames):
        x[r : r + HALO, :] = jnp.zeros((HALO, x.shape[1]), BF16)
    for r in (HALO - DILATION, HALO + frames):
        cots[r : r + DILATION, :] = jnp.zeros((DILATION, cots.shape[1]), BF16)
    for stats in (stats_one, stats_two, stats_three):
        stats[...] = jnp.zeros_like(stats)

    barrier = pltpu.get_barrier_semaphore()

    def wrapped(v, size):
        return jnp.where(v >= size, v - size, v)

    def greet(k, carry):
        t = wrapped(tm + k, tm_size)
        for c in range(2):
            pl.semaphore_signal(
                barrier, inc=1, device_id={"chan": c, "tm": t}, device_id_type=MESH
            )
        return carry

    pl.semaphore_signal(barrier, inc=1, device_id={"chan": other, "tm": tm}, device_id_type=MESH)
    if tm_size <= 16:
        for k in range(1, tm_size):
            greet(k, 0)
    else:
        lax.fori_loop(1, tm_size, greet, 0)

    load_some(2, len(loads))

    my_half = pl.ds(pl.multiple_of(chan * half, half), half)
    loaded("expand")
    w_expand[:, my_half] = expand_ref[...].astype(BF16)
    pl.semaphore_wait(barrier, devices - 1)

    partner = device(tm * 2 + other)
    left, right = device(me - 1), device(me + 1)
    has_left, has_right = me > 0, me < devices - 1

    def to_left(ref, count, name):
        copy = remote(
            ref.at[pl.ds(HALO, count), :], ref.at[pl.ds(HALO + frames, count), :], name, left
        )
        started(copy, name, has_left, has_right)

    def to_right(ref, count, name):
        copy = remote(
            ref.at[pl.ds(HALO + frames - count, count), :],
            ref.at[pl.ds(HALO - count, count), :],
            name,
            right,
        )
        started(copy, name, has_right, has_left)

    started(remote(w_expand.at[:, my_half], w_expand.at[:, my_half], 0, partner), 0)
    loaded("vectors", "taps")
    params[0:6, my_half] = vectors_ref[...]
    params[6:9, my_half] = taps_ref[...]
    params[9:12, my_half] = vectors_ref[1:2, :] * taps_ref[...]
    params[12:16, my_half] = jnp.zeros((4, half), F32)
    started(remote(params.at[:, my_half], params.at[:, my_half], 1, partner), 1)
    loaded("frames")
    to_left(x, HALO, 2)
    to_right(x, HALO, 3)
    loaded("project", "out", "skip")
    w_project[my_half, 0:LANES] = project_ref[0].astype(BF16)
    w_project[my_half, LANES : 2 * LANES] = project_ref[1].astype(BF16)
    started(remote(w_project.at[my_half, :], w_project.at[my_half, :], 4, partner), 4)
    to_left(cots, DILATION, 5)
    to_right(cots, DILATION, 6)
    loaded("lengths", "slopes", "biases")
    moments = [k for k in range(15) if k % 3]
    for k in moments:
        load = pltpu.make_async_copy(state_hbm[k], state_refs[k], local_sem.at[10 + k])
        load.start()
        pending["load", k] = load.wait

    width = table.shape[0]
    lane = lax.broadcasted_iota(jnp.int32, (8, width), 1)
    lane_item = lax.rem(lane, item_pad)
    row_item = lax.broadcasted_iota(jnp.int32, (item_pad, LANES), 0)

    def bounds(j, carry):
        lane_start, lane_end, row_start, row_end = carry
        length = len_ref[j]
        return (
            lane_start + jnp.where(lane_item > j, length, 0),
            lane_end + jnp.where(lane_item >= j, length, 0),
            row_start + jnp.where(row_item > j, length, 0),
            row_end + jnp.where(row_item >= j, length, 0),
        )

    lane_zero, row_zero = jnp.zeros_like(lane), jnp.zeros_like(row_item)
    lane_start, lane_end, row_start, row_end = lax.fori_loop(
        0, item_count, bounds, (lane_zero, lane_zero, row_zero, row_zero)
    )
    lane_end = jnp.where(lane < 3 * item_pad, lane_end, lane_start)
    first = me * frames
    lane_start_row, lane_end_row = lane_start[0:1], lane_end[0:1]
    elements = jnp.maximum((row_end - row_start).astype(F32) * hidden, 1.0)

    def count_of(index):
        low = jnp.maximum(row_start, index * frames)
        high = jnp.minimum(row_end, (index + 1) * frames)
        return jnp.maximum(high - low, 0).astype(F32) * hidden

    my_count = count_of(me)
    my_safe = jnp.maximum(my_count, 1.0)
    offsets = [sign * o for o in range(spans, 0, -1) for sign in (1, -1)]
    spots = spots_of(item_pad)[1]
    tile_lane = lax.broadcasted_iota(jnp.int32, (item_pad, LANES), 1)

    def packed(v, name):
        chosen = tile_lane == spots[name][1] + row_item
        return jnp.sum(jnp.where(chosen, v, 0.0), axis=0, keepdims=True)

    def unpacked(row, name):
        chosen = tile_lane == spots[name][1] + row_item
        return spread_lanes(jnp.where(chosen, jnp.broadcast_to(row, chosen.shape), 0.0))

    counts[len(offsets)] = packed(my_count, "mean")
    for slot, offset in enumerate(offsets):
        counts[slot] = packed(count_of(me - offset), "mean")
    column[...] = jnp.zeros_like(column)

    def put_table(place, v):
        high = v.astype(BF16)
        rest = v - high.astype(F32)
        middle = rest.astype(BF16)
        low = (rest - middle.astype(F32)).astype(BF16)
        where = slice(place * LANES, (place + 1) * LANES)
        table[0:item_pad, where] = high
        table[item_pad : 2 * item_pad, where] = middle
        table[2 * item_pad : 3 * item_pad, where] = low

    def rows_of(r, n, count):
        return dot(item_rows[pl.ds(r, n), :], table[:, 0 : count * LANES])

    def part(values, k, n, b):
        return values[k : k + n, b * LANES : (b + 1) * LANES]

    def put_seg(r, n, place, v, exact=True):
        high = v.astype(BF16)
        seg[pl.ds(r, n), pl.ds(place * LANES, LANES)] = high
        if exact:
            low = (v - high.astype(F32)).astype(BF16)
            seg[pl.ds(r, n), pl.ds((place + 1) * LANES, LANES)] = low

    def item_sums(first, widths):
        sums = dot(item_cols[...], seg[:, first * LANES : (first + sum(widths)) * LANES])
        results, k = [], 0
        for n in widths:
            v = sums[:, k * LANES : (k + 1) * LANES]
            if n == 2:
                v = v + sums[:, (k + 1) * LANES : (k + 2) * LANES]
            results.append(spread_lanes(v))
            k += n
        return results

    def loop(start, size, count, body, rep=1):
        def step(i, carry):
            i = i if rep == 1 else lax.rem(i, count)
            body(pl.multiple_of(start + i * size, 16))
            return carry

        lax.fori_loop(0, count * rep, step, 0)

    def at(r, k, shift=0):
        return pl.multiple_of(r + (k - shift), 16)

    table[...] = jnp.zeros_like(table)
    put_table(0, row_start.astype(F32))
    put_table(1, row_end.astype(F32))

    wide_block = wide
    wide_rows = wide_block // 44

    @functools.partial(loop, 0, wide_block, 1)
    def _(r):
        for k in range(0, wide_block, wide_rows):
            position = first - HALO + r + k + lax.broadcasted_iota(jnp.int32, (wide_rows, width), 0)
            inside = (position >= lane_start_row) & (position < lane_end_row)
            item_rows[pl.ds(at(r, k), wide_rows), :] = inside.astype(F32).astype(BF16)
        ends = rows_of(r, wide_block, 2)
        for k in range(0, wide_block, wide_rows):
            here = first - HALO + r + k + lax.broadcasted_iota(jnp.int32, (wide_rows, LANES), 0)
            here = here.astype(F32)
            after = here - part(ends, k, wide_rows, 0)
            before = part(ends, k, wide_rows, 1) - here
            mask_low[pl.ds(at(r, k), wide_rows), :] = (after >= DILATION).astype(F32)
            mask_high[pl.ds(at(r, k), wide_rows), :] = (before > DILATION).astype(F32)

    for i in range(frames // LANES):
        position = first + i * LANES + lax.broadcasted_iota(jnp.int32, (item_pad, LANES), 1)
        inside = (position >= row_start) & (position < row_end)
        item_cols[:, i * LANES : (i + 1) * LANES] = inside.astype(F32).astype(BF16)

    slope_one, slope_two = slope_ref[0], slope_ref[1]

    def lanes_of(which, b):
        return pl.ds(pl.multiple_of(which * half + b * LANES, LANES), LANES)

    def half_of(which):
        return pl.ds(pl.multiple_of(which * half, half), half)

    def activate(product, k, n, which, b):
        v = part(product, k, n, b) + params[0:1, lanes_of(which, b)]
        return jnp.maximum(v, slope_one * v)

    own_loop = functools.partial(functools.partial, loop, HALO, BLOCK, frames // BLOCK)

    @own_loop()
    def _(r):
        product = dot(x[pl.ds(r, BLOCK), :], w_expand[:, half_of(chan)])
        for k in range(0, BLOCK, ROWS):
            total = jnp.zeros((ROWS, LANES), F32)
            for b in range(blocks // 2):
                a = activate(product, k, ROWS, chan, b)
                act_one[pl.ds(at(r, k), ROWS), lanes_of(chan, b)] = a
                total = total + a
            put_seg(at(r, k, HALO), ROWS, 0, total)

    (total,) = item_sums(0, (2,))
    shift = total / jnp.maximum(my_count * 0.5, 1.0)
    put_table(0, shift)
    settle(*[(k, "here") for k in range(4)])

    @own_loop()
    def _(r):
        centres = rows_of(r, BLOCK, 1)
        product = dot(x[pl.ds(r, BLOCK), :], w_expand[:, half_of(other)])
        for k in range(0, BLOCK, ROWS):
            rows = pl.ds(at(r, k), ROWS)
            centre = part(centres, k, ROWS, 0)
            total = jnp.zeros((ROWS, LANES), F32)
            squares = jnp.zeros((ROWS, LANES), F32)
            for b in range(blocks // 2):
                d = act_one[rows, lanes_of(chan, b)] - centre
                total = total + d
                squares = squares + d * d
                a = activate(product, k, ROWS, other, b)
                act_one[rows, lanes_of(other, b)] = a
                d = a - centre
                total = total + d
                squares = squares + d * d
            put_seg(at(r, k, HALO), ROWS, 0, total)
            put_seg(at(r, k, HALO), ROWS, 2, squares)

    def pack_tile(tile, values):
        for r in range(tile.shape[0]):
            row = jnp.zeros((1, LANES), F32)
            for name, v in values.items():
                if spots[name][0] == r:
                    row = row + packed(v, name)
            tile[r : r + 1, :] = row

    def local_moments(shift, total, squares):
        mean = shift + total / my_safe
        spread = jnp.maximum(squares - total * total / my_safe, 0.0)
        return mean, spread

    def exchange(tile, stats, phase):
        def near(slot, offset):
            return pltpu.make_async_remote_copy(
                src_ref=tile,
                dst_ref=stats.at[slot],
                send_sem=near_send.at[phase, slot],
                recv_sem=near_recv.at[phase, slot],
                device_id=device(me + offset),
                device_id_type=MESH,
            )

        def all_near(source, act):
            for slot, offset in enumerate(offsets):
                index = me - offset if source else me + offset
                pl.when((index >= 0) & (index < devices))(lambda: act(near(slot, offset)))

        all_near(False, lambda copy: copy.start())
        pending["near", phase, "sent"] = lambda: all_near(False, lambda copy: copy.wait_send())
        pending["near", phase, "here"] = lambda: all_near(True, lambda copy: copy.wait_recv())

    def rows_with(name, tile, stats):
        r = spots[name][0]
        return [stats[slot, r : r + 1, :] for slot in range(len(offsets))] + [tile[r : r + 1, :]]

    def sum_of(name, tile, stats):
        total = None
        for row in rows_with(name, tile, stats):
            total = row if total is None else total + row
        return unpacked(total, name)

    def combined(tile, stats):
        mean = sum_of("sum", tile, stats) / elements
        centre = packed(mean, "mean")
        between = jnp.zeros((1, LANES), F32)
        for k, row in enumerate(rows_with("mean", tile, stats)):
            between = between + counts[k] * (row - centre) * (row - centre)
        spread = (sum_of("spread", tile, stats) + unpacked(between, "mean")) / elements
        return mean, centre, lax.rsqrt(spread + norm_eps)

    total, squares = item_sums(0, (2, 2))
    mean, spread = local_moments(shift, total, squares)
    pack_tile(tile_one, {"sum": mean * my_count, "spread": spread, "mean": mean})
    exchange(tile_one, stats_one, 0)

    for r in (0, HALO + frames):
        for which in (chan, other):
            product = dot(x[pl.ds(r, HALO), :], w_expand[:, half_of(which)])
            for b in range(blocks // 2):
                act_one[pl.ds(r, HALO), lanes_of(which, b)] = activate(product, 0, HALO, which, b)

    settle(*[(k, "here") for k in (4, 5, 6)])

    def lanes(b):
        return pl.ds(b * LANES, LANES)

    def mixed_rows(r, n, size, add):
        product = dot_rows(cots[pl.ds(r, n), :], w_project[...])
        for k in range(0, n, size):
            total = jnp.zeros((size, LANES), F32)
            for b in range(blocks):
                q = params[4:5, lanes(b)] * part(product, k, size, b)
                mixed_grad[pl.ds(at(r, k), size), lanes(b)] = q
                if add:
                    total = total + q
                    column[SHIFT_TWO, :, lanes(b)] += fold_rows(q)
            if add:
                put_seg(at(r, k, HALO), size, 4, total)

    @own_loop()
    def _(r):
        mixed_rows(r, BLOCK, ROWS, True)

    for r in (HALO - DILATION, HALO + frames):
        mixed_rows(r, DILATION, DILATION, False)
    bias_sum = dot(jnp.ones((16, frames), BF16), cots[own, :])[0:1]
    (q_sum,) = item_sums(4, (2,))

    settle(("near", 0, "here"))
    mean_one, _, scale_one = combined(tile_one, stats_one)
    put_table(0, mean_one)
    put_table(1, scale_one)

    @functools.partial(loop, 0, wide_block, 1)
    def _(r):
        values = rows_of(r, wide_block, 2)
        for k in range(0, wide_block, wide_rows):
            rows = pl.ds(at(r, k), wide_rows)
            mean, scale = part(values, k, wide_rows, 0), part(values, k, wide_rows, 1)
            for b in range(blocks):
                xhat = (act_one[rows, lanes(b)] - mean) * scale
                xhat_one[rows, lanes(b)] = xhat
                normed[rows, lanes(b)] = rounded(
                    params[1:2, lanes(b)] * xhat + params[2:3, lanes(b)]
                )

    def depth_rows(r, n, b):
        low, high = mask_low[pl.ds(r, n), :], mask_high[pl.ds(r, n), :]
        v = (
            params[3:4, lanes(b)]
            + params[6:7, lanes(b)] * (low * normed[pl.ds(r - DILATION, n), lanes(b)])
            + params[7:8, lanes(b)] * normed[pl.ds(r, n), lanes(b)]
            + params[8:9, lanes(b)] * (high * normed[pl.ds(r + DILATION, n), lanes(b)])
        )
        return jnp.maximum(v, slope_two * v)

    @own_loop()
    def _(r):
        for k in range(0, BLOCK, ROWS):
            a = depth_rows(at(r, k), ROWS, 0)
            act_two[pl.ds(at(r, k), ROWS), lanes(0)] = a
            put_seg(at(r, k, HALO), ROWS, 0, a)

    (total,) = item_sums(0, (2,))
    shift = total / jnp.maximum(my_count * (1.0 / blocks), 1.0)
    put_table(0, shift)

    @own_loop()
    def _(r):
        centres = rows_of(r, BLOCK, 1)
        for k in range(0, BLOCK, ROWS):
            rows = pl.ds(at(r, k), ROWS)
            centre = part(centres, k, ROWS, 0)
            total = jnp.zeros((ROWS, LANES), F32)
            squares = jnp.zeros((ROWS, LANES), F32)
            crossed = jnp.zeros((ROWS, LANES), F32)
            for b in range(blocks):
                if b == 0:
                    a = act_two[rows, lanes(b)]
                else:
                    a = depth_rows(at(r, k), ROWS, b)
                    act_two[rows, lanes(b)] = a
                d = a - centre
                total = total + d
                squares = squares + d * d
                crossed = crossed + mixed_grad[rows, lanes(b)] * d
            put_seg(at(r, k, HALO), ROWS, 0, total)
            put_seg(at(r, k, HALO), ROWS, 2, squares, exact=False)
            put_seg(at(r, k, HALO), ROWS, 3, crossed, exact=False)

    total, squares, crossed = item_sums(0, (2, 1, 1))
    mean, spread = local_moments(shift, total, squares)
    crossed = crossed - (mean - shift) * q_sum
    values = {"sum": mean * my_count, "spread": spread, "mean": mean, "crossed": crossed, "q": q_sum}
    pack_tile(tile_two, values)
    exchange(tile_two, stats_two, 1)

    for r in (HALO - DILATION, HALO + frames):
        for b in range(blocks):
            act_two[pl.ds(r, DILATION), lanes(b)] = depth_rows(r, DILATION, b)

    settle(("near", 1, "here"))
    mean_two, centre, scale_two = combined(tile_two, stats_two)
    between = jnp.zeros((1, LANES), F32)
    for row, q_row in zip(rows_with("mean", tile_two, stats_two), rows_with("q", tile_two, stats_two)):
        between = between + (row - centre) * q_row
    cross_sum = sum_of("crossed", tile_two, stats_two) + unpacked(between, "mean")
    put_table(0, mean_two)
    put_table(1, scale_two)
    put_table(2, scale_two * sum_of("q", tile_two, stats_two) / elements)
    put_table(3, scale_two * scale_two * cross_sum / elements)

    def second_back(r, n, size, add):
        values = rows_of(r, n, 4)
        for k in range(0, n, size):
            rows = pl.ds(at(r, k), size)
            mean, scale, q_mean, cross_mean = [part(values, k, size, j) for j in range(4)]
            for b in range(blocks):
                a = act_two[rows, lanes(b)]
                q = mixed_grad[rows, lanes(b)]
                xhat = (a - mean) * scale
                g = q * scale - q_mean - xhat * cross_mean
                act_two[rows, lanes(b)] = rounded(g * jnp.where(a > 0, 1.0, slope_two))
                if add:
                    mixed[pl.ds(at(r, k, HALO), size), lanes(b)] = (
                        params[4:5, lanes(b)] * xhat + params[5:6, lanes(b)]
                    ).astype(BF16)
                    column[GAIN_TWO, :, lanes(b)] += fold_rows(q * xhat)
                    column[SLOPE_TWO, :, lanes(b)] += fold_rows(g * jnp.minimum(a, 0.0))

    @own_loop()
    def _(r):
        second_back(r, BLOCK, ROWS, True)

    chips = tm_size // 2
    chip = lax.div(tm, 2)
    mates = 2 * chips
    mate = chip * 2 + chan
    spot = lax.div(chip, stride)
    is_reducer = lax.rem(chip, stride) == 0

    def when_reducer(body):
        if stride == 1:
            body()
        else:
            pl.when(is_reducer)(body)

    def by_role(body, count):
        if stride == 1:
            body(count - 1)
        else:
            pl.when(is_reducer)(lambda: body(count - 1))
            pl.when(jnp.logical_not(is_reducer))(lambda: body(count))

    spots_here = PIECES // 2

    def send_pieces(source, ref, phase, c):
        for k in range(spots_here):
            at_spot = wrapped(spot + k, spots_here)
            target = {"chan": c, "tm": at_spot * (2 * stride) + core}
            copy = remote(source(c, at_spot), ref.at[mate], phase, target)
            if k == 0:
                pl.when(jnp.logical_not(is_reducer & (chan == c)))(copy.start)
            else:
                copy.start()

    def pieces_pending(ref, phase):
        pending[phase, "sent"] = lambda: by_role(
            lambda n: wait_bytes(ref.at[pl.ds(0, n)], send_sem.at[phase]), PIECES
        )
        pending[phase, "here"] = lambda: when_reducer(
            lambda: wait_bytes(ref.at[pl.ds(0, mates - 1)], recv_sem.at[phase])
        )

    def piece_rows(at_spot):
        return pl.ds(pl.multiple_of(at_spot * 16, 16), 16)

    def project_piece(c, at_spot):
        return project_pair.at[piece_rows(at_spot), pl.ds(pl.multiple_of(c * half, half), half)]

    def expand_piece(c, at_spot):
        return expand_pair.at[c, piece_rows(at_spot), :]

    def total_of(ref, count, rows, cols):
        if count <= 32:
            total = ref[0]
            for k in range(1, count):
                total = total + ref[k]
            return total
        return lax.fori_loop(
            0, count, lambda k, total: total + ref[k], jnp.zeros((rows, cols), F32)
        )

    def fold_lanes(v):
        return v[:, 0:LANES] + v[:, LANES:half]

    def to_group(src, dst, phase, targets):
        def one(k, carry):
            if targets == chips:
                t = wrapped(chip + k, chips) * 2 + core
            else:
                t = wrapped(tm + k, tm_size)
            remote(src, dst, phase, {"chan": chan, "tm": t}).start()
            return carry

        if targets <= 16:
            for k in range(1, targets):
                one(k, 0)
        else:
            lax.fori_loop(1, targets, one, 0)

    def group_sent(ref, phase, targets):
        def one(k, carry):
            wait_bytes(ref, send_sem.at[phase])
            return carry

        lax.fori_loop(1, targets, one, 0)

    step = 512
    total = jnp.zeros((2 * LANES, hidden), F32)
    for k in range(frames // step):
        total = total + dot_frames(
            cots[pl.ds(HALO + k * step, step), :], mixed[pl.ds(k * step, step), :]
        )
    project_part[...] = total

    core = lax.rem(tm, 2)
    sibling = {"chan": chan, "tm": tm + 1 - 2 * core}
    mine = pl.ds(pl.multiple_of(core * LANES, LANES), LANES)
    yours = pl.ds(pl.multiple_of((1 - core) * LANES, LANES), LANES)
    started(remote(project_part.at[yours, :], project_pair, 7, sibling), 7)

    for r in (HALO - DILATION, HALO + frames):
        second_back(r, DILATION, DILATION, False)

    settle((7, "here"))
    project_pair[...] += project_part[mine, :]
    for c in range(2):
        send_pieces(project_piece, project_in, 11, c)
    pieces_pending(project_in, 11)

    @functools.partial(loop, HALO, 512, frames // 512)
    def _(r):
        for k in range(0, 512, ROWS):
            rows = pl.ds(at(r, k), ROWS)
            low, high = mask_low[rows, :], mask_high[rows, :]
            total = jnp.zeros((ROWS, LANES), F32)
            crossed = jnp.zeros((ROWS, LANES), F32)
            for b in range(blocks):
                later = high * act_two[pl.ds(at(r, k + DILATION), ROWS), lanes(b)]
                here = act_two[rows, lanes(b)]
                earlier = low * act_two[pl.ds(at(r, k - DILATION), ROWS), lanes(b)]
                n = normed[rows, lanes(b)]
                column[TAP_A, :, lanes(b)] += fold_rows(later * n)
                column[TAP_B, :, lanes(b)] += fold_rows(here * n)
                column[TAP_C, :, lanes(b)] += fold_rows(earlier * n)
                column[DEPTH_BIAS, :, lanes(b)] += fold_rows(here)
                q = (
                    params[9:10, lanes(b)] * later
                    + params[10:11, lanes(b)] * here
                    + params[11:12, lanes(b)] * earlier
                )
                mixed_grad[rows, lanes(b)] = q
                column[SHIFT_ONE, :, lanes(b)] += fold_rows(q)
                q_xhat = q * xhat_one[rows, lanes(b)]
                column[GAIN_ONE, :, lanes(b)] += fold_rows(q_xhat)
                total = total + q
                crossed = crossed + q_xhat
            put_seg(at(r, k, HALO), ROWS, 0, total)
            put_seg(at(r, k, HALO), ROWS, 2, crossed)

    total, crossed = item_sums(0, (2, 2))
    pack_tile(tile_three, {"sum": total, "crossed": crossed})
    exchange(tile_three, stats_three, 2)

    def column_sum(which):
        return jnp.sum(column[which], axis=0, keepdims=True)

    early_rows = {
        1: column_sum(GAIN_ONE) / params[1:2, :],
        2: column_sum(SHIFT_ONE) / params[1:2, :],
        3: column_sum(DEPTH_BIAS),
        4: column_sum(GAIN_TWO) / params[4:5, :],
        5: column_sum(SHIFT_TWO) / params[4:5, :],
        TAP_ROW: column_sum(TAP_A),
        TAP_ROW + 1: column_sum(TAP_B),
        TAP_ROW + 2: column_sum(TAP_C),
    }
    slope_two_row = column_sum(SLOPE_TWO)
    slope_two_row = (slope_two_row[:, 0:half] + slope_two_row[:, half:hidden]) / slope_two
    for c in range(2):
        small_part[c] = jnp.zeros((16, half), F32)
        for row, v in early_rows.items():
            small_part[c, row : row + 1, :] = v[:, c * half : (c + 1) * half]
        small_part[c, BIAS_ROW : BIAS_ROW + 1, :] = bias_sum
        small_part[c, SLOPE_TWO_ROW : SLOPE_TWO_ROW + 1, :] = slope_two_row

    keeper = chips // 2 // stride * stride * 2
    is_keeper = tm == keeper

    def to_keepers(parts, ref, slot, count, phase, sends):
        def each(act):
            for c in range(2):
                copy = remote(parts.at[c], ref.at[slot], phase + c, {"chan": c, "tm": keeper})
                pl.when(sends & ((tm != keeper) | (chan != c)))(lambda: act(copy))

        each(lambda copy: copy.start())
        pending[phase, "sent"] = lambda: each(lambda copy: copy.wait_send())
        pending[phase, "here"] = lambda: [
            pl.when(is_keeper & (chan == c))(
                lambda: wait_bytes(ref.at[pl.ds(0, count - 1)], recv_sem.at[phase + c])
            )
            for c in range(2)
        ]

    pair = remote(small_part, small_pair, 10, sibling)
    started(pair, 10, core == 1, core == 0)
    @own_loop()
    def _(r):
        product = dot(mixed[pl.ds(at(r, 0, HALO), BLOCK), :], w_project[...])
        for k in range(0, BLOCK, ROWS):
            rows = pl.ds(at(r, k, HALO), ROWS)
            inputs = x[pl.ds(at(r, k), ROWS), :].astype(F32)
            block_out[rows, :] = (
                inputs + part(product, k, ROWS, 0) + biases_ref[0:1, :]
            ).astype(BF16)
            skip_out[rows, :] = (part(product, k, ROWS, 1) + biases_ref[1:2, :]).astype(BF16)

    settle((10, "here"))

    @pl.when(core == 0)
    def _():
        small_part[...] += small_pair[...]

    to_keepers(small_part, small_in, mate, mates, 12, core == 0)
    settle((11, "here"))
    sum_rows = pl.ds(pl.multiple_of(core * LANES + spot * 16, 16), 16)

    @when_reducer
    def _():
        project_in[mate] = project_piece(chan, spot)[...]
        total = total_of(project_in, mates, 16, half)
        project_sum[sum_rows, :] = total
        square_part[...] = fold_lanes(jnp.sum(total * total, axis=0, keepdims=True))
        to_group(project_sum.at[sum_rows, :], project_sum.at[sum_rows, :], 17, chips)

    pending[17, "sent"] = lambda: when_reducer(
        lambda: group_sent(project_sum.at[pl.ds(0, 16), :], 17, chips)
    )
    pending[17, "here"] = lambda: by_role(
        lambda n: wait_bytes(project_sum.at[pl.ds(0, 16 * n), :], recv_sem.at[17]), PIECES // 2
    )

    settle(("near", 2, "here"))
    put_table(0, sum_of("sum", tile_three, stats_three) / elements)
    put_table(1, sum_of("crossed", tile_three, stats_three) / elements)
    put_table(2, scale_one)


    for c in range(2):

        @own_loop()
        def _(r, c=c):
            if c == 0:
                values = rows_of(r, BLOCK, 3)
                act_two[pl.ds(r, BLOCK), 0 : 3 * LANES] = values
            for k in range(0, BLOCK, ROWS):
                rows, local = pl.ds(at(r, k), ROWS), pl.ds(at(r, k, HALO), ROWS)
                if c == 0:
                    q_mean, cross_mean, scale = [part(values, k, ROWS, j) for j in range(3)]
                else:
                    q_mean, cross_mean, scale = [act_two[rows, lanes(j)] for j in range(3)]
                for b in range(c * blocks // 2, (c + 1) * blocks // 2):
                    a = act_one[rows, lanes(b)]
                    g = mixed_grad[rows, lanes(b)] - q_mean
                    g = (g - xhat_one[rows, lanes(b)] * cross_mean) * scale
                    column[SLOPE_ONE, :, lanes(b)] += fold_rows(g * jnp.minimum(a, 0.0))
                    hidden_grad[local, lanes(b)] = (g * jnp.where(a > 0, 1.0, slope_one)).astype(
                        BF16
                    )

        total = jnp.zeros((LANES, half), F32)
        for k in range(frames // step):
            total = total + dot_frames(
                x[pl.ds(HALO + k * step, step), :],
                hidden_grad[pl.ds(k * step, step), c * half : (c + 1) * half],
            )
        expand_part[:, c * half : (c + 1) * half] = total
        source = pl.ds(pl.multiple_of(c * half + (1 - core) * LANES, LANES), LANES)
        started(remote(expand_part.at[:, source], expand_pair.at[c], 8 + c, sibling), 8 + c)

    def send_expand(c):
        settle((8 + c, "here"))
        expand_pair[c] += expand_part[
            :, pl.ds(pl.multiple_of(c * half + core * LANES, LANES), LANES)
        ]
        send_pieces(expand_piece, expand_in, 16, c)

    send_expand(0)
    bias_one = dot(jnp.ones((16, frames), BF16), hidden_grad[...])[0:1]
    slope_row = column_sum(SLOPE_ONE)
    slope_row = (slope_row[:, 0:half] + slope_row[:, half:hidden]) / slope_one
    for c in range(2):
        late_part[c, 0:1, :] = bias_one[:, c * half : (c + 1) * half]
        late_part[c, 1:2, :] = slope_row
    to_keepers(late_part, late_in, me, devices, 14, tm >= 0)
    send_expand(1)
    pieces_pending(expand_in, 16)

    settle((12, "here"))

    @pl.when(is_keeper)
    def _():
        small_in[mate] = small_part[chan]
        total = total_of(small_in, mates, 16, half)
        small_sum[...] = total
        square_part[...] += fold_lanes(
            jnp.sum((total * total)[0:BIAS_ROW], axis=0, keepdims=True)
        )
        to_group(small_sum, small_sum, 18, tm_size)

    pending[18, "sent"] = lambda: pl.when(is_keeper)(lambda: group_sent(small_sum, 18, tm_size))
    pending[18, "here"] = lambda: pl.when(jnp.logical_not(is_keeper))(
        lambda: wait_bytes(small_sum, recv_sem.at[18])
    )

    @own_loop()
    def _(r):
        product = dot_rows(hidden_grad[pl.ds(at(r, 0, HALO), BLOCK), :], w_expand[...])
        for k in range(0, BLOCK, ROWS):
            above = cots[pl.ds(at(r, k), ROWS), 0:LANES].astype(F32)
            input_out[pl.ds(at(r, k, HALO), ROWS), :] = above + part(product, k, ROWS, 0)

    extra[...] = jnp.zeros_like(extra)

    def put_extra(k, v):
        high = rounded(v)
        middle = rounded(v - high)
        for j, p in enumerate((high, middle, v - high - middle)):
            extra[3 * k + j : 3 * k + j + 1, :] = p

    settle((14, "here"))

    @pl.when(is_keeper)
    def _():
        late_in[me] = late_part[chan]
        total = total_of(late_in, devices, 2, half)
        for k in range(2):
            for j in range(2):
                put_extra(1 + 2 * k + j, total[j : j + 1, k * LANES : (k + 1) * LANES])
        squares = (total * total)[0:1]
        square_part[...] += fold_lanes(squares)

    settle((16, "here"))

    @when_reducer
    def _():
        expand_in[mate] = expand_piece(chan, spot)[...]
        total = total_of(expand_in, mates, 16, LANES)
        squares = square_part[...] + jnp.sum(total * total, axis=0, keepdims=True)
        square_part[...] = squares
        put_extra(0, squares)
        last_part[0:16, :] = total.astype(BF16)
        last_part[16:32, :] = extra[...].astype(BF16)
        slot = core * spots_here + spot
        last_in[slot] = last_part[...]
        to_group(last_part, last_in.at[slot], 19, tm_size)

        def send_tail(k, carry):
            target = {"chan": other, "tm": wrapped(tm + k, tm_size)}
            remote(square_part, tail_in.at[slot], 20, target).start()
            return carry

        if tm_size <= 16:
            for k in range(tm_size):
                send_tail(k, 0)
        else:
            lax.fori_loop(0, tm_size, send_tail, 0)

    def tails_sent():
        for _ in range(stride):
            wait_bytes(tail_in, send_sem.at[20])

    def from_reducers(n):
        wait_bytes(last_in.at[pl.ds(0, n)], recv_sem.at[19])

    pending[19, "sent"] = lambda: when_reducer(lambda: group_sent(last_part, 19, tm_size))
    pending[19, "here"] = lambda: by_role(from_reducers, PIECES)
    pending[20, "sent"] = lambda: when_reducer(tails_sent)
    pending[20, "here"] = lambda: wait_bytes(tail_in, recv_sem.at[20])

    settle((17, "here"))
    started(remote(project_sum.at[mine, :], project_sum.at[mine, :], 21, sibling), 21)
    settle((18, "here"), (21, "here"))
    for k in range(2):
        project_grad_ref[k] = project_sum[k * LANES : (k + 1) * LANES, :].T
    small_grad_ref[...] = small_sum[...]
    settle((19, "here"), (20, "here"))
    for c in range(2):
        for j in range(spots_here):
            where = slice(c * LANES, (c + 1) * LANES)
            expand_grad_ref[j * 16 : j * 16 + 16, where] = last_in[c * spots_here + j, 0:16, :].astype(F32)
    keeper_spot = keeper // 2 // stride

    def extras(c, j):
        return last_in[c * spots_here + j, 16:32, :].astype(F32)

    def get_extra(rows, k):
        return rows[3 * k : 3 * k + 1] + rows[3 * k + 1 : 3 * k + 2] + rows[3 * k + 2 : 3 * k + 3]

    late = extras(0, keeper_spot)
    for k in range(2):
        where = slice(k * LANES, (k + 1) * LANES)
        small_grad_ref[0:1, where] = get_extra(late, 1 + 2 * k)
        small_grad_ref[SLOPE_ONE_ROW : SLOPE_ONE_ROW + 1, where] = get_extra(late, 2 + 2 * k)
    own_total, other_total = None, None
    for q in range(PIECES):
        c, j = q // spots_here, q % spots_here
        mine_here, theirs = get_extra(extras(c, j), 0), tail_in[q]
        own_total = mine_here if own_total is None else own_total + mine_here
        other_total = theirs if other_total is None else other_total + theirs
    small_grad_ref[SQUARES_ROW : SQUARES_ROW + 1, 0:LANES] = own_total + other_total
    small_grad_ref[SQUARES_ROW : SQUARES_ROW + 1, LANES:half] = jnp.zeros((1, half - LANES), F32)

    settle(*list(pending))


def adam(weight, moment, square, gradient, scale, step_rate):
    clipped = gradient * scale
    moment_next = beta_first * moment + (1.0 - beta_first) * clipped
    square_next = beta_second * square + (1.0 - beta_second) * clipped * clipped
    update = (
        moment_next
        / (1.0 - beta_first**step_count)
        / (jnp.sqrt(square_next / (1.0 - beta_second**step_count)) + adam_eps)
    )
    return weight - step_rate * (update + decay * weight), moment_next, square_next


def adam_kernel(
    block_in,
    skip_in,
    input_in,
    expand_grad,
    project_grad,
    small_grad,
    *refs,
):
    state, outs, slope_refs = list(refs[:15]), refs[18:40], refs[40:43]
    sem = refs[43]
    slope_loads = [
        pltpu.make_async_copy(refs[15 + k], slope_refs[k], sem.at[3 + k]) for k in range(3)
    ]
    for load in slope_loads:
        load.start()
    state += slope_refs
    copies = [
        pltpu.make_async_copy(src, dst, sem.at[k])
        for k, (src, dst) in enumerate(
            zip((block_in, skip_in, input_in), (outs[0], outs[1], outs[2]))
        )
    ]
    for copy in copies:
        copy.start()
    biases = small_grad[BIAS_ROW : BIAS_ROW + 1, :]
    slopes = [
        jnp.sum(small_grad[row : row + 1, :], axis=1, keepdims=True)
        for row in (SLOPE_ONE_ROW, SLOPE_TWO_ROW)
    ]
    total = jnp.sum(small_grad[SQUARES_ROW : SQUARES_ROW + 1, :] + biases * biases, axis=1, keepdims=True)
    total = total + slopes[0] * slopes[0] + slopes[1] * slopes[1]
    grad_norm = jnp.sqrt(total)
    scale = jnp.minimum(1.0, clip_level / grad_norm)
    outs[3][0, 0] = grad_norm[0, 0]

    def update(k, gradient, step_rate, at=...):
        results = adam(
            state[3 * k][at], state[3 * k + 1][at], state[3 * k + 2][at], gradient, scale, step_rate
        )
        for j in range(3):
            outs[4 + 3 * k + j][at] = results[j]

    update(0, expand_grad[...], rate)
    update(1, small_grad[TAP_ROW : TAP_ROW + 3, :], small_rate)
    for k in range(2):
        update(2, project_grad[k], rate, k)
    update(3, small_grad[0:6, :], small_rate)
    lanes = biases.shape[1] // 2
    for k in range(2):
        update(4, biases[:, k * lanes : (k + 1) * lanes], small_rate, slice(k, k + 1))
    for load in slope_loads:
        load.wait()
    for k in range(2):
        results = adam(
            state[15][k], state[16][k], state[17][k], slopes[k], scale, small_rate
        )
        for j in range(3):
            outs[19 + j][k] = results[j][0, 0]
    for copy in copies:
        copy.wait()


def per_device(
    tm_size,
    frames_in,
    item_lengths,
    out_cotangent,
    skip_cotangent,
    expand,
    expand_moment,
    expand_square,
    depthwise,
    depth_moment,
    depth_square,
    project,
    project_moment,
    project_square,
    channel_vectors,
    vector_moment,
    vector_square,
    output_biases,
    bias_moment,
    bias_square,
    prelu_slopes,
    slope_moment,
    slope_square,
):
    frames, inputs = frames_in.shape
    half = expand.shape[1]
    hidden = 2 * half
    items = item_lengths.shape[0]
    item_pad = -(-items // 16) * 16
    width = -(-3 * item_pad // LANES) * LANES
    wide = frames + 2 * HALO
    devices = 2 * tm_size
    peers = 2 * (-(-LONGEST_ITEM // frames))
    tile_rows = spots_of(item_pad)[0]
    vmem, smem, anywhere, hbm = (
        pl.BlockSpec(memory_space=space)
        for space in (pltpu.VMEM, pltpu.SMEM, pl.ANY, pltpu.HBM)
    )
    shape = jax.ShapeDtypeStruct
    scratch = [
        ((wide, inputs), BF16),
        ((wide, 2 * inputs), BF16),
        ((inputs, hidden), BF16),
        ((hidden, 2 * inputs), BF16),
        ((16, hidden), F32),
        ((wide, width), BF16),
        ((item_pad, frames), BF16),
        ((wide, LANES), F32),
        ((wide, LANES), F32),
        ((width, 4 * LANES), BF16),
        ((peers + 1, 1, LANES), F32),
        ((wide, hidden), F32),
        ((wide, hidden), F32),
        ((wide, hidden), F32),
        ((wide, hidden), F32),
        ((wide, hidden), F32),
        ((frames, hidden), BF16),
        ((frames, hidden), BF16),
        ((frames, 8 * LANES), BF16),
        ((COLUMN_SUMS, 8, hidden), F32),
        ((tile_rows, LANES), F32),
        ((tile_rows, LANES), F32),
        ((tile_rows, LANES), F32),
        ((peers, tile_rows, LANES), F32),
        ((peers, tile_rows, LANES), F32),
        ((peers, tile_rows, LANES), F32),
        ((2 * inputs, hidden), F32),
        ((inputs, hidden), F32),
        ((inputs, hidden), F32),
        ((2, inputs, LANES), F32),
        ((tm_size, 16, half), F32),
        ((tm_size, 16, LANES), F32),
        ((2, 16, half), F32),
        ((2, 16, half), F32),
        ((tm_size, 16, half), F32),
        ((2, 2, half), F32),
        ((devices, 2, half), F32),
        ((2 * inputs, half), F32),
        ((16, half), F32),
        ((1, LANES), F32),
        ((16, LANES), F32),
        ((32, LANES), BF16),
        ((PIECES, 32, LANES), BF16),
        ((PIECES, 1, LANES), F32),
    ]
    state = [
        expand,
        expand_moment,
        expand_square,
        depthwise,
        depth_moment,
        depth_square,
        project,
        project_moment,
        project_square,
        channel_vectors,
        vector_moment,
        vector_square,
        output_biases,
        bias_moment,
        bias_square,
    ]
    state = in_hbm(state)
    slopes = in_hbm([prelu_slopes, slope_moment, slope_square])
    arrays = in_hbm([item_lengths, frames_in, out_cotangent, skip_cotangent])
    kept = pl.pallas_call(
        functools.partial(block_kernel, tm_size, items, item_pad),
        out_shape=[
            shape((frames, inputs), BF16),
            shape((frames, inputs), BF16),
            shape((frames, inputs), F32),
            shape((inputs, half), F32),
            shape((2, half, inputs), F32),
            shape((16, half), F32),
        ]
        + [shape(v.shape, F32) for v in state],
        in_specs=[hbm] * 20,
        out_specs=[vmem] * 21,
        scratch_shapes=[pltpu.SMEM((items,), jnp.int32), pltpu.SMEM((2,), F32)]
        + [pltpu.VMEM(s, t) for s, t in scratch]
        + [
            pltpu.SemaphoreType.DMA((25,)),
            pltpu.SemaphoreType.DMA((24,)),
            pltpu.SemaphoreType.DMA((24,)),
            pltpu.SemaphoreType.DMA((3, peers)),
            pltpu.SemaphoreType.DMA((3, peers)),
        ],
        compiler_params=pltpu.CompilerParams(
            collective_id=0, has_side_effects=True, vmem_limit_bytes=48 * 2**20
        ),
        name="temporal_block",
    )(arrays[0], slopes[0], *arrays[1:], *state)
    results = pl.pallas_call(
        adam_kernel,
        out_shape=[
            shape((frames, inputs), BF16),
            shape((frames, inputs), BF16),
            shape((frames, inputs), F32),
            shape((1, 1), F32),
        ]
        + [shape(v.shape, F32) for v in state + slopes],
        in_specs=[anywhere] * 3 + [vmem] * 18 + [hbm] * 3,
        out_specs=[anywhere] * 3 + [smem] + [vmem] * 15 + [smem] * 3,
        scratch_shapes=[pltpu.SMEM((2,), F32)] * 3 + [pltpu.SemaphoreType.DMA((6,))],
        compiler_params=pltpu.CompilerParams(vmem_limit_bytes=8 * 2**20),
        name="adam_step",
    )(*kept, *slopes)
    results = list(results)
    results[3] = results[3].reshape(())
    return tuple(results)


def solution(mesh):
    frames = P(("tm", "chan"), None)
    columns = P(None, "chan")
    rows = P(None, "chan", None)
    in_specs = (
        (frames, P(), frames, frames)
        + (columns,) * 3
        + (columns,) * 3
        + (rows,) * 3
        + (columns,) * 3
        + (P(),) * 6
    )
    out_specs = (
        (frames, frames, frames, P())
        + (columns,) * 3
        + (columns,) * 3
        + (rows,) * 3
        + (columns,) * 3
        + (P(),) * 6
    )
    return jax.shard_map(
        functools.partial(per_device, mesh.shape["tm"]),
        mesh=mesh,
        in_specs=in_specs,
        out_specs=out_specs,
        check_vma=False,
    )
```
